32 devices in a mesh: wide: 8 (over z, y), narrow: 4 (over x, core).
Axes of the slice: x: 2, y: 2, z: 4, core: 2. Of those that a mesh axis runs over, the one named last changes fastest.
Arguments:
- resid: bfloat16 [32768, 767], P(('wide', 'narrow')), may hold values from -6 to 6
- gain_attn: bfloat16 [768], P(('wide', 'narrow')), may hold values from 0.25 to 1.75
- qkv_weight: bfloat16 [768, 2304], P(('wide', 'narrow')), may hold values from -0.21875 to 0.21875
- qv_bias: bfloat16 [1536], P(('wide', 'narrow')), may hold values from -1.796875 to 1.796875
- out_weight: bfloat16 [768, 767], P(('wide', 'narrow')), may hold values from -1.75 to 1.75
- out_bias: bfloat16 [767], replicated, may hold values from -1.796875 to 1.796875
- gain_mlp: bfloat16 [768], P(('wide', 'narrow')), may hold values from 0.25 to 1.75
- up_weight: bfloat16 [768, 3072], P(('wide', 'narrow')), may hold values from -0.21875 to 0.21875
- up_bias: bfloat16 [3072], P(('wide', 'narrow')), may hold values from -1.796875 to 1.796875
- down_weight: bfloat16 [3072, 767], P(('wide', 'narrow')), may hold values from -0.15625 to 0.15625
- down_bias: bfloat16 [767], replicated, may hold values from -1.796875 to 1.796875
- cotangent: bfloat16 [32768, 767], P(('wide', 'narrow')), may hold values from -6 to 6
- seq_lengths: int32 [32, 4], P(('wide', 'narrow')), may hold values from 0 to 1024, as said below
Outputs:
- out_resid: bfloat16 [32768, 767], P(('wide', 'narrow'))
- grad_resid: bfloat16 [32768, 767], P(('wide', 'narrow'))
- grad_gain_attn: float32 [768], P(('wide', 'narrow'))
- grad_qkv_weight: float32 [768, 2304], P(('wide', 'narrow'))
- grad_qv_bias: float32 [1536], P(('wide', 'narrow'))
- grad_out_weight: float32 [768, 767], P(('wide', 'narrow'))
- grad_out_bias: float32 [767], replicated
- grad_gain_mlp: float32 [768], P(('wide', 'narrow'))
- grad_up_weight: float32 [768, 3072], P(('wide', 'narrow'))
- grad_up_bias: float32 [3072], P(('wide', 'narrow'))
- grad_down_weight: float32 [3072, 767], P(('wide', 'narrow'))
- grad_down_bias: float32 [767], replicated
The draws below stay inside these ranges and needn't reach their ends.
Inputs may be any that keep to these rules, and one draw needn't show every extreme that they name: `seq_lengths`: each row holds the lengths of one device's sequences, each 512 or 1024, followed by zeros; a row sums to 1024.
All inputs are finite; a program needn't handle non-finite values.
Results may differ from the reference program's by a relative error of at most 0.013.
Values may be sent and summed in bfloat16 or wider, within the bound.
A program may use at most 256 MiB of HBM per device.

```python
import jax
import jax.numpy as jnp
from jax import lax

D = 768
H = 12
FF = 3072
TOK_DEV = 1024
HD = 64
DC = 767
DEVS = 32
TOKENS = 32768


def draw_seq_lengths(key, part):
    key = jax.random.fold_in(key, 11)
    layouts = jnp.array([[2, 0, 0, 0], [1, 1, 0, 0]], dtype=jnp.int32)
    picks = jax.random.randint(jax.random.fold_in(key, 1), (DEVS,), 0, 2)
    long_device = jax.random.randint(jax.random.fold_in(key, 2), (), 0, DEVS)
    short_device = (long_device + jax.random.randint(jax.random.fold_in(key, 3), (), 1, DEVS)) % DEVS
    picks = picks.at[long_device].set(0).at[short_device].set(1)
    return layouts[picks] * (TOK_DEV // 2)


def block_levels(stream_key, extent, split, smallest, top_value):
    def one(position, blocks):
        steps = jax.random.uniform(jax.random.fold_in(jax.random.fold_in(stream_key, 6), position), (blocks,), jnp.float32, smallest / len(split), top_value / len(split))
        return jnp.repeat(jnp.exp(steps), extent[position] // blocks).reshape((-1,) + (1,) * (len(extent) - position - 1))

    level = one(*split[0])
    for cut in split[1:]:
        level = level * one(*cut)
    return level


def bell_draw(own_key, shape, scale, limit, cuts=(), kind=jnp.bfloat16):
    entries = scale * jax.random.normal(own_key, shape, jnp.float32)
    if cuts:
        entries = entries * block_levels(own_key, shape, cuts, -0.22, 0.18)
    return jnp.clip(entries, -limit, limit).astype(kind)


def setup_inputs(seed: int = 0) -> dict:
    keys = jax.random.split(jax.random.key(seed), 14)
    return {
        "resid": bell_draw(keys[0], (TOKENS, DC), 1.0, 6.0, ((0, 32),)),
        "gain_attn": jnp.clip(1.0 + 0.15 * jax.random.normal(keys[1], (D,), jnp.float32), 0.25, 1.75).astype(jnp.bfloat16),
        "qkv_weight": bell_draw(keys[2], (D, 3 * D), D ** -0.5, 0.21875, ((0, 32),)),
        "qv_bias": bell_draw(keys[3], (2 * D,), 0.3, 1.796875, ((0, 32),)),
        "out_weight": bell_draw(keys[4], (D, DC), (D // 64) ** -0.5, 1.75, ((0, 32),)),
        "out_bias": bell_draw(keys[5], (DC,), 0.3, 1.796875),
        "gain_mlp": jnp.clip(1.0 + 0.15 * jax.random.normal(keys[6], (D,), jnp.float32), 0.25, 1.75).astype(jnp.bfloat16),
        "up_weight": bell_draw(keys[7], (D, FF), D ** -0.5, 0.21875, ((0, 32),)),
        "up_bias": bell_draw(keys[8], (FF,), 0.3, 1.796875, ((0, 32),)),
        "down_weight": bell_draw(keys[9], (FF, DC), (FF // 2) ** -0.5, 0.15625, ((0, 32),)),
        "down_bias": bell_draw(keys[10], (DC,), 0.3, 1.796875),
        "cotangent": bell_draw(keys[11], (TOKENS, DC), 1.0, 6.0, ((0, 32),)),
        "seq_lengths": draw_seq_lengths(jax.random.fold_in(keys[13], 71), 0),
    }


precise = lax.Precision.HIGHEST
norm_eps = 1e-05

@jax.custom_vjp
def low(v):
    return lax.optimization_barrier(v.astype(jnp.bfloat16)).astype(jnp.float32)

@jax.custom_vjp
def low_back(v):
    return v

def low_keep(v):
    return (low(v), None)

def low_pass(kept, grad):
    return (grad,)

def back_keep(v):
    return (v, None)

def back_low(kept, grad):
    return (low(grad),)
low.defvjp(low_keep, low_pass)
low_back.defvjp(back_keep, back_low)

def compressed_norm(values, gain_vec):
    row_total = lax.optimization_barrier(jnp.sum(values, axis=-1, keepdims=True))
    full_vector = jnp.concatenate([values, -row_total], axis=-1)
    mean_sq = lax.optimization_barrier(jnp.mean(full_vector * full_vector, axis=-1, keepdims=True))
    return full_vector * lax.rsqrt(mean_sq + norm_eps) * gain_vec

def group_layer(inputs, lengths, params):
    gain_attn, qkv_weight, qv_bias, out_weight, out_bias, gain_mlp, up_weight, up_bias, down_weight, down_bias = params
    row_count = inputs.shape[0]
    places = jnp.arange(row_count, dtype=jnp.int32)
    seq_ends = jnp.cumsum(lengths).astype(jnp.int32)
    segment = lax.optimization_barrier(jnp.sum((places[:, None] >= seq_ends[None, :]).astype(jnp.int32), axis=1))
    allowed = (segment[:, None] == segment[None, :]) & (places[None, :] <= places[:, None])
    normed = low(compressed_norm(inputs, gain_attn))
    bias_row = jnp.concatenate([qv_bias[:D], jnp.zeros((D,), jnp.float32), qv_bias[D:]])
    qkv_low = low(low_back(jnp.dot(normed, qkv_weight, precision=precise) + bias_row))
    query_heads = qkv_low[:, :D].reshape(row_count, H, HD)
    key_heads = qkv_low[:, D:2 * D].reshape(row_count, H, HD)
    value_heads = qkv_low[:, 2 * D:].reshape(row_count, H, HD)
    scores = low_back(jnp.einsum('qhd,khd->hqk', query_heads, key_heads, precision=precise) * HD ** (-0.5))
    scores = jnp.where(allowed[None], scores, -1e+30)
    attn_probs = low(jax.nn.softmax(scores, axis=-1))
    mixed_heads = jnp.einsum('hqk,khd->qhd', attn_probs, value_heads, precision=precise)
    mixed_low = low(low_back(mixed_heads.reshape(row_count, D)))
    middle = inputs + low_back(jnp.dot(mixed_low, out_weight, precision=precise) + out_bias)
    normed_mlp = low(compressed_norm(middle, gain_mlp))
    pre_act = low_back(jnp.dot(normed_mlp, up_weight, precision=precise) + up_bias)
    activated = low(jax.nn.gelu(pre_act, approximate=True))
    return middle + jnp.dot(activated, down_weight, precision=precise) + down_bias

def reference(resid, gain_attn, qkv_weight, qv_bias, out_weight, out_bias, gain_mlp, up_weight, up_bias, down_weight, down_bias, cotangent, seq_lengths):
    params = tuple((array_in.astype(jnp.float32) for array_in in (gain_attn, qkv_weight, qv_bias, out_weight, out_bias, gain_mlp, up_weight, up_bias, down_weight, down_bias)))
    groups = resid.astype(jnp.float32).reshape(DEVS, TOK_DEV, DC)
    layer_saved = jax.checkpoint(group_layer)

    def forward(group_inputs, weights):
        return lax.map(lambda group_pair: layer_saved(group_pair[0], group_pair[1], weights), (group_inputs, seq_lengths))
    outputs, pullback = jax.vjp(forward, groups, params)
    grad_groups, grads = pullback(cotangent.astype(jnp.float32).reshape(DEVS, TOK_DEV, DC))
    return (outputs.reshape(TOKENS, DC).astype(jnp.bfloat16), grad_groups.reshape(TOKENS, DC).astype(jnp.bfloat16), grads[0], grads[1], grads[2], grads[3], grads[4], grads[5], grads[6], grads[7], grads[8], grads[9])
```

```python
from functools import partial

import jax
import jax.numpy as jnp
from jax import lax
from jax.experimental import pallas as pl
from jax.experimental.pallas import tpu as pltpu
from jax.sharding import PartitionSpec as P

D = 768
H = 12
HD = 64


norm_eps = 1e-05
masked_score = -1e30


def compressed_norm(values, gain_vec):
    row_total = jnp.sum(values, axis=-1, keepdims=True)
    full_vector = jnp.concatenate([values, -row_total], axis=-1)
    mean_sq = jnp.mean(full_vector * full_vector, axis=-1, keepdims=True)
    return full_vector * lax.rsqrt(mean_sq + norm_eps) * gain_vec


def contract_rows(left_side, right_side):
    return lax.dot_general(
        left_side, right_side, (((0,), (0,)), ((), ())), preferred_element_type=jnp.float32
    )


def contract_cols(left_side, right_side):
    return lax.dot_general(
        left_side, right_side, (((1,), (1,)), ((), ())), preferred_element_type=jnp.float32
    )


def segment_ids(lengths, row_count):
    places = jnp.arange(row_count, dtype=jnp.int32)
    seq_ends = jnp.cumsum(lengths)
    segment = jnp.sum((places[:, None] >= seq_ends[None, :]).astype(jnp.int32), axis=1)
    return (places, segment)


def block_scores(query_block, key_heads, places, segment, first_row, last_row):
    scores = jnp.einsum(
        "qhd,khd->hqk", query_block, key_heads[:last_row], preferred_element_type=jnp.float32
    ) * HD ** (-0.5)
    allowed = (segment[first_row:last_row, None] == segment[None, :last_row]) & (
        places[None, :last_row] <= places[first_row:last_row, None]
    )
    return jnp.where(allowed[None], scores, masked_score)


def attend_forward(query_heads, key_heads, value_heads, places, segment):
    row_count = query_heads.shape[0]
    block_rows = min(512, row_count)
    mixed_parts = []
    log_parts = []
    for block_index in range(row_count // block_rows):
        first_row = block_index * block_rows
        last_row = first_row + block_rows
        scores = block_scores(
            query_heads[first_row:last_row], key_heads, places, segment, first_row, last_row
        )
        row_max = jnp.max(scores, axis=-1, keepdims=True)
        exp_scores = jnp.exp(scores - row_max)
        summed = jnp.sum(exp_scores, axis=-1, keepdims=True)
        attn_probs = (exp_scores / summed).astype(jnp.bfloat16)
        mixed_parts.append(
            jnp.einsum(
                "hqk,khd->qhd",
                attn_probs,
                value_heads[:last_row],
                preferred_element_type=jnp.float32,
            )
        )
        log_parts.append(row_max + jnp.log(summed))
    return (jnp.concatenate(mixed_parts, axis=0), jnp.concatenate(log_parts, axis=1))


def attend_backward(query_heads, key_heads, value_heads, grad_mixed, log_sums, places, segment):
    row_count = query_heads.shape[0]
    block_rows = min(512, row_count)
    grad_query_parts = []
    grad_keys = jnp.zeros(key_heads.shape, jnp.float32)
    grad_values = jnp.zeros(value_heads.shape, jnp.float32)
    for block_index in range(row_count // block_rows):
        first_row = block_index * block_rows
        last_row = first_row + block_rows
        query_block = query_heads[first_row:last_row]
        grad_block = grad_mixed[first_row:last_row]
        scores = block_scores(query_block, key_heads, places, segment, first_row, last_row)
        attn_probs = jnp.exp(scores - log_sums[:, first_row:last_row])
        grad_probs = jnp.einsum(
            "qhd,khd->hqk", grad_block, value_heads[:last_row], preferred_element_type=jnp.float32
        )
        row_dot = jnp.sum(attn_probs * grad_probs, axis=-1, keepdims=True)
        grad_scores = (attn_probs * (grad_probs - row_dot)).astype(jnp.bfloat16)
        grad_query_parts.append(
            jnp.einsum(
                "hqk,khd->qhd",
                grad_scores,
                key_heads[:last_row],
                preferred_element_type=jnp.float32,
            )
            * HD ** (-0.5)
        )
        grad_keys = grad_keys.at[:last_row].add(
            jnp.einsum("hqk,qhd->khd", grad_scores, query_block, preferred_element_type=jnp.float32)
            * HD ** (-0.5)
        )
        grad_values = grad_values.at[:last_row].add(
            jnp.einsum(
                "hqk,qhd->khd",
                attn_probs.astype(jnp.bfloat16),
                grad_block,
                preferred_element_type=jnp.float32,
            )
        )
    return (jnp.concatenate(grad_query_parts, axis=0), grad_keys, grad_values)


def attention_part(resid_f, weights, places, segment):
    row_count = resid_f.shape[0]
    normed = compressed_norm(resid_f, weights[6].astype(jnp.float32)).astype(jnp.bfloat16)
    bias_pair = weights[4].astype(jnp.float32)
    bias_row = jnp.concatenate([bias_pair[:D], jnp.zeros((D,), jnp.float32), bias_pair[D:]])
    qkv_low = (jnp.dot(normed, weights[0], preferred_element_type=jnp.float32) + bias_row).astype(
        jnp.bfloat16
    )
    query_heads = qkv_low[:, :D].reshape(row_count, H, HD)
    key_heads = qkv_low[:, D : 2 * D].reshape(row_count, H, HD)
    value_heads = qkv_low[:, 2 * D :].reshape(row_count, H, HD)
    mixed_heads, log_sums = attend_forward(query_heads, key_heads, value_heads, places, segment)
    mixed_low = mixed_heads.reshape(row_count, D).astype(jnp.bfloat16)
    return (normed, query_heads, key_heads, value_heads, mixed_low, log_sums)


def mlp_part(middle, weights):
    normed_mlp = compressed_norm(middle, weights[7].astype(jnp.float32)).astype(jnp.bfloat16)
    pre_act = jnp.dot(normed_mlp, weights[2], preferred_element_type=jnp.float32) + weights[
        5
    ].astype(jnp.float32)
    activated = jax.nn.gelu(pre_act, approximate=True).astype(jnp.bfloat16)
    return (normed_mlp, pre_act, activated)


MESH = pl.DeviceIdType.MESH
ZF, ZN, Y, X, CORE = range(5)
CHIP_AXES = 4
BLOCK = 48


class Place:
    def __init__(self):
        wide = lax.axis_index("wide")
        narrow = lax.axis_index("narrow")
        self.wide, self.narrow = wide, narrow
        self.bits = (
            lax.div(wide, 4),
            lax.rem(lax.div(wide, 2), 2),
            lax.rem(wide, 2),
            lax.div(narrow, 2),
            lax.rem(narrow, 2),
        )

    def other(self, axis):
        flip = 1 - 2 * self.bits[axis]
        if axis == X:
            return (self.wide, self.narrow + 2 * flip)
        if axis == CORE:
            return (self.wide, self.narrow + flip)
        return (self.wide + (4, 2, 1)[axis] * flip, self.narrow)

    def region(self, full, flipped):
        return tuple(
            pl.ds(0, 2)
            if axis in full
            else (1 - self.bits[axis] if axis in flipped else self.bits[axis])
            for axis in range(CHIP_AXES)
        )


def enter(place, axes):
    barrier = pltpu.get_barrier_semaphore()
    for axis in axes:
        pl.semaphore_signal(
            barrier, inc=1, device_id=place.other(axis), device_id_type=MESH
        )
    pl.semaphore_wait(barrier, len(axes))


def send(place, axis, src, dst, send_sem, recv_sem):
    return pltpu.make_async_remote_copy(
        src_ref=src,
        dst_ref=dst,
        send_sem=send_sem,
        recv_sem=recv_sem,
        device_id=place.other(axis),
        device_id_type=MESH,
    )


GATHER_COPIES = 15


def pair_index(stage, piece):
    return stage * (stage - 1) // 2 + piece


class GatherChunk:
    def __init__(self, place, order, view, own, send_sems, recv_sems):
        self.place, self.order, self.view, self.own = place, order, view, own
        self.send_sems, self.recv_sems = send_sems, recv_sems
        self.started = []

    def piece_region(self, piece, flipped=()):
        full = self.order[: max(piece - 1, 0)]
        turned = ((self.order[piece - 1],) if piece else ()) + tuple(flipped)
        return self.place.region(full, turned)

    def copy(self, stage, piece):
        axis = (self.order + (CORE,))[stage - 1]
        core = self.place.bits[CORE]
        here = self.view(self.piece_region(piece), core)
        src = self.own if piece == 0 else here
        slot = pair_index(stage, piece)
        return send(
            self.place, axis, src, here, self.send_sems.at[slot], self.recv_sems.at[slot]
        )

    def arrival(self, stage, piece):
        axis = (self.order + (CORE,))[stage - 1]
        core = self.place.bits[CORE]
        if axis == CORE:
            there = self.view(self.piece_region(piece), 1 - core)
        else:
            there = self.view(self.piece_region(piece, (axis,)), core)
        slot = pair_index(stage, piece)
        return send(
            self.place, axis, there, there, self.send_sems.at[slot], self.recv_sems.at[slot]
        )

    def start(self, piece):
        for stage in range(piece + 1, CHIP_AXES + 2):
            copy = self.copy(stage, piece)
            copy.start()
            self.started.append(copy)

    def step(self, stage):
        if stage:
            for piece in range(stage):
                self.arrival(stage, piece).wait_recv()
        if stage <= CHIP_AXES:
            self.start(stage)

    def drain(self):
        for copy in self.started:
            copy.wait_send()


def sum_small(place, steps, send_sems, recv_sems, first, count):
    values, landing = steps
    axis = first
    copy = send(
        place, axis, values.at[count], landing.at[count], send_sems.at[count], recv_sems.at[count]
    )
    return copy


def gather_kernel(
    qkv_in, out_in, up_in, down_in, small_in,
    qkv_w, out_w, up_w, down_w, small_out,
    pair_f32, pair_low, small_values, small_landing,
    pair_send, pair_recv, own_sems, small_send, small_recv, send_sems, recv_sems,
):
    place = Place()
    core = place.bits[CORE]
    enter(place, range(5))
    widths = (qkv_in.shape[1], out_in.shape[1], up_in.shape[1])
    offsets = (0, widths[0], widths[0] + widths[1])
    rows = qkv_in.shape[0]
    small_values[0] = small_in[...]

    def small_copy(count):
        return send(
            place, count, small_values.at[count], small_landing.at[count],
            small_send.at[count], small_recv.at[count],
        )

    pair_copies = []
    own_rows = pl.ds(pl.multiple_of(core * rows, 8), rows)
    for slot, (shard, offset, width) in enumerate(zip((qkv_in, out_in, up_in), offsets, widths)):
        copy = send(
            place, CORE, shard, pair_f32.at[own_rows, pl.ds(offset, width)],
            pair_send.at[slot], pair_recv.at[slot],
        )
        copy.start()
        pair_copies.append(copy)
    small_copy(0).start()
    for shard, offset, width in zip((qkv_in, out_in, up_in), offsets, widths):
        pair_f32[own_rows, pl.ds(offset, width)] = shard[...]

    chunks = []
    own_copies = []
    for slot, (whole, offset, width) in enumerate(zip((qkv_w, out_w, up_w), offsets, widths)):
        pair_copies[slot].wait()
        pair_low[:, pl.ds(offset, width)] = pair_f32[:, pl.ds(offset, width)].astype(jnp.bfloat16)
        half = width // 2
        first = -(-half // 256) * 128
        here = place.region((), ())
        own_copy = pltpu.make_async_copy(
            pair_low.at[:, pl.ds(pl.multiple_of(offset + core * half, 128), half)],
            whole.at[here + (pl.ds(0, BLOCK), pl.ds(pl.multiple_of(core * half, 128), half))],
            own_sems.at[slot],
        )
        own_copy.start()
        own_copies.append(own_copy)
        for order, start, count in (
            ((ZF, ZN, Y, X), 0, first),
            ((ZF, ZN, X, Y), first, half - first),
        ):
            def view(region, bit, whole=whole, half=half, start=start, count=count):
                return whole.at[
                    region
                    + (pl.ds(0, BLOCK), pl.ds(pl.multiple_of(bit * half + start, 128), count))
                ]

            own = pair_low.at[:, pl.ds(pl.multiple_of(offset + core * half + start, 128), count)]
            index = len(chunks)
            chunks.append(
                GatherChunk(place, order, view, own, send_sems.at[index], recv_sems.at[index])
            )
            chunks[-1].step(0)
    own_copy = pltpu.make_async_copy(
        down_in, down_w.at[place.region((), ()) + (core,)], own_sems.at[3]
    )
    own_copy.start()
    own_copies.append(own_copy)
    half = down_in.shape[1] // 2
    for order, start in (((ZF, ZN, Y, X), 0), ((ZF, ZN, X, Y), half)):
        def view(region, bit, start=start):
            return down_w.at[region + (bit, pl.ds(0, down_in.shape[0]), pl.ds(start, half))]

        own = down_in.at[:, pl.ds(start, half)]
        index = len(chunks)
        chunks.append(
            GatherChunk(place, order, view, own, send_sems.at[index], recv_sems.at[index])
        )
        chunks[-1].step(0)

    for count in range(5):
        small_copy(count).wait()
        small_values[count + 1] = small_values[count] + small_landing[count]
        if count < 4:
            small_copy(count + 1).start()
    small_out[...] = small_values[5]

    for slot in range(4 + 4):
        for tensor in range(4):
            stage = slot - tensor + 1
            if 1 <= stage <= 5:
                chunks[2 * tensor].step(stage)
                chunks[2 * tensor + 1].step(stage)
    for own_copy in own_copies:
        own_copy.wait()
    for chunk in chunks:
        chunk.drain()


def gather_weights(qkv_in, out_in, up_in, down_in, small_in):
    rows = qkv_in.shape[0]
    widths = (qkv_in.shape[1], out_in.shape[1], up_in.shape[1])
    grid = (2, 2, 2, 2)
    outs = [
        jax.ShapeDtypeStruct(grid + (BLOCK, width), jnp.bfloat16) for width in widths
    ] + [
        jax.ShapeDtypeStruct(grid + (2,) + down_in.shape, jnp.bfloat16),
        jax.ShapeDtypeStruct(small_in.shape, jnp.float32),
    ]
    in_vmem = pl.BlockSpec(memory_space=pltpu.VMEM)
    in_hbm = pl.BlockSpec(memory_space=pl.ANY)
    dma = pltpu.SemaphoreType.DMA
    results = pl.pallas_call(
        gather_kernel,
        out_shape=outs,
        in_specs=[in_vmem] * 5,
        out_specs=[in_hbm] * 4 + [in_vmem],
        scratch_shapes=[
            pltpu.VMEM((BLOCK, sum(widths)), jnp.float32),
            pltpu.VMEM((BLOCK, sum(widths)), jnp.bfloat16),
            pltpu.VMEM((6,) + small_in.shape, jnp.float32),
            pltpu.VMEM((5,) + small_in.shape, jnp.float32),
            dma((3,)),
            dma((3,)),
            dma((4,)),
            dma((5,)),
            dma((5,)),
            dma((8, GATHER_COPIES)),
            dma((8, GATHER_COPIES)),
        ],
        compiler_params=pltpu.CompilerParams(
            collective_id=1, has_side_effects=True, vmem_limit_bytes=48 * 2**20
        ),
        name="gather_weights",
    )(qkv_in, out_in, up_in, down_in, small_in)
    return [
        results[0].reshape(-1, widths[0]),
        results[1].reshape(-1, widths[1]),
        results[2].reshape(-1, widths[2]),
        results[3].reshape(-1, down_in.shape[1]),
        results[4],
    ]


class ReduceChunk:
    def __init__(self, place, order, source, total, landings, sems, send_sems, recv_sems):
        self.place, self.order, self.source = place, order, source
        self.total, self.landings = total, landings
        self.sem, self.send_sems, self.recv_sems = sems, send_sems, recv_sems
        self.copies = {}

    def region(self, stage, flipped):
        full = self.order[stage:]
        return self.place.region(full, (self.order[stage - 1],) if flipped else ())

    def launch(self, stage):
        core = self.place.bits[CORE]
        if stage == 0:
            local = pltpu.make_async_copy(self.source(core), self.total, self.sem)
            local.start()
            self.local = local
            src, axis = self.source(1 - core), CORE
        else:
            axis = self.order[stage - 1]
            src = self.total.at[self.region(stage, True)]
        copy = send(
            self.place, axis, src, self.landings[stage],
            self.send_sems.at[stage], self.recv_sems.at[stage],
        )
        copy.start()
        self.copies[stage] = copy

    def absorb(self, stage):
        self.copies[stage].wait_recv()
        landing = self.landings[stage]
        if stage == 0:
            self.local.wait()
            free = (0, 1, 2, 3)
        else:
            free = tuple(sorted(self.order[stage:]))
        blocks = 2 ** len(free)

        def add(block, carry):
            index = list(self.place.bits[:CHIP_AXES])
            where = []
            rest = block
            for axis in reversed(free):
                bit = lax.rem(rest, 2)
                rest = lax.div(rest, 2)
                index[axis] = bit
                where.insert(0, bit)
            summed = self.total[tuple(index)].astype(jnp.float32) + landing[tuple(where)].astype(
                jnp.float32
            )
            self.total[tuple(index)] = summed.astype(jnp.bfloat16)
            return carry

        lax.fori_loop(0, blocks, add, 0)

    def last(self):
        self.copies[CHIP_AXES].wait_recv()
        return self.total[self.place.region((), ())].astype(jnp.float32) + self.landings[
            CHIP_AXES
        ][...].astype(jnp.float32)

    def drain(self):
        for copy in self.copies.values():
            copy.wait_send()


REDUCE_ORDERS = ((X, Y, ZN, ZF), (Y, X, ZN, ZF))


def landing_shapes(rows, count):
    return [
        pltpu.VMEM((2,) * (CHIP_AXES - stage) + (rows, count), jnp.bfloat16)
        for stage in range(CHIP_AXES + 1)
    ]


def reduce_plan(widths, down_shape):
    plan = []
    for tensor in (3, 2, 0, 1):
        if tensor == 3:
            half = down_shape[1] // 2
            plan += [(3, 0, half, down_shape[0]), (3, half, half, down_shape[0])]
        else:
            half = widths[tensor] // 2
            first = -(-half // 256) * 128
            plan += [(tensor, 0, first, BLOCK), (tensor, first, half - first, BLOCK)]
    return plan


def reduce_kernel(widths, down_shape, *refs):
    grads, small_in = refs[:4], refs[4]
    outs, small_out = refs[5:9], refs[9]
    refs = refs[10:]
    plan = reduce_plan(widths, down_shape)
    place = Place()
    core = place.bits[CORE]
    buffers = [refs[6 * k : 6 * k + 6] for k in range(len(plan))]
    refs = refs[6 * len(plan) :]
    (finals, refs) = (refs[:3], refs[3:])
    small_values, small_landing, local_sems, final_send, final_recv, final_own = refs[:6]
    small_send, small_recv, send_sems, recv_sems = refs[6:]
    enter(place, range(5))
    small_values[0] = small_in[...]

    def small_copy(count):
        return send(
            place, count, small_values.at[count], small_landing.at[count],
            small_send.at[count], small_recv.at[count],
        )

    chunks = []
    for index, (tensor, start, count, rows) in enumerate(plan):
        def source(bit, tensor=tensor, start=start, count=count, rows=rows):
            every = (pl.ds(0, 2),) * CHIP_AXES
            if tensor == 3:
                return grads[3].at[every + (bit, pl.ds(0, rows), pl.ds(start, count))]
            first = pl.multiple_of(bit * (widths[tensor] // 2) + start, 128)
            return grads[tensor].at[every + (pl.ds(0, rows), pl.ds(first, count))]

        chunks.append(
            ReduceChunk(
                place, REDUCE_ORDERS[index % 2], source, buffers[index][0], buffers[index][1:],
                local_sems.at[index], send_sems.at[index], recv_sems.at[index],
            )
        )
        chunks[-1].launch(0)
    small_copy(0).start()
    final_copies = []
    pairs = len(chunks) // 2
    for slot in range(pairs + 4):
        if slot < 5:
            small_copy(slot).wait()
            small_values[slot + 1] = small_values[slot] + small_landing[slot]
            if slot < 4:
                small_copy(slot + 1).start()
        for pair in range(pairs):
            stage = slot - pair
            for chunk in (2 * pair, 2 * pair + 1):
                if 0 <= stage < CHIP_AXES:
                    chunks[chunk].absorb(stage)
                    chunks[chunk].launch(stage + 1)
                elif stage == CHIP_AXES:
                    tensor, start, count, rows = plan[chunk]
                    if tensor == 3:
                        outs[3][:, pl.ds(start, count)] = chunks[chunk].last()
                    else:
                        finals[tensor][:, pl.ds(start, count)] = chunks[chunk].last()
            if stage == CHIP_AXES and plan[2 * pair][0] != 3:
                tensor = plan[2 * pair][0]
                half = widths[tensor] // 2
                columns = pl.ds(pl.multiple_of(core * half, 128), half)
                rows = BLOCK // 2
                copy = send(
                    place, CORE,
                    finals[tensor].at[pl.ds(pl.multiple_of((1 - core) * rows, 8), rows)],
                    outs[tensor].at[:, columns],
                    final_send.at[tensor], final_recv.at[tensor],
                )
                copy.start()
                final_copies.append(copy)
                own = pltpu.make_async_copy(
                    finals[tensor].at[pl.ds(pl.multiple_of(core * rows, 8), rows)],
                    outs[tensor].at[:, columns],
                    final_own.at[tensor],
                )
                own.start()
                final_copies.append(own)
    small_out[...] = small_values[5]
    for copy in final_copies:
        copy.wait()
    for chunk in chunks:
        chunk.drain()


def reduce_grads(g_qkv, g_out, g_up, g_down, small_in, down_rows):
    grid = (2, 2, 2, 2)
    widths = (g_qkv.shape[1], g_out.shape[1], g_up.shape[1])
    down_shape = (down_rows, g_down.shape[1])
    grads = [
        g.reshape(grid + (BLOCK, width)) for g, width in zip((g_qkv, g_out, g_up), widths)
    ] + [g_down.reshape(grid + (2,) + down_shape)]
    plan = reduce_plan(widths, down_shape)
    scratch = []
    for tensor, start, count, rows in plan:
        scratch.append(pltpu.VMEM(grid + (rows, count), jnp.bfloat16))
        scratch += landing_shapes(rows, count)
    dma = pltpu.SemaphoreType.DMA
    scratch += [pltpu.VMEM((BLOCK, width // 2), jnp.float32) for width in widths]
    scratch += [
        pltpu.VMEM((6,) + small_in.shape, jnp.float32),
        pltpu.VMEM((5,) + small_in.shape, jnp.float32),
        dma((len(plan),)),
        dma((3,)),
        dma((3,)),
        dma((3,)),
        dma((5,)),
        dma((5,)),
        dma((len(plan), 5)),
        dma((len(plan), 5)),
    ]
    in_vmem = pl.BlockSpec(memory_space=pltpu.VMEM)
    in_hbm = pl.BlockSpec(memory_space=pl.ANY)
    outs = [jax.ShapeDtypeStruct((BLOCK // 2, width), jnp.float32) for width in widths] + [
        jax.ShapeDtypeStruct(down_shape, jnp.float32),
        jax.ShapeDtypeStruct(small_in.shape, jnp.float32),
    ]
    return pl.pallas_call(
        partial(reduce_kernel, widths, down_shape),
        out_shape=outs,
        in_specs=[in_hbm] * 4 + [in_vmem],
        out_specs=[in_vmem] * 5,
        scratch_shapes=scratch,
        compiler_params=pltpu.CompilerParams(
            collective_id=2, has_side_effects=True, vmem_limit_bytes=56 * 2**20
        ),
        name="reduce_grads",
    )(*grads, small_in)


def device_index():
    return lax.axis_index("wide") * lax.axis_size("narrow") + lax.axis_index("narrow")


def spread(shard, whole):
    row = jnp.zeros((whole,), jnp.float32)
    return lax.dynamic_update_slice(
        row, shard.astype(jnp.float32), (device_index() * shard.shape[0],)
    )


def pad_columns(values):
    return jnp.pad(values, ((0, 0), (0, D - values.shape[1])))


def gather_by_kernel(shards):
    qkv, out, up, down, qv_bias, up_bias, gain_attn, gain_mlp = shards
    devices = lax.axis_size("wide") * lax.axis_size("narrow")
    small = jnp.concatenate(
        [spread(v, v.shape[0] * devices) for v in (gain_attn, gain_mlp, qv_bias, up_bias)]
    ).reshape(-1, D)
    qkv_w, out_w, up_w, down_w, small = gather_weights(
        qkv.astype(jnp.float32),
        pad_columns(out).astype(jnp.float32),
        up.astype(jnp.float32),
        pad_columns(down),
        small,
    )
    small = small.reshape(-1)
    width = out.shape[1]
    return (
        qkv_w, out_w[:, :width], up_w, down_w[:, :width],
        small[2 * D : 4 * D].astype(jnp.bfloat16), small[4 * D :].astype(jnp.bfloat16),
        small[:D].astype(jnp.bfloat16), small[D : 2 * D].astype(jnp.bfloat16),
    )


def reduce_by_kernel(sums, grad_b_out, grad_b_down, down_rows):
    w_qkv, w_out, b_qv, g_attn, w_up, w_down, b_up, g_mlp = sums
    width = w_out.shape[1]
    small = jnp.concatenate(
        [g_attn, g_mlp, b_qv, b_up]
        + [jnp.pad(v, (0, D - width)) for v in (grad_b_out, grad_b_down)]
    ).reshape(-1, D)
    rows = small.shape[0]
    small = jnp.pad(small, ((0, -rows % 8), (0, 0)))
    qkv, out, up, down, small = reduce_grads(
        w_qkv.astype(jnp.bfloat16),
        pad_columns(w_out).astype(jnp.bfloat16),
        w_up.astype(jnp.bfloat16),
        pad_columns(w_down).astype(jnp.bfloat16),
        small,
        down_rows,
    )
    small = small.reshape(-1)
    devices = lax.axis_size("wide") * lax.axis_size("narrow")

    def shard(first, count):
        part = count // devices
        return lax.dynamic_slice(small, (first + device_index() * part,), (part,))

    every_shard = (
        qkv, out[:, :width], shard(2 * D, 2 * D), shard(0, D), up, down[:, :width],
        shard(4 * D, b_up.shape[0]), shard(D, D),
    )
    first = 4 * D + b_up.shape[0]
    return every_shard, (small[first : first + width], small[first + D : first + D + width])


def on_device(
    by_kernel,
    resid,
    gain_attn,
    qkv_weight,
    qv_bias,
    out_weight,
    out_bias,
    gain_mlp,
    up_weight,
    up_bias,
    down_weight,
    down_bias,
    cotangent,
    seq_lengths,
):
    shards = (qkv_weight, out_weight, up_weight, down_weight, qv_bias, up_bias, gain_attn, gain_mlp)
    if by_kernel:
        gathered = gather_by_kernel(shards)
    else:
        gathered = tuple(
            lax.all_gather(shard, ("wide", "narrow"), axis=0, tiled=True) for shard in shards
        )
    row_count = resid.shape[0]
    places, segment = segment_ids(seq_lengths[0], row_count)
    resid_f = resid.astype(jnp.float32)
    attn_first = attention_part(resid_f, gathered, places, segment)
    middle = (
        resid_f
        + jnp.dot(attn_first[4], gathered[1], preferred_element_type=jnp.float32)
        + out_bias.astype(jnp.float32)
    )
    mlp_first = mlp_part(middle, gathered)
    out_resid = (
        middle
        + jnp.dot(mlp_first[2], gathered[3], preferred_element_type=jnp.float32)
        + down_bias.astype(jnp.float32)
    ).astype(jnp.bfloat16)
    weights_back = gathered
    normed_mlp, pre_act, activated = mlp_part(middle, weights_back)
    grad_out = cotangent.astype(jnp.float32)
    grad_w_down = contract_rows(activated, cotangent)
    grad_b_down = jnp.sum(grad_out, axis=0)
    grad_act = contract_cols(cotangent, weights_back[3])
    gelu_value, gelu_pull = jax.vjp(partial(jax.nn.gelu, approximate=True), pre_act)
    grad_pre = gelu_pull(grad_act)[0].astype(jnp.bfloat16)
    grad_w_up = contract_rows(normed_mlp, grad_pre)
    grad_b_up = jnp.sum(grad_pre.astype(jnp.float32), axis=0)
    grad_normed_mlp = contract_cols(grad_pre, weights_back[2])
    norm_value, norm_pull = jax.vjp(compressed_norm, middle, weights_back[7].astype(jnp.float32))
    grad_middle_norm, grad_g_mlp = norm_pull(grad_normed_mlp)
    grad_middle = grad_out + grad_middle_norm
    grad_branch = grad_middle.astype(jnp.bfloat16)
    grad_b_out = jnp.sum(grad_branch.astype(jnp.float32), axis=0)
    normed, query_heads, key_heads, value_heads, mixed_low, log_sums = attention_part(
        resid_f, weights_back, places, segment
    )
    grad_w_out = contract_rows(mixed_low, grad_branch)
    grad_mixed = (
        contract_cols(grad_branch, weights_back[1]).astype(jnp.bfloat16).reshape(row_count, H, HD)
    )
    grad_query, grad_keys, grad_values = attend_backward(
        query_heads, key_heads, value_heads, grad_mixed, log_sums, places, segment
    )
    grad_qkv = jnp.concatenate(
        [
            grad_query.reshape(row_count, D),
            grad_keys.reshape(row_count, D),
            grad_values.reshape(row_count, D),
        ],
        axis=1,
    ).astype(jnp.bfloat16)
    grad_w_qkv = contract_rows(normed, grad_qkv)
    column_sums = jnp.sum(grad_qkv.astype(jnp.float32), axis=0)
    grad_b_qv = jnp.concatenate([column_sums[:D], column_sums[2 * D :]])
    grad_normed = contract_cols(grad_qkv, weights_back[0])
    first_value, first_pull = jax.vjp(compressed_norm, resid_f, weights_back[6].astype(jnp.float32))
    grad_resid_norm, grad_g_attn = first_pull(grad_normed)
    grad_resid = (grad_middle + grad_resid_norm).astype(jnp.bfloat16)
    sums = (
        grad_w_qkv, grad_w_out, grad_b_qv, grad_g_attn, grad_w_up, grad_w_down, grad_b_up, grad_g_mlp
    )
    if by_kernel:
        every_shard, bias_sums = reduce_by_kernel(sums, grad_b_out, grad_b_down, down_weight.shape[0])
    else:
        every_shard = tuple(
            lax.psum_scatter(total, ("wide", "narrow"), scatter_dimension=0, tiled=True)
            for total in sums
        )
        bias_sums = lax.psum((grad_b_out, grad_b_down), ("wide", "narrow"))
    attn_shards = every_shard[:4]
    mlp_shards = every_shard[4:]
    return (
        out_resid,
        grad_resid,
        attn_shards[3],
        attn_shards[0],
        attn_shards[2],
        attn_shards[1],
        bias_sums[0],
        mlp_shards[3],
        mlp_shards[0],
        mlp_shards[2],
        mlp_shards[1],
        bias_sums[1],
    )


def solution(mesh):
    by_kernel = mesh.shape["wide"] == 8 and mesh.shape["narrow"] == 4
    return jax.shard_map(
        partial(on_device, by_kernel),
        mesh=mesh,
        in_specs=(
            P(("wide", "narrow"), None),
            P(("wide", "narrow")),
            P(("wide", "narrow"), None),
            P(("wide", "narrow")),
            P(("wide", "narrow"), None),
            P(),
            P(("wide", "narrow")),
            P(("wide", "narrow"), None),
            P(("wide", "narrow")),
            P(("wide", "narrow"), None),
            P(),
            P(("wide", "narrow"), None),
            P(("wide", "narrow"), None),
        ),
        out_specs=(
            P(("wide", "narrow"), None),
            P(("wide", "narrow"), None),
            P(("wide", "narrow")),
            P(("wide", "narrow"), None),
            P(("wide", "narrow")),
            P(("wide", "narrow"), None),
            P(),
            P(("wide", "narrow")),
            P(("wide", "narrow"), None),
            P(("wide", "narrow")),
            P(("wide", "narrow"), None),
            P(),
        ),
        check_vma=False,
    )
```

```python
from functools import partial

import jax
import jax.numpy as jnp
from jax import lax
from jax.experimental import pallas as pl
from jax.experimental.pallas import tpu as pltpu
from jax.sharding import PartitionSpec as P

D = 768
H = 12
HD = 64
LANES = 128
ROWS = 256
FF_BLOCK = 768
GROUP = 256
GROUPS = D // GROUP
TICKS = 2

norm_eps = 1e-05
masked_score = -1e30
gelu_root = 0.7978845608028654

bf16 = jnp.bfloat16
f32 = jnp.float32

MESH = pl.DeviceIdType.MESH
ZF, ZN, Y, X, CORE = range(5)
CHIP_AXES = 4
BLOCK = 48


NN = (((1,), (0,)), ((), ()))
NT = (((1,), (1,)), ((), ()))
TN = (((0,), (0,)), ((), ()))


def dot(left, right, dims=NN):
    return lax.dot_general(left, right, dims, preferred_element_type=f32)


def column_sum(values):
    return jnp.sum(values, axis=0, keepdims=True)


def aligned(index, multiple):
    return pl.multiple_of(index, multiple)


class Place:
    def __init__(self):
        wide = lax.axis_index("wide")
        narrow = lax.axis_index("narrow")
        self.wide, self.narrow = wide, narrow
        self.bits = (
            lax.div(wide, 4),
            lax.rem(lax.div(wide, 2), 2),
            lax.rem(wide, 2),
            lax.div(narrow, 2),
            lax.rem(narrow, 2),
        )
        self.core = self.bits[CORE]

    def other(self, axis):
        flip = 1 - 2 * self.bits[axis]
        if axis == X:
            return (self.wide, self.narrow + 2 * flip)
        if axis == CORE:
            return (self.wide, self.narrow + flip)
        return (self.wide + (4, 2, 1)[axis] * flip, self.narrow)

    def region(self, full=(), flipped=()):
        return tuple(
            pl.ds(0, 2)
            if axis in full
            else (1 - self.bits[axis] if axis in flipped else self.bits[axis])
            for axis in range(CHIP_AXES)
        )


def enter(place):
    barrier = pltpu.get_barrier_semaphore()
    for axis in range(5):
        pl.semaphore_signal(
            barrier, inc=1, device_id=place.other(axis), device_id_type=MESH
        )
    pl.semaphore_wait(barrier, 5)


def send(place, axis, src, dst, send_sem, recv_sem):
    return pltpu.make_async_remote_copy(
        src_ref=src,
        dst_ref=dst,
        send_sem=send_sem,
        recv_sem=recv_sem,
        device_id=place.other(axis),
        device_id_type=MESH,
    )


GATHER_COPIES = 15


class GatherChunk:
    def __init__(self, place, order, view, send_sems, recv_sems):
        self.place, self.axes, self.view = place, order + (CORE,), view
        self.send_sems, self.recv_sems = send_sems, recv_sems

    def copy(self, stage, piece, arriving=False):
        axis = self.axes[stage - 1]
        flipped = (self.axes[piece - 1],) if piece else ()
        bit = self.place.core
        if arriving and axis == CORE:
            bit = 1 - bit
        elif arriving:
            flipped += (axis,)
        where = self.view(self.place.region(self.axes[: max(piece - 1, 0)], flipped), bit)
        slot = stage * (stage - 1) // 2 + piece
        return send(
            self.place, axis, where, where, self.send_sems.at[slot], self.recv_sems.at[slot]
        )

    def step(self, stage):
        for piece in range(stage):
            self.copy(stage, piece, arriving=True).wait_recv()
        for later in range(stage + 1, CHIP_AXES + 2):
            self.copy(later, stage).start()

    def drain(self):
        for stage in range(1, CHIP_AXES + 2):
            for piece in range(stage):
                self.copy(stage, piece).wait_send()


class ReduceChunk:
    def __init__(self, place, order, view, lead, landings, send_sems, recv_sems):
        self.place, self.order, self.view, self.lead = place, order, view, lead
        self.landings, self.send_sems, self.recv_sems = landings, send_sems, recv_sems

    def copy(self, stage):
        if stage == 0:
            axis = CORE
            src = self.view(self.place.region(range(CHIP_AXES)), 1 - self.place.core)
        else:
            axis = self.order[stage - 1]
            src = self.view(
                self.place.region(self.order[stage:], (axis,)), self.place.core
            )
        return send(
            self.place, axis, src, self.landings[stage],
            self.send_sems.at[stage], self.recv_sems.at[stage],
        )

    def launch(self, stage):
        self.copy(stage).start()

    def absorb(self, stage):
        self.copy(stage).wait_recv()
        landing = self.landings[stage]
        free = tuple(sorted(self.order[stage:]))

        def add(block, carry):
            index = list(self.place.bits[:CHIP_AXES])
            where = ()
            rest = block
            for axis in reversed(free):
                index[axis] = lax.rem(rest, 2)
                where = (index[axis],) + where
                rest = lax.div(rest, 2)
            here = self.view(tuple(index), self.place.core)
            here[...] = here[...] + landing[self.lead + where]
            return carry

        lax.fori_loop(0, 2 ** len(free), add, 0)
        self.launch(stage + 1)

    def total(self):
        self.copy(CHIP_AXES).wait_recv()
        here = self.view(self.place.region(), self.place.core)
        return here[...].astype(f32) + self.landings[CHIP_AXES][...].astype(f32)

    def drain(self):
        for stage in range(CHIP_AXES + 1):
            self.copy(stage).wait_send()


def weight_chunks(weights):
    qkv_w, out_w, up_w, down_w = weights
    block = pl.ds(0, BLOCK)

    def qkv_view(group):
        def view(region, bit):
            columns = pl.ds(aligned(group * GROUP + bit * LANES, LANES), LANES)
            return qkv_w.at[(pl.ds(0, 3),) + region + (block, columns)]

        return view

    def half_view(whole, start, count):
        half = whole.shape[-1] // 2

        def view(region, bit):
            return whole.at[region + (block, pl.ds(aligned(bit * half + start, LANES), count))]

        return view

    def down_view(start, count):
        def view(region, bit):
            return down_w.at[region + (bit, pl.ds(0, down_w.shape[-2]), pl.ds(start, count))]

        return view

    half = up_w.shape[-1] // 4
    third = down_w.shape[-1] // 2
    return [
        (qkv_view(0), (3,), (BLOCK, LANES)),
        (qkv_view(1), (3,), (BLOCK, LANES)),
        (qkv_view(2), (3,), (BLOCK, LANES)),
        (half_view(out_w, 0, out_w.shape[-1] // 2), (), (BLOCK, out_w.shape[-1] // 2)),
        (half_view(up_w, 0, half), (), (BLOCK, half)),
        (half_view(up_w, half, half), (), (BLOCK, half)),
        (down_view(0, third), (), (down_w.shape[-2], third)),
        (down_view(third, third), (), (down_w.shape[-2], third)),
    ]


CHUNKS = 8
Q0, Q1, Q2, OUT, UP_A, UP_B, DOWN_A, DOWN_B = range(CHUNKS)

GATHER_ORDERS = {
    Q0: (ZF, ZN, Y, X),
    Q1: (ZF, ZN, X, Y),
    Q2: (Y, X, ZF, ZN),
    OUT: (X, Y, ZF, ZN),
    UP_A: (ZF, ZN, Y, X),
    UP_B: (ZF, ZN, X, Y),
    DOWN_A: (ZF, ZN, Y, X),
    DOWN_B: (ZF, ZN, X, Y),
}
REDUCE_ORDERS = {
    Q0: (X, Y, ZN, ZF),
    Q1: (Y, X, ZN, ZF),
    Q2: (X, Y, ZN, ZF),
    OUT: (Y, X, ZN, ZF),
    UP_A: (X, Y, ZN, ZF),
    UP_B: (Y, X, ZN, ZF),
    DOWN_A: (X, Y, ZN, ZF),
    DOWN_B: (Y, X, ZN, ZF),
}

GATHER_STEPS = {
    "FIRST": [(Q0, 0), (Q1, 0), (Q2, 0), (Q0, 1), (Q2, 1), (Q1, 1), (UP_A, 0), (UP_B, 0), (Q2, 2), (Q0, 2), (OUT, 0), (Q1, 2), (Q0, 3), (UP_A, 1), (OUT, 1), (Q1, 3), (UP_B, 1), (OUT, 2), (Q0, 4), (Q2, 3), (Q0, 5)],
    "FORWARD": [[(Q1, 4), (UP_A, 2), (DOWN_A, 0), (DOWN_B, 0)], [(Q1, 5), (UP_B, 2)], [], [(OUT, 3), (UP_A, 3)], [(Q2, 4)], [], [(Q2, 5), (UP_B, 3), (DOWN_A, 1)], [], [(DOWN_B, 1)], [(OUT, 4), (UP_A, 4)], [(UP_B, 4), (DOWN_A, 2)], [(OUT, 5), (UP_A, 5), (DOWN_B, 2)]],
    "NORMED": [],
    "UP": [(UP_B, 5)],
    "FEED": [[], [(DOWN_A, 3)], [(DOWN_B, 3)], [], [], [], [], [], [], [], [(DOWN_A, 4)], [(DOWN_B, 4)]],
    "BACK": [(DOWN_A, 5), (DOWN_B, 5)],
}

REDUCE_STEPS = {
    "GRAD_UP": [[], [], [(DOWN_A, 0)], [(DOWN_B, 0)]],
    "PREPARED": [(UP_A, 0), (UP_B, 0), (OUT, 0)],
    "BACKWARD": [[], [], [(DOWN_A, 1)], [(DOWN_B, 1)], [], [(Q0, 0)], [(UP_A, 1), (UP_B, 1)], [], [], [(Q0, 1), (Q1, 0), (DOWN_B, 3)], [(DOWN_A, 2)], [(UP_B, 2)]],
    "FINISHED": [[], [(DOWN_B, 2), (OUT, 1)], [(DOWN_A, 3), (UP_A, 2), (OUT, 2)]],
    "NORM": [(UP_B, 3), (Q0, 2), (Q2, 0)],
    "REST": [(UP_A, 3), (Q1, 1), (OUT, 3), (Q0, 3), (Q2, 1), (Q1, 2), (Q2, 2), (Q1, 3), (Q2, 3)],
}


class SmallSum:
    def __init__(self, place, values, landing, send_sems, recv_sems):
        self.place, self.values, self.landing = place, values, landing
        self.send_sems, self.recv_sems = send_sems, recv_sems

    def copy(self, axis):
        return send(
            self.place, axis, self.values.at[axis], self.landing.at[axis],
            self.send_sems.at[axis], self.recv_sems.at[axis],
        )

    def step(self, axis):
        self.copy(axis).wait()
        self.values[axis + 1] = self.values[axis] + self.landing[axis]
        if axis < CORE:
            self.copy(axis + 1).start()


def complete(values):
    lane = lax.broadcasted_iota(jnp.int32, values.shape, 1)
    total = jnp.sum(values, axis=1, keepdims=True)
    return jnp.where(lane == values.shape[1] - 1, -total, values)


def widen(values):
    return jnp.concatenate([values, jnp.zeros((values.shape[0], 1), values.dtype)], axis=1)


def spread(shards, device):
    count = shards.shape[1]
    unit = count // 8
    lane = lax.broadcasted_iota(jnp.int32, (1, count), 1)
    flat = lane + device * unit
    flat = jnp.where(lane >= unit, flat - unit + D, flat)
    flat = jnp.where(lane >= 2 * unit, lane - 2 * unit + 2 * D + device * 2 * unit, flat)
    flat = jnp.where(lane >= 4 * unit, lane - 4 * unit + 4 * D + device * 4 * unit, flat)
    row = lax.broadcasted_iota(jnp.int32, (8, count), 0)
    inside = flat - row * D
    mine = jnp.where((inside >= 0) & (inside < D), shards, 0.0)
    for _ in range(7):
        flat = jnp.where(flat >= D, flat - D, flat)
    column = lax.broadcasted_iota(jnp.int32, (D, count), 0)
    place = jnp.where(column == flat, 1.0, 0.0)
    return dot(mine.astype(bf16), place.astype(bf16), NT)


def inverse_size(full):
    return lax.rsqrt(jnp.mean(full * full, axis=1, keepdims=True) + norm_eps)


def norm_backward(grad, full, inverse, gain):
    scaled = grad * gain
    inner = jnp.sum(scaled * full, axis=1, keepdims=True)
    grad_full = scaled * inverse - full * (inverse * inverse * inverse * (inner * (1.0 / D)))
    return grad * full * inverse, grad_full - grad_full[:, D - 1 : D]


def gelu_and_slope(value):
    square = value * value
    bend = square * (gelu_root * 0.044715) + gelu_root
    half = 0.5 * jnp.tanh(value * bend) + 0.5
    act = value * half
    return act, half + act * (1.0 - half) * (6.0 * bend - 4.0 * gelu_root)


def norm_rows(rows, resid, gain, normed):
    full = complete(widen(resid[rows, :].astype(f32)))
    normed[rows, :] = (full * inverse_size(full) * gain).astype(bf16)


def project(group, normed, qkv_w, small, qkv):
    columns = pl.ds(aligned(group * GROUP, GROUP), GROUP)

    def body(part, carry):
        weight = qkv_w[part, :, :, :, :, :, columns].reshape(D, GROUP)
        bias = jnp.where(part == 1, 0.0, small[pl.ds(2 + lax.div(part, 2), 1), columns])
        qkv[:, pl.ds(aligned(part * D + group * GROUP, GROUP), GROUP)] = (
            dot(normed[...], weight) + bias
        ).astype(bf16)
        return carry

    lax.fori_loop(0, 3, body, 0)


def pair_columns(pair):
    return tuple(pl.ds(aligned(part * D + pair * LANES, LANES), LANES) for part in range(3))


def pair_forward(pair, block, cross, qkv, mixed, mixed_rest, lse):
    count = qkv.shape[0]
    lane = lax.broadcasted_iota(jnp.int32, (ROWS, LANES), 1)
    row = lax.broadcasted_iota(jnp.int32, (ROWS, ROWS), 0)
    column = lax.broadcasted_iota(jnp.int32, (ROWS, ROWS), 1)
    rows = pl.ds(block * ROWS, ROWS)
    last = (block + 1) * ROWS
    query_columns, key_columns, value_columns = pair_columns(pair)
    query = qkv[rows, query_columns] * jnp.asarray(HD**-0.5, bf16)
    key = qkv[pl.ds(0, last), key_columns]
    value = qkv[pl.ds(0, last), value_columns]
    value = jnp.concatenate([value, jnp.ones((last, LANES), bf16)], axis=1)
    outs = []
    stats = lse[rows, :]
    for head in range(2):
        mine = lane < HD if head == 0 else lane >= HD
        scores = dot(jnp.where(mine, query, jnp.zeros_like(query)), key, NT)
        parts = []
        for other in range(block + 1):
            part = scores[:, other * ROWS : (other + 1) * ROWS]
            if other == block:
                part = jnp.where(row >= column, part, masked_score)
            elif block * ROWS >= count // 2 and other * ROWS < count // 2:
                part = part + cross
            parts.append(part)
        scores = jnp.concatenate(parts, axis=1) if block else parts[0]
        largest = jnp.max(scores, axis=1, keepdims=True)
        summed = dot(jnp.exp(scores - largest).astype(bf16), value)
        outs.append(summed[:, :LANES] / summed[:, LANES:])
        stats = jnp.where(lane == 2 * pair + head, largest + jnp.log(summed[:, LANES:]), stats)
    lse[rows, :] = stats
    out = jnp.where(lane < HD, outs[0], outs[1])
    low = out.astype(bf16)
    mixed[rows, query_columns] = low
    mixed_rest[rows, query_columns] = (out - low.astype(f32)).astype(bf16)


def middle_rows(rows, resid, mixed, out_w, biases):
    branch = dot(mixed[rows, :], out_w[...].reshape(D, D))
    return widen(resid[rows, :].astype(f32)) + branch + biases[pl.ds(0, 1), :]


def feed_normed_rows(rows, resid, mixed, small, biases, out_w, normed, normed_t):
    full = complete(middle_rows(rows, resid, mixed, out_w, biases))
    values = (full * inverse_size(full) * small[pl.ds(1, 1), :]).astype(bf16)
    normed[rows, :] = values
    normed_t[:, rows] = jnp.transpose(values)


def feed_forward_columns(part, normed, small, up_w, activated, slopes):
    columns = pl.ds(aligned(part * GROUP, GROUP), GROUP)
    up = up_w[:, :, :, :, :, columns].reshape(D, GROUP)
    bias = small[pl.ds(4 + lax.div(part, GROUPS), 1), pl.ds(aligned(lax.rem(part, GROUPS) * GROUP, GROUP), GROUP)]
    act, slope = gelu_and_slope(dot(normed[...], up) + bias)
    activated[:, columns] = act.astype(bf16)
    slopes[:, columns] = slope.astype(bf16)


def feed_backward_rows(
    rows, starting, resid, cotangent, mixed, small, biases, weights, activated, grad_pre, keep, totals, sums, emit
):
    _, out_w, up_w, down_w = weights
    branch, grad_mixed, whole_cotangent = keep
    out, grad_normed = totals
    cot = widen(cotangent[rows, :].astype(f32))
    low_cot = cot.astype(bf16)
    whole_cotangent[rows, :] = low_cot
    middle = middle_rows(rows, resid, mixed, out_w, biases)
    out[...] = middle + biases[pl.ds(1, 1), :]
    grad_normed[...] = jnp.zeros(middle.shape, f32)

    def body(part, carry):
        columns = pl.ds(aligned(part * FF_BLOCK, FF_BLOCK), FF_BLOCK)
        up = up_w[:, :, :, :, :, columns].reshape(D, FF_BLOCK)
        down = down_w[lax.div(part, 2), lax.rem(part, 2)].reshape(FF_BLOCK, D)
        grad = (dot(low_cot, down, NT) * grad_pre[rows, columns].astype(f32)).astype(bf16)
        grad_pre[rows, columns] = grad
        out[...] = out[...] + dot(activated[rows, columns], down)
        grad_normed[...] = grad_normed[...] + dot(grad, up, NT)
        total = column_sum(grad.astype(f32))
        here = pl.ds(4 + part, 1)
        sums[here, :] = jnp.where(starting, total, sums[here, :] + total)
        return carry

    lax.fori_loop(0, up_w.shape[-1] // FF_BLOCK, body, 0)
    emit(out[...].astype(bf16))
    full = complete(middle)
    gain_terms, grad_input = norm_backward(
        grad_normed[...], full, inverse_size(full), small[pl.ds(1, 1), :]
    )
    rounded = (cot + grad_input).astype(bf16)
    branch[rows, :] = rounded
    grad_mixed[rows, :] = dot(rounded, out_w[...].reshape(D, D), NT).astype(bf16)
    for where, terms in ((1, gain_terms), (8, rounded.astype(f32)), (9, cot)):
        total = column_sum(terms)
        here = pl.ds(where, 1)
        sums[here, :] = jnp.where(starting, total, sums[here, :] + total)


def pair_backward(pair, block, cross, qkv, grad_mixed, lse_t, delta_t, grad_query):
    count = qkv.shape[0]
    lane = lax.broadcasted_iota(jnp.int32, (ROWS, LANES), 1)
    row = lax.broadcasted_iota(jnp.int32, (ROWS, ROWS), 0)
    column = lax.broadcasted_iota(jnp.int32, (ROWS, ROWS), 1)
    keys = pl.ds(block * ROWS, ROWS)
    queries = pl.ds(block * ROWS, count - block * ROWS)
    query_columns, key_columns, value_columns = pair_columns(pair)
    key = qkv[keys, key_columns] * jnp.asarray(HD**-0.5, bf16)
    value = qkv[keys, value_columns]
    query = qkv[queries, query_columns]
    grad = grad_mixed[queries, query_columns]
    grad_values = []
    grad_keys = []
    grad_queries = None
    for head in range(2):
        mine = lane < HD if head == 0 else lane >= HD
        my_key = jnp.where(mine, key, jnp.zeros_like(key))
        my_value = jnp.where(mine, value, jnp.zeros_like(value))
        scores = dot(my_key, query, NT)
        grad_probs = dot(my_value, grad, NT)
        log_row = lse_t[pl.ds(2 * pair + head, 1), queries]
        dot_row = delta_t[pl.ds(2 * pair + head, 1), queries]
        probs = []
        grad_scores = []
        for other in range(count // ROWS - block):
            span = slice(other * ROWS, (other + 1) * ROWS)
            shifted = scores[:, span] - log_row[:, span]
            if other == 0:
                shifted = jnp.where(column >= row, shifted, masked_score)
            elif block * ROWS < count // 2 and (block + other) * ROWS >= count // 2:
                shifted = shifted + cross
            prob = jnp.exp(shifted)
            probs.append(prob.astype(bf16))
            grad_scores.append((prob * (grad_probs[:, span] - dot_row[:, span])).astype(bf16))
        probs = jnp.concatenate(probs, axis=1) if len(probs) > 1 else probs[0]
        grad_scores = jnp.concatenate(grad_scores, axis=1) if len(grad_scores) > 1 else grad_scores[0]
        grad_values.append(dot(probs, grad))
        grad_keys.append(dot(grad_scores, query))
        part = dot(grad_scores, my_key, TN)
        grad_queries = part if grad_queries is None else grad_queries + part
    qkv[keys, value_columns] = jnp.where(lane < HD, grad_values[0], grad_values[1]).astype(bf16)
    qkv[keys, key_columns] = (
        jnp.where(lane < HD, grad_keys[0], grad_keys[1]) * HD**-0.5
    ).astype(bf16)
    if block == 0:
        grad_query[...] = grad_queries
    else:
        grad_query[queries, :] = grad_query[queries, :] + grad_queries


def backward_rows(mixed, mixed_rest, grad_mixed, lse, lse_t, delta_t):
    heads = lse_t.shape[0]
    lse_t[...] = jnp.transpose(lse[...])[:heads]
    head = lax.broadcasted_iota(jnp.int32, (heads, D), 0)
    column = lax.broadcasted_iota(jnp.int32, (heads, D), 1)
    pick = jnp.where((column >= head * HD) & (column < head * HD + HD), 1.0, 0.0).astype(f32)

    def body(block, carry):
        rows = pl.ds(aligned(block * ROWS, ROWS), ROWS)
        whole = mixed[rows, :].astype(f32) + mixed_rest[rows, :].astype(f32)
        product = whole * grad_mixed[rows, :].astype(f32)
        delta_t[:, rows] = lax.dot_general(
            pick, product, NT, precision=lax.Precision.HIGHEST, preferred_element_type=f32
        )
        return carry

    lax.fori_loop(0, mixed.shape[0] // ROWS, body, 0)


def layer_kernel(
    resid, cotangent, qkv_in, out_in, up_in, down_in, small_in, biases_in, lengths,
    out_resid, grad_resid, qkv_out, out_out, up_out, down_out, small_out, qkv_away,
    *scratch,
):
    scratch = list(scratch)
    take = lambda n: [scratch.pop(0) for _ in range(n)]
    weights = take(4)
    qkv_w, out_w, up_w, down_w = weights
    landings = [take(CHIP_AXES + 1) for _ in range(CHUNKS)]
    normed, qkv, mixed, mixed_rest, grad_mixed, branch, lse, staging = take(8)
    my_rows, pair_rows, biases, small_values, small_landing, sum_values, sum_landing = take(7)
    (
        pair_send, pair_recv, small_send, small_recv, sum_send, sum_recv,
        gather_send, gather_recv, reduce_send, reduce_recv,
        final_send, final_recv, final_own, row_sems,
    ) = take(14)
    activated = qkv
    qkv = activated.at[:, pl.ds(0, 3 * D)]
    count = resid.shape[0]
    place = Place()
    core = place.core
    cross = jnp.where(lengths[0, 0] == count, 0.0, masked_score)
    enter(place)

    shards = (qkv_in, out_in, up_in)
    shard_rows = BLOCK // 2
    offsets = ((0, 0), (0, qkv_in.shape[1]), (shard_rows, 0))
    for shard, (top, left) in zip(shards, offsets):
        values = shard[...].astype(f32)
        values = widen(values) if values.shape[1] == D - 1 else values
        my_rows[pl.ds(top, shard_rows), pl.ds(left, values.shape[1])] = values
    pair_copy = send(place, CORE, my_rows, pair_rows, pair_send.at[0], pair_recv.at[0])
    pair_copy.start()
    small_values[0] = spread(small_in[...], place.wide * 4 + place.narrow)
    small_sum = SmallSum(place, small_values, small_landing, small_send, small_recv)
    small_sum.copy(0).start()
    biases[...] = widen(biases_in[...])

    def own_block(slot, first, width):
        top, left = offsets[slot]
        here = (pl.ds(top, shard_rows), pl.ds(aligned(left + first, LANES), width))
        mine, theirs = my_rows[here], pair_rows[here]
        return jnp.concatenate(
            [jnp.where(core == 0, mine, theirs), jnp.where(core == 0, theirs, mine)], axis=0
        ).astype(bf16)

    here = place.region()
    gathers = [
        GatherChunk(place, GATHER_ORDERS[index], view, gather_send.at[index], gather_recv.at[index])
        for index, (view, _, _) in enumerate(weight_chunks(weights))
    ]
    down_w[here + (core,)] = widen(down_in[...].astype(f32)).astype(bf16)
    pair_copy.wait()
    for group in range(GROUPS):
        for part in range(3):
            first = group * GROUP + core * LANES
            qkv_w[(part,) + here + (slice(None), pl.ds(aligned(first, LANES), LANES))] = own_block(
                0, part * D + first, LANES
            )
    opening = list(GATHER_STEPS["FIRST"])
    while opening[0] in ((Q0, 0), (Q1, 0), (Q2, 0)):
        gathers[opening.pop(0)[0]].step(0)
    for slot, whole in ((1, out_w), (2, up_w)):
        half = whole.shape[-1] // 2
        first = aligned(core * half, LANES)
        whole[here + (slice(None), pl.ds(first, half))] = own_block(slot, first, half)

    lse[...] = jnp.zeros_like(lse)

    def norm_all():
        def body(block, carry):
            norm_rows(
                pl.ds(aligned(block * ROWS, ROWS), ROWS), resid, small_values[5][0:1], normed
            )
            return carry

        lax.fori_loop(0, count // ROWS, body, 0)

    axis = 0
    for number, (chunk, stage) in enumerate(opening):
        if (chunk, stage) == (Q0, 5):
            norm_all()
        gathers[chunk].step(stage)
        while axis <= CORE and (axis + 1) * (opening.index((Q0, 4)) + 1) <= (number + 1) * 5:
            small_sum.step(axis)
            axis += 1

    small = small_values.at[5]
    save = pltpu.make_async_copy(qkv, qkv_away, row_sems.at[4])
    blocks = count // ROWS
    pairs = H // 2
    per_group = pairs // GROUPS
    ticks = GATHER_STEPS["FORWARD"]
    after_up = GATHER_STEPS["FEED"]

    def gather_steps(where):
        for chunk, stage in GATHER_STEPS[where]:
            gathers[chunk].step(stage)

    def after(number, index, steps_of, run):
        for which in range(number):
            steps = steps_of(which)
            if steps:
                @pl.when(index == which)
                def _():
                    for chunk, stage in steps:
                        run(chunk, stage)

    def forward(pair, carry):
        @pl.when(lax.rem(pair, per_group) == 0)
        def _():
            project(lax.div(pair, per_group), normed, qkv_w, small, qkv)

        @pl.when(pair == pairs - per_group)
        def _():
            save.start()

        for block in range(blocks):
            pair_forward(pair, block, cross, qkv, mixed, mixed_rest, lse)
            if (block + 1) * TICKS % blocks == 0:
                turn = (block + 1) * TICKS // blocks - 1
                after(
                    pairs, pair, lambda which: ticks[which * TICKS + turn],
                    lambda chunk, stage: gathers[chunk].step(stage),
                )
        return carry

    lax.fori_loop(0, pairs, forward, 0)
    save.wait()

    sums = sum_values.at[0]
    sums[...] = jnp.zeros(sums.shape, f32)
    reduces = [
        ReduceChunk(
            place, REDUCE_ORDERS[index], view, (slice(None),) * len(lead),
            landings[index], reduce_send.at[index], reduce_recv.at[index],
        )
        for index, (view, lead, _) in enumerate(weight_chunks(weights))
    ]

    def emit_rows(target, block, sem, values):
        rows = pl.ds(aligned(block * ROWS, ROWS), ROWS)

        @pl.when(block > 0)
        def _():
            pltpu.make_async_copy(staging, target.at[rows, :], sem).wait()

        staging[...] = values
        pltpu.make_async_copy(staging, target.at[rows, :], sem).start()

    def emit_last(target, sem):
        pltpu.make_async_copy(staging, target.at[pl.ds(0, ROWS), :], sem).wait()

    def feed_forward(grad_pre, whole_cotangent, normed_t, out_total, grad_total):
        def normed_body(block, carry):
            rows = pl.ds(aligned(block * ROWS, ROWS), ROWS)
            feed_normed_rows(rows, resid, mixed, small, biases, out_w, grad_mixed, normed_t)
            return carry

        gather_steps("NORMED")
        lax.fori_loop(0, blocks, normed_body, 0)
        gather_steps("UP")

        def there(part, carry):
            feed_forward_columns(part, grad_mixed, small, up_w, activated, grad_pre)
            after(
                len(after_up), part, lambda which: after_up[which],
                lambda chunk, stage: gathers[chunk].step(stage),
            )
            return carry

        lax.fori_loop(0, len(after_up), there, 0)
        gather_steps("BACK")
        for chunk in gathers:
            chunk.drain()

        def back(block, carry):
            rows = pl.ds(aligned(block * ROWS, ROWS), ROWS)
            feed_backward_rows(
                rows, block == 0, resid, cotangent, mixed, small, biases, weights, activated,
                grad_pre, (branch, grad_mixed, whole_cotangent), (out_total, grad_total), sums,
                partial(emit_rows, out_resid, block, row_sems.at[1]),
            )
            return carry

        lax.fori_loop(0, blocks, back, 0)

        def grad_down(part, carry):
            columns = pl.ds(aligned(part * FF_BLOCK, FF_BLOCK), FF_BLOCK)
            down_w[lax.div(part, 2), lax.rem(part, 2)] = (
                dot(activated[:, columns], whole_cotangent[...], TN)
                .astype(bf16)
                .reshape(down_w.shape[2:])
            )
            return carry

        lax.fori_loop(0, up_w.shape[-1] // FF_BLOCK, grad_down, 0)
        reduces[DOWN_A].launch(0)
        reduces[DOWN_B].launch(0)
        pltpu.make_async_copy(qkv_away, qkv, row_sems.at[4]).start()

        def grad_up(part, carry):
            columns = pl.ds(aligned(part * FF_BLOCK, FF_BLOCK), FF_BLOCK)
            up_w[:, :, :, :, :, columns] = (
                dot(normed_t[...], grad_pre[:, columns])
                .astype(bf16)
                .reshape((2,) * CHIP_AXES + (BLOCK, FF_BLOCK))
            )
            after(
                len(REDUCE_STEPS["GRAD_UP"]), part, lambda which: REDUCE_STEPS["GRAD_UP"][which],
                lambda chunk, stage: reduces[chunk].absorb(stage),
            )
            return carry

        lax.fori_loop(0, up_w.shape[-1] // FF_BLOCK, grad_up, 0)
        reduces[UP_A].launch(0)
        reduces[UP_B].launch(0)

        def grad_out(half, carry):
            columns = pl.ds(aligned(half * (D // 2), LANES), D // 2)
            out_w[half] = (
                dot(mixed[:, columns], branch[...], TN).astype(bf16).reshape(out_w.shape[1:])
            )
            return carry

        lax.fori_loop(0, 2, grad_out, 0)
        reduces[OUT].launch(0)
        emit_last(out_resid, row_sems.at[1])

    pl.run_scoped(
        feed_forward,
        pltpu.VMEM((count, up_w.shape[-1]), bf16),
        pltpu.VMEM((count, D), bf16),
        pltpu.VMEM((D, count), bf16),
        pltpu.VMEM((ROWS, D), f32),
        pltpu.VMEM((ROWS, D), f32),
    )
    pltpu.make_async_copy(qkv_away, qkv, row_sems.at[4]).wait()

    def reduce_steps(where):
        for chunk, stage in REDUCE_STEPS[where]:
            reduces[chunk].absorb(stage)

    def attention_backward(grad_normed, lse_t, delta_t, grad_query, normed_t):
        def turn(block, carry):
            rows = pl.ds(aligned(block * ROWS, ROWS), ROWS)
            normed_t[:, rows] = jnp.transpose(normed[rows, :])
            grad_normed[rows, :] = jnp.zeros((ROWS, D), f32)
            return carry

        lax.fori_loop(0, blocks, turn, 0)
        backward_rows(mixed, mixed_rest, grad_mixed, lse, lse_t, delta_t)
        reduce_steps("PREPARED")
        ticks = REDUCE_STEPS["BACKWARD"]

        def finish_group(group):
            columns = pl.ds(aligned(group * GROUP, GROUP), GROUP)

            def grad_columns(part):
                return pl.ds(aligned(part * D + group * GROUP, GROUP), GROUP)

            def of_rows(block, carry):
                rows = pl.ds(aligned(block * ROWS, ROWS), ROWS)
                total = grad_normed[rows, :]
                for part in range(3):
                    weight = qkv_w[part, :, :, :, :, :, columns].reshape(D, GROUP)
                    total = total + dot(qkv[rows, grad_columns(part)], weight, NT)
                grad_normed[rows, :] = total
                return carry

            lax.fori_loop(0, blocks, of_rows, 0)

            def of_weight(part, carry):
                grads = qkv[:, grad_columns(part)]
                qkv_w[part, :, :, :, :, :, columns] = (
                    dot(normed_t[...], grads)
                    .astype(bf16)
                    .reshape((2,) * CHIP_AXES + (BLOCK, GROUP))
                )
                here = jnp.where(part == 1, 10, 2 + lax.div(part, 2))
                sums[pl.ds(here, 1), columns] = column_sum(grads.astype(f32))
                return carry

            lax.fori_loop(0, 3, of_weight, 0)

        def backward(pair, carry):
            for block in range(blocks):
                pair_backward(pair, block, cross, qkv, grad_mixed, lse_t, delta_t, grad_query)
                if (block + 1) * TICKS % blocks == 0:
                    turn = (block + 1) * TICKS // blocks - 1
                    after(
                        pairs, pair, lambda which: ticks[which * TICKS + turn],
                        lambda chunk, stage: reduces[chunk].absorb(stage),
                    )
            qkv[:, pair_columns(pair)[0]] = grad_query[...].astype(bf16)

            @pl.when(lax.rem(pair, per_group) == per_group - 1)
            def _():
                finish_group(lax.div(pair, per_group))

            def finished(chunk, stage):
                if stage is None:
                    reduces[chunk].launch(0)
                else:
                    reduces[chunk].absorb(stage)

            def steps_of(which):
                if which % per_group < per_group - 1:
                    return []
                group = which // per_group
                return [(group, None)] + REDUCE_STEPS["FINISHED"][group]

            after(pairs, pair, steps_of, finished)
            return carry

        lax.fori_loop(0, pairs, backward, 0)

        def body(block, carry):
            rows = pl.ds(aligned(block * ROWS, ROWS), ROWS)
            full = complete(widen(resid[rows, :].astype(f32)))
            gain_terms, grad_input = norm_backward(
                grad_normed[rows, :], full, inverse_size(full), small[pl.ds(0, 1), :]
            )
            emit_rows(
                grad_resid, block, row_sems.at[2],
                (branch[rows, :].astype(f32) + grad_input).astype(bf16),
            )
            total = column_sum(gain_terms)
            sums[pl.ds(0, 1), :] = jnp.where(block == 0, total, sums[pl.ds(0, 1), :] + total)
            return carry

        lax.fori_loop(0, count // ROWS, body, 0)

    pl.run_scoped(
        attention_backward,
        pltpu.VMEM((count, D), f32),
        pltpu.VMEM((16, count), f32),
        pltpu.VMEM((16, count), f32),
        pltpu.VMEM((count, LANES), f32),
        pltpu.VMEM((D, count), bf16),
    )
    sum_all = SmallSum(place, sum_values, sum_landing, sum_send, sum_recv)
    sum_all.copy(0).start()
    reduce_steps("NORM")
    rest = REDUCE_STEPS["REST"]
    axis = 0
    for number, (chunk, stage) in enumerate(rest):
        reduces[chunk].absorb(stage)
        if axis < CORE:
            sum_all.step(axis)
            axis += 1
    while axis <= CORE:
        sum_all.step(axis)
        axis += 1
    small_out[...] = sum_values[5]

    for chunk, start in ((DOWN_A, 0), (DOWN_B, D // 2)):
        down_out[:, pl.ds(start, D // 2)] = reduces[chunk].total()
    their_rows = pl.ds(aligned((1 - core) * shard_rows, 8), shard_rows)
    kept_rows = pl.ds(aligned(core * shard_rows, 8), shard_rows)
    copies = []

    def deliver(slot, part_of, target):
        away = send(
            place, CORE, part_of(their_rows), target, final_send.at[slot], final_recv.at[slot]
        )
        away.start()
        home = pltpu.make_async_copy(part_of(kept_rows), target, final_own.at[slot])
        home.start()
        copies.extend((away, home))

    finals = pair_rows
    half = up_w.shape[-1] // 4
    finals[:, pl.ds(0, half)] = reduces[UP_A].total()
    finals[:, pl.ds(half, half)] = reduces[UP_B].total()
    deliver(
        0, lambda rows: finals.at[rows, pl.ds(0, 2 * half)],
        up_out.at[:, pl.ds(aligned(core * 2 * half, LANES), 2 * half)],
    )
    first = 2 * half
    finals[:, pl.ds(first, D // 2)] = reduces[OUT].total()
    deliver(
        1, lambda rows: finals.at[rows, pl.ds(2 * half, D // 2)],
        out_out.at[:, pl.ds(aligned(core * (D // 2), LANES), D // 2)],
    )
    first += D // 2
    for group in range(GROUPS):
        total = reduces[group].total()
        for part in range(3):
            here = pl.ds(first, LANES)
            finals[:, here] = total[part]
            deliver(
                2 + group * 3 + part, lambda rows, here=here: finals.at[rows, here],
                qkv_out.at[:, pl.ds(aligned(part * D + group * GROUP + core * LANES, LANES), LANES)],
            )
            first += LANES
    for copy in copies:
        copy.wait()
    for chunk in reduces:
        chunk.drain()
    emit_last(grad_resid, row_sems.at[2])


def layer_by_kernel(resid, cotangent, qkv_in, out_in, up_in, down_in, small_in, biases, lengths):
    count = resid.shape[0]
    grid = (2,) * CHIP_AXES
    ff = up_in.shape[1]
    weight_shapes = [
        (3,) + grid + (BLOCK, D),
        grid + (BLOCK, D),
        grid + (BLOCK, ff),
        grid + (2, down_in.shape[0], D),
    ]
    weights = [pltpu.VMEM(shape, bf16) for shape in weight_shapes]
    shapes = [jax.ShapeDtypeStruct(shape, bf16) for shape in weight_shapes]
    landings = [
        pltpu.VMEM(lead + (2,) * (CHIP_AXES - stage) + block, bf16)
        for _, lead, block in weight_chunks(shapes)
        for stage in range(CHIP_AXES + 1)
    ]
    dma = pltpu.SemaphoreType.DMA
    small_rows, sum_rows = 8, 16
    scratch = (
        weights
        + landings
        + [
            pltpu.VMEM((count, D), bf16),
            pltpu.VMEM((count, ff), bf16),
            pltpu.VMEM((count, D), bf16),
            pltpu.VMEM((count, D), bf16),
            pltpu.VMEM((count, D), bf16),
            pltpu.VMEM((count, D), bf16),
            pltpu.VMEM((count, LANES), f32),
            pltpu.VMEM((ROWS, D), bf16),
            pltpu.VMEM((BLOCK, (3 * D + D + ff) // 2), f32),
            pltpu.VMEM((BLOCK, (3 * D + D + ff) // 2), f32),
            pltpu.VMEM((2, D), f32),
            pltpu.VMEM((6, small_rows, D), f32),
            pltpu.VMEM((5, small_rows, D), f32),
            pltpu.VMEM((6, sum_rows, D), f32),
            pltpu.VMEM((5, sum_rows, D), f32),
            dma((3,)),
            dma((3,)),
            dma((5,)),
            dma((5,)),
            dma((5,)),
            dma((5,)),
            dma((CHUNKS, GATHER_COPIES)),
            dma((CHUNKS, GATHER_COPIES)),
            dma((CHUNKS, CHIP_AXES + 1)),
            dma((CHUNKS, CHIP_AXES + 1)),
            dma((11,)),
            dma((11,)),
            dma((11,)),
            dma((5,)),
        ]
    )
    in_vmem = pl.BlockSpec(memory_space=pltpu.VMEM)
    in_hbm = pl.BlockSpec(memory_space=pl.ANY)
    shard_rows = BLOCK // 2
    return pl.pallas_call(
        layer_kernel,
        out_shape=[
            jax.ShapeDtypeStruct((count, D), bf16),
            jax.ShapeDtypeStruct((count, D), bf16),
            jax.ShapeDtypeStruct((shard_rows, 3 * D), f32),
            jax.ShapeDtypeStruct((shard_rows, D), f32),
            jax.ShapeDtypeStruct((shard_rows, ff), f32),
            jax.ShapeDtypeStruct((down_in.shape[0], D), f32),
            jax.ShapeDtypeStruct((sum_rows, D), f32),
            jax.ShapeDtypeStruct((count, 3 * D), bf16),
        ],
        in_specs=[in_vmem] * 8 + [pl.BlockSpec(memory_space=pltpu.SMEM)],
        out_specs=[in_hbm] * 2 + [in_vmem] * 5 + [in_hbm],
        scratch_shapes=scratch,
        compiler_params=pltpu.CompilerParams(
            collective_id=1, has_side_effects=True, vmem_limit_bytes=VMEM_BYTES
        ),
        name="layer",
    )(resid, cotangent, qkv_in, out_in, up_in, down_in, small_in, biases, lengths)


VMEM_BYTES = 63 * 2**20


def device_index():
    return lax.axis_index("wide") * lax.axis_size("narrow") + lax.axis_index("narrow")


def on_device_by_kernel(
    resid, gain_attn, qkv_weight, qv_bias, out_weight, out_bias, gain_mlp,
    up_weight, up_bias, down_weight, down_bias, cotangent, seq_lengths,
):
    devices = lax.axis_size("wide") * lax.axis_size("narrow")
    width = out_weight.shape[1]
    small = jnp.concatenate([gain_attn, gain_mlp, qv_bias, up_bias]).astype(f32)
    biases = jnp.stack([out_bias, down_bias]).astype(f32)
    out_resid, grad_resid, qkv, out, up, down, sums, _ = layer_by_kernel(
        resid, cotangent, qkv_weight, out_weight, up_weight, down_weight,
        small.reshape(1, -1), biases, seq_lengths,
    )
    sums = sums.reshape(-1)

    def shard(first, count):
        part = count // devices
        return lax.dynamic_slice(sums, (first + device_index() * part,), (part,))

    ff = up_weight.shape[1]
    last = 4 * D + ff
    return (
        out_resid[:, :width],
        grad_resid[:, :width],
        shard(0, D),
        qkv,
        shard(2 * D, 2 * D),
        out[:, :width],
        sums[last : last + width],
        shard(D, D),
        up,
        shard(4 * D, ff),
        down[:, :width],
        sums[last + D : last + D + width],
    )


def compressed_norm(values, gain_vec):
    row_total = jnp.sum(values, axis=-1, keepdims=True)
    full_vector = jnp.concatenate([values, -row_total], axis=-1)
    mean_sq = jnp.mean(full_vector * full_vector, axis=-1, keepdims=True)
    return full_vector * lax.rsqrt(mean_sq + norm_eps) * gain_vec


def contract_rows(left_side, right_side):
    return lax.dot_general(
        left_side, right_side, (((0,), (0,)), ((), ())), preferred_element_type=jnp.float32
    )


def contract_cols(left_side, right_side):
    return lax.dot_general(
        left_side, right_side, (((1,), (1,)), ((), ())), preferred_element_type=jnp.float32
    )


def segment_ids(lengths, row_count):
    places = jnp.arange(row_count, dtype=jnp.int32)
    seq_ends = jnp.cumsum(lengths)
    segment = jnp.sum((places[:, None] >= seq_ends[None, :]).astype(jnp.int32), axis=1)
    return (places, segment)


def block_scores(query_block, key_heads, places, segment, first_row, last_row):
    scores = jnp.einsum(
        "qhd,khd->hqk", query_block, key_heads[:last_row], preferred_element_type=jnp.float32
    ) * HD ** (-0.5)
    allowed = (segment[first_row:last_row, None] == segment[None, :last_row]) & (
        places[None, :last_row] <= places[first_row:last_row, None]
    )
    return jnp.where(allowed[None], scores, masked_score)


def attend_forward(query_heads, key_heads, value_heads, places, segment):
    row_count = query_heads.shape[0]
    block_rows = min(512, row_count)
    mixed_parts = []
    log_parts = []
    for block_index in range(row_count // block_rows):
        first_row = block_index * block_rows
        last_row = first_row + block_rows
        scores = block_scores(
            query_heads[first_row:last_row], key_heads, places, segment, first_row, last_row
        )
        row_max = jnp.max(scores, axis=-1, keepdims=True)
        exp_scores = jnp.exp(scores - row_max)
        summed = jnp.sum(exp_scores, axis=-1, keepdims=True)
        attn_probs = (exp_scores / summed).astype(jnp.bfloat16)
        mixed_parts.append(
            jnp.einsum(
                "hqk,khd->qhd",
                attn_probs,
                value_heads[:last_row],
                preferred_element_type=jnp.float32,
            )
        )
        log_parts.append(row_max + jnp.log(summed))
    return (jnp.concatenate(mixed_parts, axis=0), jnp.concatenate(log_parts, axis=1))


def attend_backward(query_heads, key_heads, value_heads, grad_mixed, log_sums, places, segment):
    row_count = query_heads.shape[0]
    block_rows = min(512, row_count)
    grad_query_parts = []
    grad_keys = jnp.zeros(key_heads.shape, jnp.float32)
    grad_values = jnp.zeros(value_heads.shape, jnp.float32)
    for block_index in range(row_count // block_rows):
        first_row = block_index * block_rows
        last_row = first_row + block_rows
        query_block = query_heads[first_row:last_row]
        grad_block = grad_mixed[first_row:last_row]
        scores = block_scores(query_block, key_heads, places, segment, first_row, last_row)
        attn_probs = jnp.exp(scores - log_sums[:, first_row:last_row])
        grad_probs = jnp.einsum(
            "qhd,khd->hqk", grad_block, value_heads[:last_row], preferred_element_type=jnp.float32
        )
        row_dot = jnp.sum(attn_probs * grad_probs, axis=-1, keepdims=True)
        grad_scores = (attn_probs * (grad_probs - row_dot)).astype(jnp.bfloat16)
        grad_query_parts.append(
            jnp.einsum(
                "hqk,khd->qhd",
                grad_scores,
                key_heads[:last_row],
                preferred_element_type=jnp.float32,
            )
            * HD ** (-0.5)
        )
        grad_keys = grad_keys.at[:last_row].add(
            jnp.einsum("hqk,qhd->khd", grad_scores, query_block, preferred_element_type=jnp.float32)
            * HD ** (-0.5)
        )
        grad_values = grad_values.at[:last_row].add(
            jnp.einsum(
                "hqk,qhd->khd",
                attn_probs.astype(jnp.bfloat16),
                grad_block,
                preferred_element_type=jnp.float32,
            )
        )
    return (jnp.concatenate(grad_query_parts, axis=0), grad_keys, grad_values)


def attention_part(resid_f, weights, places, segment):
    row_count = resid_f.shape[0]
    normed = compressed_norm(resid_f, weights[6].astype(jnp.float32)).astype(jnp.bfloat16)
    bias_pair = weights[4].astype(jnp.float32)
    bias_row = jnp.concatenate([bias_pair[:D], jnp.zeros((D,), jnp.float32), bias_pair[D:]])
    qkv_low = (jnp.dot(normed, weights[0], preferred_element_type=jnp.float32) + bias_row).astype(
        jnp.bfloat16
    )
    query_heads = qkv_low[:, :D].reshape(row_count, H, HD)
    key_heads = qkv_low[:, D : 2 * D].reshape(row_count, H, HD)
    value_heads = qkv_low[:, 2 * D :].reshape(row_count, H, HD)
    mixed_heads, log_sums = attend_forward(query_heads, key_heads, value_heads, places, segment)
    mixed_low = mixed_heads.reshape(row_count, D).astype(jnp.bfloat16)
    return (normed, query_heads, key_heads, value_heads, mixed_low, log_sums)


def mlp_part(middle, weights):
    normed_mlp = compressed_norm(middle, weights[7].astype(jnp.float32)).astype(jnp.bfloat16)
    pre_act = jnp.dot(normed_mlp, weights[2], preferred_element_type=jnp.float32) + weights[
        5
    ].astype(jnp.float32)
    activated = jax.nn.gelu(pre_act, approximate=True).astype(jnp.bfloat16)
    return (normed_mlp, pre_act, activated)


def on_device(
    resid,
    gain_attn,
    qkv_weight,
    qv_bias,
    out_weight,
    out_bias,
    gain_mlp,
    up_weight,
    up_bias,
    down_weight,
    down_bias,
    cotangent,
    seq_lengths,
):
    shards = (qkv_weight, out_weight, up_weight, down_weight, qv_bias, up_bias, gain_attn, gain_mlp)
    gathered = (
        lax.all_gather(shards[0], ("wide", "narrow"), axis=0, tiled=True),
        lax.all_gather(shards[1], ("wide", "narrow"), axis=0, tiled=True),
        lax.all_gather(shards[2], ("wide", "narrow"), axis=0, tiled=True),
        lax.all_gather(shards[3], ("wide", "narrow"), axis=0, tiled=True),
        lax.all_gather(shards[4], ("wide", "narrow"), axis=0, tiled=True),
        lax.all_gather(shards[5], ("wide", "narrow"), axis=0, tiled=True),
        lax.all_gather(shards[6], ("wide", "narrow"), axis=0, tiled=True),
        lax.all_gather(shards[7], ("wide", "narrow"), axis=0, tiled=True),
    )
    row_count = resid.shape[0]
    places, segment = segment_ids(seq_lengths[0], row_count)
    resid_f = resid.astype(jnp.float32)
    attn_first = attention_part(resid_f, gathered, places, segment)
    middle = (
        resid_f
        + jnp.dot(attn_first[4], gathered[1], preferred_element_type=jnp.float32)
        + out_bias.astype(jnp.float32)
    )
    mlp_first = mlp_part(middle, gathered)
    out_resid = (
        middle
        + jnp.dot(mlp_first[2], gathered[3], preferred_element_type=jnp.float32)
        + down_bias.astype(jnp.float32)
    ).astype(jnp.bfloat16)
    weights_back = gathered
    normed_mlp, pre_act, activated = mlp_part(middle, weights_back)
    grad_out = cotangent.astype(jnp.float32)
    grad_w_down = contract_rows(activated, cotangent)
    grad_b_down = jnp.sum(grad_out, axis=0)
    grad_act = contract_cols(cotangent, weights_back[3])
    gelu_value, gelu_pull = jax.vjp(partial(jax.nn.gelu, approximate=True), pre_act)
    grad_pre = gelu_pull(grad_act)[0].astype(jnp.bfloat16)
    grad_w_up = contract_rows(normed_mlp, grad_pre)
    grad_b_up = jnp.sum(grad_pre.astype(jnp.float32), axis=0)
    grad_normed_mlp = contract_cols(grad_pre, weights_back[2])
    norm_value, norm_pull = jax.vjp(compressed_norm, middle, weights_back[7].astype(jnp.float32))
    grad_middle_norm, grad_g_mlp = norm_pull(grad_normed_mlp)
    grad_middle = grad_out + grad_middle_norm
    grad_branch = grad_middle.astype(jnp.bfloat16)
    grad_b_out = jnp.sum(grad_branch.astype(jnp.float32), axis=0)
    normed, query_heads, key_heads, value_heads, mixed_low, log_sums = attention_part(
        resid_f, weights_back, places, segment
    )
    grad_w_out = contract_rows(mixed_low, grad_branch)
    grad_mixed = (
        contract_cols(grad_branch, weights_back[1]).astype(jnp.bfloat16).reshape(row_count, H, HD)
    )
    grad_query, grad_keys, grad_values = attend_backward(
        query_heads, key_heads, value_heads, grad_mixed, log_sums, places, segment
    )
    grad_qkv = jnp.concatenate(
        [
            grad_query.reshape(row_count, D),
            grad_keys.reshape(row_count, D),
            grad_values.reshape(row_count, D),
        ],
        axis=1,
    ).astype(jnp.bfloat16)
    grad_w_qkv = contract_rows(normed, grad_qkv)
    column_sums = jnp.sum(grad_qkv.astype(jnp.float32), axis=0)
    grad_b_qv = jnp.concatenate([column_sums[:D], column_sums[2 * D :]])
    grad_normed = contract_cols(grad_qkv, weights_back[0])
    first_value, first_pull = jax.vjp(compressed_norm, resid_f, weights_back[6].astype(jnp.float32))
    grad_resid_norm, grad_g_attn = first_pull(grad_normed)
    grad_resid = (grad_middle + grad_resid_norm).astype(jnp.bfloat16)
    every_shard = (
        lax.psum_scatter(grad_w_qkv, ("wide", "narrow"), scatter_dimension=0, tiled=True),
        lax.psum_scatter(grad_w_out, ("wide", "narrow"), scatter_dimension=0, tiled=True),
        lax.psum_scatter(grad_b_qv, ("wide", "narrow"), scatter_dimension=0, tiled=True),
        lax.psum_scatter(grad_g_attn, ("wide", "narrow"), scatter_dimension=0, tiled=True),
        lax.psum_scatter(grad_w_up, ("wide", "narrow"), scatter_dimension=0, tiled=True),
        lax.psum_scatter(grad_w_down, ("wide", "narrow"), scatter_dimension=0, tiled=True),
        lax.psum_scatter(grad_b_up, ("wide", "narrow"), scatter_dimension=0, tiled=True),
        lax.psum_scatter(grad_g_mlp, ("wide", "narrow"), scatter_dimension=0, tiled=True),
    )
    attn_shards = every_shard[:4]
    mlp_shards = every_shard[4:]
    bias_sums = lax.psum((grad_b_out, grad_b_down), ("wide", "narrow"))
    return (
        out_resid,
        grad_resid,
        attn_shards[3],
        attn_shards[0],
        attn_shards[2],
        attn_shards[1],
        bias_sums[0],
        mlp_shards[3],
        mlp_shards[0],
        mlp_shards[2],
        mlp_shards[1],
        bias_sums[1],
    )


def solution(mesh):
    by_kernel = mesh.shape["wide"] == 8 and mesh.shape["narrow"] == 4
    return jax.shard_map(
        on_device_by_kernel if by_kernel else on_device,
        mesh=mesh,
        in_specs=(
            P(("wide", "narrow"), None),
            P(("wide", "narrow")),
            P(("wide", "narrow"), None),
            P(("wide", "narrow")),
            P(("wide", "narrow"), None),
            P(),
            P(("wide", "narrow")),
            P(("wide", "narrow"), None),
            P(("wide", "narrow")),
            P(("wide", "narrow"), None),
            P(),
            P(("wide", "narrow"), None),
            P(("wide", "narrow"), None),
        ),
        out_specs=(
            P(("wide", "narrow"), None),
            P(("wide", "narrow"), None),
            P(("wide", "narrow")),
            P(("wide", "narrow"), None),
            P(("wide", "narrow")),
            P(("wide", "narrow"), None),
            P(),
            P(("wide", "narrow")),
            P(("wide", "narrow"), None),
            P(("wide", "narrow")),
            P(("wide", "narrow"), None),
            P(),
        ),
        check_vma=False,
    )
```

```python
from functools import partial

import jax
import jax.numpy as jnp
from jax import lax
from jax.experimental import pallas as pl
from jax.experimental.pallas import tpu as pltpu
from jax.sharding import PartitionSpec as P

D = 768
H = 12
HD = 64
LANES = 128
ROWS = 256
FF_BLOCK = 768
GROUP = 256
GROUPS = D // GROUP
TICKS = 2

norm_eps = 1e-05
masked_score = -1e30
gelu_root = 0.7978845608028654

bf16 = jnp.bfloat16
f32 = jnp.float32

MESH = pl.DeviceIdType.MESH
ZF, ZN, Y, X, CORE = range(5)
CHIP_AXES = 4
BLOCK = 48


NN = (((1,), (0,)), ((), ()))
NT = (((1,), (1,)), ((), ()))
TN = (((0,), (0,)), ((), ()))


def dot(left, right, dims=NN):
    return lax.dot_general(left, right, dims, preferred_element_type=f32)


def column_sum(values):
    return jnp.sum(values, axis=0, keepdims=True)


def aligned(index, multiple):
    return pl.multiple_of(index, multiple)


class Place:
    def __init__(self):
        wide = lax.axis_index("wide")
        narrow = lax.axis_index("narrow")
        self.wide, self.narrow = wide, narrow
        self.bits = (
            lax.div(wide, 4),
            lax.rem(lax.div(wide, 2), 2),
            lax.rem(wide, 2),
            lax.div(narrow, 2),
            lax.rem(narrow, 2),
        )
        self.core = self.bits[CORE]

    def other(self, axis):
        flip = 1 - 2 * self.bits[axis]
        if axis == X:
            return (self.wide, self.narrow + 2 * flip)
        if axis == CORE:
            return (self.wide, self.narrow + flip)
        return (self.wide + (4, 2, 1)[axis] * flip, self.narrow)

    def region(self, full=(), flipped=()):
        return tuple(
            pl.ds(0, 2)
            if axis in full
            else (1 - self.bits[axis] if axis in flipped else self.bits[axis])
            for axis in range(CHIP_AXES)
        )


def enter(place):
    barrier = pltpu.get_barrier_semaphore()
    for axis in range(5):
        pl.semaphore_signal(
            barrier, inc=1, device_id=place.other(axis), device_id_type=MESH
        )
    pl.semaphore_wait(barrier, 5)


def send(place, axis, src, dst, send_sem, recv_sem):
    return pltpu.make_async_remote_copy(
        src_ref=src,
        dst_ref=dst,
        send_sem=send_sem,
        recv_sem=recv_sem,
        device_id=place.other(axis),
        device_id_type=MESH,
    )


GATHER_COPIES = 15


class GatherChunk:
    def __init__(self, place, order, view, send_sems, recv_sems):
        self.place, self.axes, self.view = place, order + (CORE,), view
        self.send_sems, self.recv_sems = send_sems, recv_sems

    def copy(self, stage, piece, arriving=False):
        axis = self.axes[stage - 1]
        flipped = (self.axes[piece - 1],) if piece else ()
        bit = self.place.core
        if arriving and axis == CORE:
            bit = 1 - bit
        elif arriving:
            flipped += (axis,)
        where = self.view(self.place.region(self.axes[: max(piece - 1, 0)], flipped), bit)
        slot = stage * (stage - 1) // 2 + piece
        return send(
            self.place, axis, where, where, self.send_sems.at[slot], self.recv_sems.at[slot]
        )

    def step(self, stage):
        for piece in range(stage):
            self.copy(stage, piece, arriving=True).wait_recv()
        for later in range(stage + 1, CHIP_AXES + 2):
            self.copy(later, stage).start()

    def drain(self):
        for stage in range(1, CHIP_AXES + 2):
            for piece in range(stage):
                self.copy(stage, piece).wait_send()


class ReduceChunk:
    def __init__(self, place, order, view, lead, landings, send_sems, recv_sems):
        self.place, self.order, self.view, self.lead = place, order, view, lead
        self.landings, self.send_sems, self.recv_sems = landings, send_sems, recv_sems

    def copy(self, stage):
        if stage == 0:
            axis = CORE
            src = self.view(self.place.region(range(CHIP_AXES)), 1 - self.place.core)
        else:
            axis = self.order[stage - 1]
            src = self.view(
                self.place.region(self.order[stage:], (axis,)), self.place.core
            )
        return send(
            self.place, axis, src, self.landings[stage],
            self.send_sems.at[stage], self.recv_sems.at[stage],
        )

    def launch(self, stage):
        self.copy(stage).start()

    def absorb(self, stage):
        self.copy(stage).wait_recv()
        landing = self.landings[stage]
        free = tuple(sorted(self.order[stage:]))

        def add(block, carry):
            index = list(self.place.bits[:CHIP_AXES])
            where = ()
            rest = block
            for axis in reversed(free):
                index[axis] = lax.rem(rest, 2)
                where = (index[axis],) + where
                rest = lax.div(rest, 2)
            here = self.view(tuple(index), self.place.core)
            here[...] = here[...] + landing[self.lead + where]
            return carry

        lax.fori_loop(0, 2 ** len(free), add, 0)
        self.launch(stage + 1)

    def total(self):
        self.copy(CHIP_AXES).wait_recv()
        here = self.view(self.place.region(), self.place.core)
        return here[...].astype(f32) + self.landings[CHIP_AXES][...].astype(f32)

    def drain(self):
        for stage in range(CHIP_AXES + 1):
            self.copy(stage).wait_send()


def weight_chunks(weights):
    qkv_w, out_w, up_w, down_w = weights
    block = pl.ds(0, BLOCK)

    def qkv_view(group):
        def view(region, bit):
            columns = pl.ds(aligned(group * GROUP + bit * LANES, LANES), LANES)
            return qkv_w.at[(pl.ds(0, 3),) + region + (block, columns)]

        return view

    def half_view(whole, start, count):
        half = whole.shape[-1] // 2

        def view(region, bit):
            return whole.at[region + (block, pl.ds(aligned(bit * half + start, LANES), count))]

        return view

    def down_view(start, count):
        def view(region, bit):
            return down_w.at[region + (bit, pl.ds(0, down_w.shape[-2]), pl.ds(start, count))]

        return view

    half = up_w.shape[-1] // 4
    third = down_w.shape[-1] // 2
    return [
        (qkv_view(0), (3,), (BLOCK, LANES)),
        (qkv_view(1), (3,), (BLOCK, LANES)),
        (qkv_view(2), (3,), (BLOCK, LANES)),
        (half_view(out_w, 0, out_w.shape[-1] // 2), (), (BLOCK, out_w.shape[-1] // 2)),
        (half_view(up_w, 0, half), (), (BLOCK, half)),
        (half_view(up_w, half, half), (), (BLOCK, half)),
        (down_view(0, third), (), (down_w.shape[-2], third)),
        (down_view(third, third), (), (down_w.shape[-2], third)),
    ]


CHUNKS = 8
Q0, Q1, Q2, OUT, UP_A, UP_B, DOWN_A, DOWN_B = range(CHUNKS)

GATHER_ORDERS = {
    Q0: (ZF, ZN, Y, X),
    Q1: (ZF, ZN, X, Y),
    Q2: (Y, X, ZF, ZN),
    OUT: (X, Y, ZF, ZN),
    UP_A: (ZF, ZN, Y, X),
    UP_B: (ZF, ZN, X, Y),
    DOWN_A: (ZF, ZN, Y, X),
    DOWN_B: (ZF, ZN, X, Y),
}
REDUCE_ORDERS = {
    Q0: (X, Y, ZN, ZF),
    Q1: (Y, X, ZN, ZF),
    Q2: (X, Y, ZN, ZF),
    OUT: (Y, X, ZN, ZF),
    UP_A: (X, Y, ZN, ZF),
    UP_B: (Y, X, ZN, ZF),
    DOWN_A: (X, Y, ZN, ZF),
    DOWN_B: (Y, X, ZN, ZF),
}

GATHER_STEPS = {
    "FIRST": [(Q0, 0), (Q1, 0), (Q2, 0), (Q0, 1), (Q2, 1), (Q1, 1), (UP_A, 0), (UP_B, 0), (Q2, 2), (Q0, 2), (OUT, 0), (Q1, 2), (Q0, 3), (UP_A, 1), (OUT, 1), (Q1, 3), (UP_B, 1), (OUT, 2), (Q0, 4), (Q2, 3), (Q0, 5)],
    "FORWARD": [[(Q1, 4), (UP_A, 2), (DOWN_A, 0), (DOWN_B, 0)], [(Q1, 5), (UP_B, 2)], [], [(OUT, 3), (UP_A, 3)], [(Q2, 4)], [], [(Q2, 5), (UP_B, 3), (DOWN_A, 1)], [], [(DOWN_B, 1)], [(OUT, 4), (UP_A, 4)], [(UP_B, 4), (DOWN_A, 2)], [(OUT, 5), (UP_A, 5), (DOWN_B, 2)]],
    "NORMED": [],
    "UP": [(UP_B, 5)],
    "FEED": [[], [(DOWN_A, 3)], [(DOWN_B, 3)], [], [], [], [], [], [], [], [(DOWN_A, 4)], [(DOWN_B, 4)]],
    "GRAD_DOWN": [[], [(DOWN_A, 5), (DOWN_B, 5)], [], []],
    "BACK": [],
}

REDUCE_STEPS = {
    "STARTED": [(DOWN_A, 0)],
    "BACK": [[(DOWN_B, 0)], [], [], []],
    "GRAD_UP": [[(DOWN_A, 1)], [], [], [(DOWN_B, 1)]],
    "PREPARED": [(UP_A, 0), (UP_B, 0), (OUT, 0), (DOWN_A, 2)],
    "BACKWARD": [[], [(DOWN_B, 2)], [(DOWN_A, 3)], [], [(DOWN_B, 3)], [(Q0, 0)], [(UP_B, 1)], [(UP_A, 1)], [], [(Q0, 1), (Q1, 0), (OUT, 1)], [], []],
    "FINISHED": [[], [], [(UP_A, 2), (UP_B, 2)]],
    "RESID": [[], [(Q0, 2), (Q2, 0), (OUT, 2)], [(UP_A, 3)], []],
    "OUT": [[(Q1, 1), (UP_B, 3)], [(Q0, 3)], [(Q2, 1), (OUT, 3)], []],
    "REST": [(Q1, 2), (Q2, 2), (Q1, 3), (Q2, 3)],
}


class SmallSum:
    def __init__(self, place, values, landing, send_sems, recv_sems):
        self.place, self.values, self.landing = place, values, landing
        self.send_sems, self.recv_sems = send_sems, recv_sems

    def copy(self, axis):
        return send(
            self.place, axis, self.values.at[axis], self.landing.at[axis],
            self.send_sems.at[axis], self.recv_sems.at[axis],
        )

    def step(self, axis):
        self.copy(axis).wait()
        self.values[axis + 1] = self.values[axis] + self.landing[axis]
        if axis < CORE:
            self.copy(axis + 1).start()


def complete(values):
    lane = lax.broadcasted_iota(jnp.int32, values.shape, 1)
    total = jnp.sum(values, axis=1, keepdims=True)
    return jnp.where(lane == values.shape[1] - 1, -total, values)


def widen(values):
    return jnp.concatenate([values, jnp.zeros((values.shape[0], 1), values.dtype)], axis=1)


def spread(shards, device):
    count = shards.shape[1]
    unit = count // 8
    lane = lax.broadcasted_iota(jnp.int32, (1, count), 1)
    flat = lane + device * unit
    flat = jnp.where(lane >= unit, flat - unit + D, flat)
    flat = jnp.where(lane >= 2 * unit, lane - 2 * unit + 2 * D + device * 2 * unit, flat)
    flat = jnp.where(lane >= 4 * unit, lane - 4 * unit + 4 * D + device * 4 * unit, flat)
    row = lax.broadcasted_iota(jnp.int32, (8, count), 0)
    inside = flat - row * D
    mine = jnp.where((inside >= 0) & (inside < D), shards, 0.0)
    for _ in range(7):
        flat = jnp.where(flat >= D, flat - D, flat)
    column = lax.broadcasted_iota(jnp.int32, (D, count), 0)
    place = jnp.where(column == flat, 1.0, 0.0)
    return dot(mine.astype(bf16), place.astype(bf16), NT)


def inverse_size(full):
    return lax.rsqrt(jnp.mean(full * full, axis=1, keepdims=True) + norm_eps)


def norm_backward(grad, full, inverse, gain):
    scaled = grad * gain
    inner = jnp.sum(scaled * full, axis=1, keepdims=True)
    grad_full = scaled * inverse - full * (inverse * inverse * inverse * (inner * (1.0 / D)))
    return grad * full * inverse, grad_full - grad_full[:, D - 1 : D]


def gelu_and_slope(value):
    square = value * value
    bend = square * (gelu_root * 0.044715) + gelu_root
    half = 0.5 * jnp.tanh(value * bend) + 0.5
    act = value * half
    return act, half + act * (1.0 - half) * (6.0 * bend - 4.0 * gelu_root)


def norm_rows(rows, resid, gain, normed):
    full = complete(widen(resid[rows, :].astype(f32)))
    normed[rows, :] = (full * inverse_size(full) * gain).astype(bf16)


def project(group, normed, qkv_w, small, qkv):
    columns = pl.ds(aligned(group * GROUP, GROUP), GROUP)

    def body(part, carry):
        weight = qkv_w[part, :, :, :, :, :, columns].reshape(D, GROUP)
        bias = jnp.where(part == 1, 0.0, small[pl.ds(2 + lax.div(part, 2), 1), columns])
        qkv[:, pl.ds(aligned(part * D + group * GROUP, GROUP), GROUP)] = (
            dot(normed[...], weight) + bias
        ).astype(bf16)
        return carry

    lax.fori_loop(0, 3, body, 0)


def pair_columns(pair):
    return tuple(pl.ds(aligned(part * D + pair * LANES, LANES), LANES) for part in range(3))


def pair_forward(pair, block, cross, qkv, mixed, mixed_rest, lse):
    count = qkv.shape[0]
    lane = lax.broadcasted_iota(jnp.int32, (ROWS, LANES), 1)
    row = lax.broadcasted_iota(jnp.int32, (ROWS, ROWS), 0)
    column = lax.broadcasted_iota(jnp.int32, (ROWS, ROWS), 1)
    rows = pl.ds(block * ROWS, ROWS)
    last = (block + 1) * ROWS
    query_columns, key_columns, value_columns = pair_columns(pair)
    query = qkv[rows, query_columns] * jnp.asarray(HD**-0.5, bf16)
    key = qkv[pl.ds(0, last), key_columns]
    value = qkv[pl.ds(0, last), value_columns]
    value = jnp.concatenate([value, jnp.ones((last, LANES), bf16)], axis=1)
    outs = []
    stats = lse[rows, :]
    for head in range(2):
        mine = lane < HD if head == 0 else lane >= HD
        scores = dot(jnp.where(mine, query, jnp.zeros_like(query)), key, NT)
        parts = []
        for other in range(block + 1):
            part = scores[:, other * ROWS : (other + 1) * ROWS]
            if other == block:
                part = jnp.where(row >= column, part, masked_score)
            elif block * ROWS >= count // 2 and other * ROWS < count // 2:
                part = part + cross
            parts.append(part)
        scores = jnp.concatenate(parts, axis=1) if block else parts[0]
        largest = jnp.max(scores, axis=1, keepdims=True)
        summed = dot(jnp.exp(scores - largest).astype(bf16), value)
        outs.append(summed[:, :LANES] / summed[:, LANES:])
        stats = jnp.where(lane == 2 * pair + head, largest + jnp.log(summed[:, LANES:]), stats)
    lse[rows, :] = stats
    out = jnp.where(lane < HD, outs[0], outs[1])
    low = out.astype(bf16)
    mixed[rows, query_columns] = low
    mixed_rest[rows, query_columns] = (out - low.astype(f32)).astype(bf16)


def middle_rows(rows, resid, mixed, out_w, biases):
    branch = dot(mixed[rows, :], out_w[...].reshape(D, D))
    return widen(resid[rows, :].astype(f32)) + branch + biases[pl.ds(0, 1), :]


def feed_normed_rows(rows, resid, mixed, small, biases, out_w, normed, normed_t):
    full = complete(middle_rows(rows, resid, mixed, out_w, biases))
    values = (full * inverse_size(full) * small[pl.ds(1, 1), :]).astype(bf16)
    normed[rows, :] = values
    normed_t[:, rows] = jnp.transpose(values)


def feed_forward_columns(part, normed, small, up_w, activated, slopes):
    columns = pl.ds(aligned(part * GROUP, GROUP), GROUP)
    up = up_w[:, :, :, :, :, columns].reshape(D, GROUP)
    bias = small[pl.ds(4 + lax.div(part, GROUPS), 1), pl.ds(aligned(lax.rem(part, GROUPS) * GROUP, GROUP), GROUP)]
    act, slope = gelu_and_slope(dot(normed[...], up) + bias)
    activated[:, columns] = act.astype(bf16)
    slopes[:, columns] = slope.astype(bf16)


def feed_backward_rows(
    rows, starting, resid, cotangent, mixed, small, biases, weights, grad_pre, branch, grad_mixed, grad_normed, sums
):
    _, out_w, up_w, down_w = weights
    low_cot = cotangent[rows, :]
    grad_normed[...] = jnp.zeros(grad_normed.shape, f32)

    def body(part, carry):
        columns = pl.ds(aligned(part * FF_BLOCK, FF_BLOCK), FF_BLOCK)
        up = up_w[:, :, :, :, :, columns].reshape(D, FF_BLOCK)
        down = down_w[lax.div(part, 2), lax.rem(part, 2)].reshape(FF_BLOCK, D)
        grad = (dot(low_cot, down, NT) * grad_pre[rows, columns].astype(f32)).astype(bf16)
        grad_pre[rows, columns] = grad
        grad_normed[...] = grad_normed[...] + dot(grad, up, NT)
        total = column_sum(grad.astype(f32))
        here = pl.ds(4 + part, 1)
        sums[here, :] = jnp.where(starting, total, sums[here, :] + total)
        return carry

    lax.fori_loop(0, up_w.shape[-1] // FF_BLOCK, body, 0)
    full = complete(middle_rows(rows, resid, mixed, out_w, biases))
    gain_terms, grad_input = norm_backward(
        grad_normed[...], full, inverse_size(full), small[pl.ds(1, 1), :]
    )
    cot = low_cot.astype(f32)
    rounded = (cot + grad_input).astype(bf16)
    branch[rows, :] = rounded
    grad_mixed[rows, :] = dot(rounded, out_w[...].reshape(D, D), NT).astype(bf16)
    for where, terms in ((1, gain_terms), (8, rounded.astype(f32)), (9, cot)):
        total = column_sum(terms)
        here = pl.ds(where, 1)
        sums[here, :] = jnp.where(starting, total, sums[here, :] + total)


def feed_out_rows(rows, resid, mixed, biases, out_w, down_w, activated, total):
    total[...] = middle_rows(rows, resid, mixed, out_w, biases) + biases[pl.ds(1, 1), :]

    def body(part, carry):
        columns = pl.ds(aligned(part * FF_BLOCK, FF_BLOCK), FF_BLOCK)
        down = down_w[lax.div(part, 2), lax.rem(part, 2)].reshape(FF_BLOCK, D)
        total[...] = total[...] + dot(activated[rows, columns], down)
        return carry

    lax.fori_loop(0, down_w.shape[0] * down_w.shape[1], body, 0)
    return total[...].astype(bf16)


def pair_backward(pair, block, cross, qkv, grad_mixed, lse_t, delta_t, grad_query):
    count = qkv.shape[0]
    lane = lax.broadcasted_iota(jnp.int32, (ROWS, LANES), 1)
    row = lax.broadcasted_iota(jnp.int32, (ROWS, ROWS), 0)
    column = lax.broadcasted_iota(jnp.int32, (ROWS, ROWS), 1)
    keys = pl.ds(block * ROWS, ROWS)
    queries = pl.ds(block * ROWS, count - block * ROWS)
    query_columns, key_columns, value_columns = pair_columns(pair)
    key = qkv[keys, key_columns] * jnp.asarray(HD**-0.5, bf16)
    value = qkv[keys, value_columns]
    query = qkv[queries, query_columns]
    grad = grad_mixed[queries, query_columns]
    grad_values = []
    grad_keys = []
    grad_queries = None
    for head in range(2):
        mine = lane < HD if head == 0 else lane >= HD
        my_key = jnp.where(mine, key, jnp.zeros_like(key))
        my_value = jnp.where(mine, value, jnp.zeros_like(value))
        scores = dot(my_key, query, NT)
        grad_probs = dot(my_value, grad, NT)
        log_row = lse_t[pl.ds(2 * pair + head, 1), queries]
        dot_row = delta_t[pl.ds(2 * pair + head, 1), queries]
        probs = []
        grad_scores = []
        for other in range(count // ROWS - block):
            span = slice(other * ROWS, (other + 1) * ROWS)
            shifted = scores[:, span] - log_row[:, span]
            if other == 0:
                shifted = jnp.where(column >= row, shifted, masked_score)
            elif block * ROWS < count // 2 and (block + other) * ROWS >= count // 2:
                shifted = shifted + cross
            prob = jnp.exp(shifted)
            probs.append(prob.astype(bf16))
            grad_scores.append((prob * (grad_probs[:, span] - dot_row[:, span])).astype(bf16))
        probs = jnp.concatenate(probs, axis=1) if len(probs) > 1 else probs[0]
        grad_scores = jnp.concatenate(grad_scores, axis=1) if len(grad_scores) > 1 else grad_scores[0]
        grad_values.append(dot(probs, grad))
        grad_keys.append(dot(grad_scores, query))
        part = dot(my_key, grad_scores, TN)
        grad_queries = part if grad_queries is None else grad_queries + part
    qkv[keys, value_columns] = jnp.where(lane < HD, grad_values[0], grad_values[1]).astype(bf16)
    qkv[keys, key_columns] = (
        jnp.where(lane < HD, grad_keys[0], grad_keys[1]) * HD**-0.5
    ).astype(bf16)
    if block == 0:
        grad_query[...] = grad_queries
    else:
        grad_query[:, queries] = grad_query[:, queries] + grad_queries


def backward_rows(mixed, mixed_rest, grad_mixed, lse, lse_t, delta_t):
    heads = lse_t.shape[0]
    lse_t[...] = jnp.transpose(lse[...])[:heads]
    head = lax.broadcasted_iota(jnp.int32, (heads, D), 0)
    column = lax.broadcasted_iota(jnp.int32, (heads, D), 1)
    pick = jnp.where((column >= head * HD) & (column < head * HD + HD), 1.0, 0.0).astype(f32)

    def body(block, carry):
        rows = pl.ds(aligned(block * ROWS, ROWS), ROWS)
        whole = mixed[rows, :].astype(f32) + mixed_rest[rows, :].astype(f32)
        product = whole * grad_mixed[rows, :].astype(f32)
        delta_t[:, rows] = lax.dot_general(
            pick, product, NT, precision=lax.Precision.HIGHEST, preferred_element_type=f32
        )
        return carry

    lax.fori_loop(0, mixed.shape[0] // ROWS, body, 0)


def layer_kernel(
    resid, cotangent, qkv_in, out_in, up_in, down_in, small_in, biases_in, lengths,
    out_resid, grad_resid, qkv_out, out_out, up_out, down_out, small_out, qkv_away, rest_away, activated_away,
    *scratch,
):
    scratch = list(scratch)
    take = lambda n: [scratch.pop(0) for _ in range(n)]
    weights = take(4)
    qkv_w, out_w, up_w, down_w = weights
    landings = [take(CHIP_AXES + 1) for _ in range(CHUNKS)]
    normed, qkv, mixed, mixed_rest, grad_mixed, lse, staging, down_g, out_g = take(9)
    branch = mixed_rest
    my_rows, pair_rows, biases, small_values, small_landing, sum_values, sum_landing = take(7)
    (
        pair_send, pair_recv, small_send, small_recv, sum_send, sum_recv,
        gather_send, gather_recv, reduce_send, reduce_recv,
        final_send, final_recv, final_own, row_sems,
    ) = take(14)
    activated = qkv
    qkv = activated.at[:, pl.ds(0, 3 * D)]
    count = resid.shape[0]
    place = Place()
    core = place.core
    cross = jnp.where(lengths[0, 0] == count, 0.0, masked_score)
    enter(place)

    shards = (qkv_in, out_in, up_in)
    shard_rows = BLOCK // 2
    offsets = ((0, 0), (0, qkv_in.shape[1]), (shard_rows, 0))
    for shard, (top, left) in zip(shards, offsets):
        values = shard[...].astype(f32)
        values = widen(values) if values.shape[1] == D - 1 else values
        my_rows[pl.ds(top, shard_rows), pl.ds(left, values.shape[1])] = values
    pair_copy = send(place, CORE, my_rows, pair_rows, pair_send.at[0], pair_recv.at[0])
    pair_copy.start()
    small_values[0] = spread(small_in[...], place.wide * 4 + place.narrow)
    small_sum = SmallSum(place, small_values, small_landing, small_send, small_recv)
    small_sum.copy(0).start()
    biases[...] = widen(biases_in[...])

    def own_block(slot, first, width):
        top, left = offsets[slot]
        here = (pl.ds(top, shard_rows), pl.ds(aligned(left + first, LANES), width))
        mine, theirs = my_rows[here], pair_rows[here]
        return jnp.concatenate(
            [jnp.where(core == 0, mine, theirs), jnp.where(core == 0, theirs, mine)], axis=0
        ).astype(bf16)

    here = place.region()
    gathers = [
        GatherChunk(place, GATHER_ORDERS[index], view, gather_send.at[index], gather_recv.at[index])
        for index, (view, _, _) in enumerate(weight_chunks(weights))
    ]
    down_w[here + (core,)] = widen(down_in[...].astype(f32)).astype(bf16)
    pair_copy.wait()
    for group in range(GROUPS):
        for part in range(3):
            first = group * GROUP + core * LANES
            qkv_w[(part,) + here + (slice(None), pl.ds(aligned(first, LANES), LANES))] = own_block(
                0, part * D + first, LANES
            )
    opening = list(GATHER_STEPS["FIRST"])
    while opening[0] in ((Q0, 0), (Q1, 0), (Q2, 0)):
        gathers[opening.pop(0)[0]].step(0)
    for slot, whole in ((1, out_w), (2, up_w)):
        half = whole.shape[-1] // 2
        first = aligned(core * half, LANES)
        whole[here + (slice(None), pl.ds(first, half))] = own_block(slot, first, half)

    lse[...] = jnp.zeros_like(lse)

    def norm_all():
        def body(block, carry):
            norm_rows(
                pl.ds(aligned(block * ROWS, ROWS), ROWS), resid, small_values[5][0:1], normed
            )
            return carry

        lax.fori_loop(0, count // ROWS, body, 0)

    axis = 0
    for number, (chunk, stage) in enumerate(opening):
        if (chunk, stage) == (Q0, 5):
            norm_all()
        gathers[chunk].step(stage)
        while axis <= CORE and (axis + 1) * (opening.index((Q0, 4)) + 1) <= (number + 1) * 5:
            small_sum.step(axis)
            axis += 1

    small = small_values.at[5]
    save = pltpu.make_async_copy(qkv, qkv_away, row_sems.at[4])
    blocks = count // ROWS
    pairs = H // 2
    per_group = pairs // GROUPS
    ticks = GATHER_STEPS["FORWARD"]
    after_up = GATHER_STEPS["FEED"]

    def gather_steps(where):
        for chunk, stage in GATHER_STEPS[where]:
            gathers[chunk].step(stage)

    def after(number, index, steps_of, run):
        for which in range(number):
            steps = steps_of(which)
            if steps:
                @pl.when(index == which)
                def _():
                    for chunk, stage in steps:
                        run(chunk, stage)

    def forward(pair, carry):
        @pl.when(lax.rem(pair, per_group) == 0)
        def _():
            project(lax.div(pair, per_group), normed, qkv_w, small, qkv)

        @pl.when(pair == pairs - per_group)
        def _():
            save.start()

        for block in range(blocks):
            pair_forward(pair, block, cross, qkv, mixed, mixed_rest, lse)
            if (block + 1) * TICKS % blocks == 0:
                turn = (block + 1) * TICKS // blocks - 1
                after(
                    pairs, pair, lambda which: ticks[which * TICKS + turn],
                    lambda chunk, stage: gathers[chunk].step(stage),
                )
        return carry

    lax.fori_loop(0, pairs, forward, 0)
    save.wait()
    pltpu.make_async_copy(mixed_rest, rest_away, row_sems.at[3]).start()

    sums = sum_values.at[0]
    sums[...] = jnp.zeros(sums.shape, f32)
    def reduce_chunks(qkv_g):
        return [
            ReduceChunk(
                place, REDUCE_ORDERS[index], view, (slice(None),) * len(lead),
                landings[index], reduce_send.at[index], reduce_recv.at[index],
            )
            for index, (view, lead, _) in enumerate(weight_chunks((qkv_g, out_g, up_w, down_g)))
        ]

    reduces = reduce_chunks(qkv_w)

    def emit_rows(target, block, sem, values):
        rows = pl.ds(aligned(block * ROWS, ROWS), ROWS)

        @pl.when(block > 0)
        def _():
            pltpu.make_async_copy(staging, target.at[rows, :], sem).wait()

        staging[...] = values
        pltpu.make_async_copy(staging, target.at[rows, :], sem).start()

    def emit_last(target, sem):
        pltpu.make_async_copy(staging, target.at[pl.ds(0, ROWS), :], sem).wait()

    def reduce_steps(where):
        for chunk, stage in REDUCE_STEPS[where]:
            reduces[chunk].absorb(stage)

    def absorb(chunk, stage):
        reduces[chunk].absorb(stage)

    def feed_forward(grad_pre, normed_t, grad_total):
        def normed_body(block, carry):
            rows = pl.ds(aligned(block * ROWS, ROWS), ROWS)
            feed_normed_rows(rows, resid, mixed, small, biases, out_w, grad_mixed, normed_t)
            return carry

        gather_steps("NORMED")
        lax.fori_loop(0, blocks, normed_body, 0)
        gather_steps("UP")

        def there(part, carry):
            feed_forward_columns(part, grad_mixed, small, up_w, activated, grad_pre)
            after(
                len(after_up), part, lambda which: after_up[which],
                lambda chunk, stage: gathers[chunk].step(stage),
            )
            return carry

        lax.fori_loop(0, len(after_up), there, 0)

        def grad_down(part, carry):
            columns = pl.ds(aligned(part * FF_BLOCK, FF_BLOCK), FF_BLOCK)
            down_g[lax.div(part, 2), lax.rem(part, 2)] = (
                dot(activated[:, columns], cotangent[...], TN)
                .astype(bf16)
                .reshape(down_g.shape[2:])
            )
            after(
                4, part, lambda which: GATHER_STEPS["GRAD_DOWN"][which],
                lambda chunk, stage: gathers[chunk].step(stage),
            )
            return carry

        lax.fori_loop(0, up_w.shape[-1] // FF_BLOCK, grad_down, 0)
        reduces[DOWN_A].launch(0)
        reduces[DOWN_B].launch(0)
        keep = pltpu.make_async_copy(activated, activated_away, row_sems.at[0])
        keep.start()
        gather_steps("BACK")
        for chunk in gathers:
            chunk.drain()
        reduce_steps("STARTED")
        pltpu.make_async_copy(mixed_rest, rest_away, row_sems.at[3]).wait()
        keep.wait()
        pltpu.make_async_copy(qkv_away, qkv, row_sems.at[4]).start()

        def back(block, carry):
            rows = pl.ds(aligned(block * ROWS, ROWS), ROWS)
            feed_backward_rows(
                rows, block == 0, resid, cotangent, mixed, small, biases, weights,
                grad_pre, branch, grad_mixed, grad_total, sums,
            )
            after(
                blocks, block, lambda which: REDUCE_STEPS["BACK"][which],
                lambda chunk, stage: reduces[chunk].absorb(stage),
            )
            return carry

        lax.fori_loop(0, blocks, back, 0)

        def grad_up(part, carry):
            columns = pl.ds(aligned(part * FF_BLOCK, FF_BLOCK), FF_BLOCK)
            up_w[:, :, :, :, :, columns] = (
                dot(normed_t[...], grad_pre[:, columns])
                .astype(bf16)
                .reshape((2,) * CHIP_AXES + (BLOCK, FF_BLOCK))
            )
            after(
                len(REDUCE_STEPS["GRAD_UP"]), part, lambda which: REDUCE_STEPS["GRAD_UP"][which],
                lambda chunk, stage: reduces[chunk].absorb(stage),
            )
            return carry

        lax.fori_loop(0, up_w.shape[-1] // FF_BLOCK, grad_up, 0)
        reduces[UP_A].launch(0)
        reduces[UP_B].launch(0)

        def grad_out(half, carry):
            columns = pl.ds(aligned(half * (D // 2), LANES), D // 2)
            out_g[half] = (
                dot(mixed[:, columns], branch[...], TN).astype(bf16).reshape(out_g.shape[1:])
            )
            return carry

        lax.fori_loop(0, 2, grad_out, 0)
        reduces[OUT].launch(0)

    pl.run_scoped(
        feed_forward,
        pltpu.VMEM((count, up_w.shape[-1]), bf16),
        pltpu.VMEM((D, count), bf16),
        pltpu.VMEM((ROWS, D), f32),
    )
    pltpu.make_async_copy(qkv_away, qkv, row_sems.at[4]).wait()

    def attention_backward(qkv_g, row_total, lse_t, delta_t, grad_query, normed_t):
        reduces[:] = reduce_chunks(qkv_g)

        def turn(block, carry):
            rows = pl.ds(aligned(block * ROWS, ROWS), ROWS)
            normed_t[:, rows] = jnp.transpose(normed[rows, :])
            return carry

        lax.fori_loop(0, blocks, turn, 0)
        back_again = pltpu.make_async_copy(rest_away, normed, row_sems.at[3])
        back_again.start()
        back_again.wait()
        backward_rows(mixed, normed, grad_mixed, lse, lse_t, delta_t)
        reduce_steps("PREPARED")
        ticks = REDUCE_STEPS["BACKWARD"]

        def finish_group(group):
            columns = pl.ds(aligned(group * GROUP, GROUP), GROUP)

            def grad_columns(part):
                return pl.ds(aligned(part * D + group * GROUP, GROUP), GROUP)

            def of_weight(part, carry):
                grads = qkv[:, grad_columns(part)]
                qkv_g[part, :, :, :, :, :, columns] = (
                    dot(normed_t[...], grads)
                    .astype(bf16)
                    .reshape((2,) * CHIP_AXES + (BLOCK, GROUP))
                )
                here = jnp.where(part == 1, 10, 2 + lax.div(part, 2))
                sums[pl.ds(here, 1), columns] = column_sum(grads.astype(f32))
                return carry

            lax.fori_loop(0, 3, of_weight, 0)

        def backward(pair, carry):
            for block in range(blocks):
                pair_backward(pair, block, cross, qkv, grad_mixed, lse_t, delta_t, grad_query)
                if (block + 1) * TICKS % blocks == 0:
                    turn = (block + 1) * TICKS // blocks - 1
                    after(
                        pairs, pair, lambda which: ticks[which * TICKS + turn],
                        lambda chunk, stage: reduces[chunk].absorb(stage),
                    )
            qkv[:, pair_columns(pair)[0]] = jnp.transpose(grad_query[...]).astype(bf16)

            @pl.when(lax.rem(pair, per_group) == per_group - 1)
            def _():
                finish_group(lax.div(pair, per_group))

            def finished(chunk, stage):
                if stage is None:
                    reduces[chunk].launch(0)
                else:
                    reduces[chunk].absorb(stage)

            def steps_of(which):
                if which % per_group < per_group - 1:
                    return []
                group = which // per_group
                return [(group, None)] + REDUCE_STEPS["FINISHED"][group]

            after(pairs, pair, steps_of, finished)
            return carry

        lax.fori_loop(0, pairs, backward, 0)

        def resid_rows(block, carry):
            rows = pl.ds(aligned(block * ROWS, ROWS), ROWS)
            row_total[...] = jnp.zeros(row_total.shape, f32)

            def add(part, carry):
                grads = qkv[rows, pl.ds(aligned(part * D, D), D)]
                row_total[...] = row_total[...] + dot(grads, qkv_w[part].reshape(D, D), NT)
                return carry

            lax.fori_loop(0, 3, add, 0)
            full = complete(widen(resid[rows, :].astype(f32)))
            gain_terms, grad_input = norm_backward(
                row_total[...], full, inverse_size(full), small[pl.ds(0, 1), :]
            )
            emit_rows(
                grad_resid, block, row_sems.at[2],
                (branch[rows, :].astype(f32) + grad_input).astype(bf16),
            )
            total = column_sum(gain_terms)
            sums[pl.ds(0, 1), :] = jnp.where(block == 0, total, sums[pl.ds(0, 1), :] + total)
            after(blocks, block, lambda which: REDUCE_STEPS["RESID"][which], absorb)
            return carry

        lax.fori_loop(0, blocks, resid_rows, 0)
        reload = pltpu.make_async_copy(activated_away, activated, row_sems.at[0])
        reload.start()
        sum_all = SmallSum(place, sum_values, sum_landing, sum_send, sum_recv)
        sum_all.copy(0).start()
        reload.wait()
        emit_last(grad_resid, row_sems.at[2])

        def out_rows(block, carry):
            rows = pl.ds(aligned(block * ROWS, ROWS), ROWS)
            values = feed_out_rows(rows, resid, mixed, biases, out_w, down_w, activated, row_total)
            emit_rows(out_resid, block, row_sems.at[1], values)
            after(blocks, block, lambda which: REDUCE_STEPS["OUT"][which], absorb)
            for which in range(blocks):
                @pl.when(block == which)
                def _():
                    sum_all.step(which)

            return carry

        lax.fori_loop(0, blocks, out_rows, 0)
        for axis in range(blocks, CORE + 1):
            sum_all.step(axis)
        reduce_steps("REST")
        small_out[...] = sum_values[5]

        for chunk, start in ((DOWN_A, 0), (DOWN_B, D // 2)):
            down_out[:, pl.ds(start, D // 2)] = reduces[chunk].total()
        their_rows = pl.ds(aligned((1 - core) * shard_rows, 8), shard_rows)
        kept_rows = pl.ds(aligned(core * shard_rows, 8), shard_rows)
        copies = []

        def deliver(slot, part_of, target):
            away = send(
                place, CORE, part_of(their_rows), target, final_send.at[slot], final_recv.at[slot]
            )
            away.start()
            home = pltpu.make_async_copy(part_of(kept_rows), target, final_own.at[slot])
            home.start()
            copies.extend((away, home))

        finals = pair_rows
        half = up_w.shape[-1] // 4
        finals[:, pl.ds(0, half)] = reduces[UP_A].total()
        finals[:, pl.ds(half, half)] = reduces[UP_B].total()
        deliver(
            0, lambda rows: finals.at[rows, pl.ds(0, 2 * half)],
            up_out.at[:, pl.ds(aligned(core * 2 * half, LANES), 2 * half)],
        )
        first = 2 * half
        finals[:, pl.ds(first, D // 2)] = reduces[OUT].total()
        deliver(
            1, lambda rows: finals.at[rows, pl.ds(2 * half, D // 2)],
            out_out.at[:, pl.ds(aligned(core * (D // 2), LANES), D // 2)],
        )
        first += D // 2
        for group in range(GROUPS):
            total = reduces[group].total()
            for part in range(3):
                here = pl.ds(first, LANES)
                finals[:, here] = total[part]
                deliver(
                    2 + group * 3 + part, lambda rows, here=here: finals.at[rows, here],
                    qkv_out.at[:, pl.ds(aligned(part * D + group * GROUP + core * LANES, LANES), LANES)],
                )
                first += LANES
        for copy in copies:
            copy.wait()
        for chunk in reduces:
            chunk.drain()
        emit_last(out_resid, row_sems.at[1])

    pl.run_scoped(
        attention_backward,
        pltpu.VMEM(qkv_w.shape, bf16),
        pltpu.VMEM((ROWS, D), f32),
        pltpu.VMEM((16, count), f32),
        pltpu.VMEM((16, count), f32),
        pltpu.VMEM((LANES, count), f32),
        pltpu.VMEM((D, count), bf16),
    )


def layer_by_kernel(resid, cotangent, qkv_in, out_in, up_in, down_in, small_in, biases, lengths):
    count = resid.shape[0]
    grid = (2,) * CHIP_AXES
    ff = up_in.shape[1]
    weight_shapes = [
        (3,) + grid + (BLOCK, D),
        grid + (BLOCK, D),
        grid + (BLOCK, ff),
        grid + (2, down_in.shape[0], D),
    ]
    weights = [pltpu.VMEM(shape, bf16) for shape in weight_shapes]
    shapes = [jax.ShapeDtypeStruct(shape, bf16) for shape in weight_shapes]
    landings = [
        pltpu.VMEM(lead + (2,) * (CHIP_AXES - stage) + block, bf16)
        for _, lead, block in weight_chunks(shapes)
        for stage in range(CHIP_AXES + 1)
    ]
    dma = pltpu.SemaphoreType.DMA
    small_rows, sum_rows = 8, 16
    scratch = (
        weights
        + landings
        + [
            pltpu.VMEM((count, D), bf16),
            pltpu.VMEM((count, ff), bf16),
            pltpu.VMEM((count, D), bf16),
            pltpu.VMEM((count, D), bf16),
            pltpu.VMEM((count, D), bf16),
            pltpu.VMEM((count, LANES), f32),
            pltpu.VMEM((ROWS, D), bf16),
            pltpu.VMEM(weight_shapes[3], bf16),
            pltpu.VMEM(weight_shapes[1], bf16),
            pltpu.VMEM((BLOCK, (3 * D + D + ff) // 2), f32),
            pltpu.VMEM((BLOCK, (3 * D + D + ff) // 2), f32),
            pltpu.VMEM((2, D), f32),
            pltpu.VMEM((6, small_rows, D), f32),
            pltpu.VMEM((5, small_rows, D), f32),
            pltpu.VMEM((6, sum_rows, D), f32),
            pltpu.VMEM((5, sum_rows, D), f32),
            dma((3,)),
            dma((3,)),
            dma((5,)),
            dma((5,)),
            dma((5,)),
            dma((5,)),
            dma((CHUNKS, GATHER_COPIES)),
            dma((CHUNKS, GATHER_COPIES)),
            dma((CHUNKS, CHIP_AXES + 1)),
            dma((CHUNKS, CHIP_AXES + 1)),
            dma((11,)),
            dma((11,)),
            dma((11,)),
            dma((5,)),
        ]
    )
    in_vmem = pl.BlockSpec(memory_space=pltpu.VMEM)
    in_hbm = pl.BlockSpec(memory_space=pl.ANY)
    shard_rows = BLOCK // 2
    return pl.pallas_call(
        layer_kernel,
        out_shape=[
            jax.ShapeDtypeStruct((count, D), bf16),
            jax.ShapeDtypeStruct((count, D), bf16),
            jax.ShapeDtypeStruct((shard_rows, 3 * D), f32),
            jax.ShapeDtypeStruct((shard_rows, D), f32),
            jax.ShapeDtypeStruct((shard_rows, ff), f32),
            jax.ShapeDtypeStruct((down_in.shape[0], D), f32),
            jax.ShapeDtypeStruct((sum_rows, D), f32),
            jax.ShapeDtypeStruct((count, 3 * D), bf16),
            jax.ShapeDtypeStruct((count, D), bf16),
            jax.ShapeDtypeStruct((count, ff), bf16),
        ],
        in_specs=[in_vmem] * 8 + [pl.BlockSpec(memory_space=pltpu.SMEM)],
        out_specs=[in_hbm] * 2 + [in_vmem] * 5 + [in_hbm] * 3,
        scratch_shapes=scratch,
        compiler_params=pltpu.CompilerParams(
            collective_id=1, has_side_effects=True, vmem_limit_bytes=VMEM_BYTES
        ),
        name="layer",
    )(resid, cotangent, qkv_in, out_in, up_in, down_in, small_in, biases, lengths)


VMEM_BYTES = 63 * 2**20


def device_index():
    return lax.axis_index("wide") * lax.axis_size("narrow") + lax.axis_index("narrow")


def on_device_by_kernel(
    resid, gain_attn, qkv_weight, qv_bias, out_weight, out_bias, gain_mlp,
    up_weight, up_bias, down_weight, down_bias, cotangent, seq_lengths,
):
    devices = lax.axis_size("wide") * lax.axis_size("narrow")
    width = out_weight.shape[1]
    small = jnp.concatenate([gain_attn, gain_mlp, qv_bias, up_bias]).astype(f32)
    biases = jnp.stack([out_bias, down_bias]).astype(f32)
    out_resid, grad_resid, qkv, out, up, down, sums, _, _, _ = layer_by_kernel(
        resid, jnp.pad(cotangent, ((0, 0), (0, D - width))), qkv_weight, out_weight, up_weight, down_weight,
        small.reshape(1, -1), biases, seq_lengths,
    )
    sums = sums.reshape(-1)

    def shard(first, count):
        part = count // devices
        return lax.dynamic_slice(sums, (first + device_index() * part,), (part,))

    ff = up_weight.shape[1]
    last = 4 * D + ff
    return (
        out_resid[:, :width],
        grad_resid[:, :width],
        shard(0, D),
        qkv,
        shard(2 * D, 2 * D),
        out[:, :width],
        sums[last : last + width],
        shard(D, D),
        up,
        shard(4 * D, ff),
        down[:, :width],
        sums[last + D : last + D + width],
    )


def compressed_norm(values, gain_vec):
    row_total = jnp.sum(values, axis=-1, keepdims=True)
    full_vector = jnp.concatenate([values, -row_total], axis=-1)
    mean_sq = jnp.mean(full_vector * full_vector, axis=-1, keepdims=True)
    return full_vector * lax.rsqrt(mean_sq + norm_eps) * gain_vec


def contract_rows(left_side, right_side):
    return lax.dot_general(
        left_side, right_side, (((0,), (0,)), ((), ())), preferred_element_type=jnp.float32
    )


def contract_cols(left_side, right_side):
    return lax.dot_general(
        left_side, right_side, (((1,), (1,)), ((), ())), preferred_element_type=jnp.float32
    )


def segment_ids(lengths, row_count):
    places = jnp.arange(row_count, dtype=jnp.int32)
    seq_ends = jnp.cumsum(lengths)
    segment = jnp.sum((places[:, None] >= seq_ends[None, :]).astype(jnp.int32), axis=1)
    return (places, segment)


def block_scores(query_block, key_heads, places, segment, first_row, last_row):
    scores = jnp.einsum(
        "qhd,khd->hqk", query_block, key_heads[:last_row], preferred_element_type=jnp.float32
    ) * HD ** (-0.5)
    allowed = (segment[first_row:last_row, None] == segment[None, :last_row]) & (
        places[None, :last_row] <= places[first_row:last_row, None]
    )
    return jnp.where(allowed[None], scores, masked_score)


def attend_forward(query_heads, key_heads, value_heads, places, segment):
    row_count = query_heads.shape[0]
    block_rows = min(512, row_count)
    mixed_parts = []
    log_parts = []
    for block_index in range(row_count // block_rows):
        first_row = block_index * block_rows
        last_row = first_row + block_rows
        scores = block_scores(
            query_heads[first_row:last_row], key_heads, places, segment, first_row, last_row
        )
        row_max = jnp.max(scores, axis=-1, keepdims=True)
        exp_scores = jnp.exp(scores - row_max)
        summed = jnp.sum(exp_scores, axis=-1, keepdims=True)
        attn_probs = (exp_scores / summed).astype(jnp.bfloat16)
        mixed_parts.append(
            jnp.einsum(
                "hqk,khd->qhd",
                attn_probs,
                value_heads[:last_row],
                preferred_element_type=jnp.float32,
            )
        )
        log_parts.append(row_max + jnp.log(summed))
    return (jnp.concatenate(mixed_parts, axis=0), jnp.concatenate(log_parts, axis=1))


def attend_backward(query_heads, key_heads, value_heads, grad_mixed, log_sums, places, segment):
    row_count = query_heads.shape[0]
    block_rows = min(512, row_count)
    grad_query_parts = []
    grad_keys = jnp.zeros(key_heads.shape, jnp.float32)
    grad_values = jnp.zeros(value_heads.shape, jnp.float32)
    for block_index in range(row_count // block_rows):
        first_row = block_index * block_rows
        last_row = first_row + block_rows
        query_block = query_heads[first_row:last_row]
        grad_block = grad_mixed[first_row:last_row]
        scores = block_scores(query_block, key_heads, places, segment, first_row, last_row)
        attn_probs = jnp.exp(scores - log_sums[:, first_row:last_row])
        grad_probs = jnp.einsum(
            "qhd,khd->hqk", grad_block, value_heads[:last_row], preferred_element_type=jnp.float32
        )
        row_dot = jnp.sum(attn_probs * grad_probs, axis=-1, keepdims=True)
        grad_scores = (attn_probs * (grad_probs - row_dot)).astype(jnp.bfloat16)
        grad_query_parts.append(
            jnp.einsum(
                "hqk,khd->qhd",
                grad_scores,
                key_heads[:last_row],
                preferred_element_type=jnp.float32,
            )
            * HD ** (-0.5)
        )
        grad_keys = grad_keys.at[:last_row].add(
            jnp.einsum("hqk,qhd->khd", grad_scores, query_block, preferred_element_type=jnp.float32)
            * HD ** (-0.5)
        )
        grad_values = grad_values.at[:last_row].add(
            jnp.einsum(
                "hqk,qhd->khd",
                attn_probs.astype(jnp.bfloat16),
                grad_block,
                preferred_element_type=jnp.float32,
            )
        )
    return (jnp.concatenate(grad_query_parts, axis=0), grad_keys, grad_values)


def attention_part(resid_f, weights, places, segment):
    row_count = resid_f.shape[0]
    normed = compressed_norm(resid_f, weights[6].astype(jnp.float32)).astype(jnp.bfloat16)
    bias_pair = weights[4].astype(jnp.float32)
    bias_row = jnp.concatenate([bias_pair[:D], jnp.zeros((D,), jnp.float32), bias_pair[D:]])
    qkv_low = (jnp.dot(normed, weights[0], preferred_element_type=jnp.float32) + bias_row).astype(
        jnp.bfloat16
    )
    query_heads = qkv_low[:, :D].reshape(row_count, H, HD)
    key_heads = qkv_low[:, D : 2 * D].reshape(row_count, H, HD)
    value_heads = qkv_low[:, 2 * D :].reshape(row_count, H, HD)
    mixed_heads, log_sums = attend_forward(query_heads, key_heads, value_heads, places, segment)
    mixed_low = mixed_heads.reshape(row_count, D).astype(jnp.bfloat16)
    return (normed, query_heads, key_heads, value_heads, mixed_low, log_sums)


def mlp_part(middle, weights):
    normed_mlp = compressed_norm(middle, weights[7].astype(jnp.float32)).astype(jnp.bfloat16)
    pre_act = jnp.dot(normed_mlp, weights[2], preferred_element_type=jnp.float32) + weights[
        5
    ].astype(jnp.float32)
    activated = jax.nn.gelu(pre_act, approximate=True).astype(jnp.bfloat16)
    return (normed_mlp, pre_act, activated)


def on_device(
    resid,
    gain_attn,
    qkv_weight,
    qv_bias,
    out_weight,
    out_bias,
    gain_mlp,
    up_weight,
    up_bias,
    down_weight,
    down_bias,
    cotangent,
    seq_lengths,
):
    shards = (qkv_weight, out_weight, up_weight, down_weight, qv_bias, up_bias, gain_attn, gain_mlp)
    gathered = (
        lax.all_gather(shards[0], ("wide", "narrow"), axis=0, tiled=True),
        lax.all_gather(shards[1], ("wide", "narrow"), axis=0, tiled=True),
        lax.all_gather(shards[2], ("wide", "narrow"), axis=0, tiled=True),
        lax.all_gather(shards[3], ("wide", "narrow"), axis=0, tiled=True),
        lax.all_gather(shards[4], ("wide", "narrow"), axis=0, tiled=True),
        lax.all_gather(shards[5], ("wide", "narrow"), axis=0, tiled=True),
        lax.all_gather(shards[6], ("wide", "narrow"), axis=0, tiled=True),
        lax.all_gather(shards[7], ("wide", "narrow"), axis=0, tiled=True),
    )
    row_count = resid.shape[0]
    places, segment = segment_ids(seq_lengths[0], row_count)
    resid_f = resid.astype(jnp.float32)
    attn_first = attention_part(resid_f, gathered, places, segment)
    middle = (
        resid_f
        + jnp.dot(attn_first[4], gathered[1], preferred_element_type=jnp.float32)
        + out_bias.astype(jnp.float32)
    )
    mlp_first = mlp_part(middle, gathered)
    out_resid = (
        middle
        + jnp.dot(mlp_first[2], gathered[3], preferred_element_type=jnp.float32)
        + down_bias.astype(jnp.float32)
    ).astype(jnp.bfloat16)
    weights_back = gathered
    normed_mlp, pre_act, activated = mlp_part(middle, weights_back)
    grad_out = cotangent.astype(jnp.float32)
    grad_w_down = contract_rows(activated, cotangent)
    grad_b_down = jnp.sum(grad_out, axis=0)
    grad_act = contract_cols(cotangent, weights_back[3])
    gelu_value, gelu_pull = jax.vjp(partial(jax.nn.gelu, approximate=True), pre_act)
    grad_pre = gelu_pull(grad_act)[0].astype(jnp.bfloat16)
    grad_w_up = contract_rows(normed_mlp, grad_pre)
    grad_b_up = jnp.sum(grad_pre.astype(jnp.float32), axis=0)
    grad_normed_mlp = contract_cols(grad_pre, weights_back[2])
    norm_value, norm_pull = jax.vjp(compressed_norm, middle, weights_back[7].astype(jnp.float32))
    grad_middle_norm, grad_g_mlp = norm_pull(grad_normed_mlp)
    grad_middle = grad_out + grad_middle_norm
    grad_branch = grad_middle.astype(jnp.bfloat16)
    grad_b_out = jnp.sum(grad_branch.astype(jnp.float32), axis=0)
    normed, query_heads, key_heads, value_heads, mixed_low, log_sums = attention_part(
        resid_f, weights_back, places, segment
    )
    grad_w_out = contract_rows(mixed_low, grad_branch)
    grad_mixed = (
        contract_cols(grad_branch, weights_back[1]).astype(jnp.bfloat16).reshape(row_count, H, HD)
    )
    grad_query, grad_keys, grad_values = attend_backward(
        query_heads, key_heads, value_heads, grad_mixed, log_sums, places, segment
    )
    grad_qkv = jnp.concatenate(
        [
            grad_query.reshape(row_count, D),
            grad_keys.reshape(row_count, D),
            grad_values.reshape(row_count, D),
        ],
        axis=1,
    ).astype(jnp.bfloat16)
    grad_w_qkv = contract_rows(normed, grad_qkv)
    column_sums = jnp.sum(grad_qkv.astype(jnp.float32), axis=0)
    grad_b_qv = jnp.concatenate([column_sums[:D], column_sums[2 * D :]])
    grad_normed = contract_cols(grad_qkv, weights_back[0])
    first_value, first_pull = jax.vjp(compressed_norm, resid_f, weights_back[6].astype(jnp.float32))
    grad_resid_norm, grad_g_attn = first_pull(grad_normed)
    grad_resid = (grad_middle + grad_resid_norm).astype(jnp.bfloat16)
    every_shard = (
        lax.psum_scatter(grad_w_qkv, ("wide", "narrow"), scatter_dimension=0, tiled=True),
        lax.psum_scatter(grad_w_out, ("wide", "narrow"), scatter_dimension=0, tiled=True),
        lax.psum_scatter(grad_b_qv, ("wide", "narrow"), scatter_dimension=0, tiled=True),
        lax.psum_scatter(grad_g_attn, ("wide", "narrow"), scatter_dimension=0, tiled=True),
        lax.psum_scatter(grad_w_up, ("wide", "narrow"), scatter_dimension=0, tiled=True),
        lax.psum_scatter(grad_w_down, ("wide", "narrow"), scatter_dimension=0, tiled=True),
        lax.psum_scatter(grad_b_up, ("wide", "narrow"), scatter_dimension=0, tiled=True),
        lax.psum_scatter(grad_g_mlp, ("wide", "narrow"), scatter_dimension=0, tiled=True),
    )
    attn_shards = every_shard[:4]
    mlp_shards = every_shard[4:]
    bias_sums = lax.psum((grad_b_out, grad_b_down), ("wide", "narrow"))
    return (
        out_resid,
        grad_resid,
        attn_shards[3],
        attn_shards[0],
        attn_shards[2],
        attn_shards[1],
        bias_sums[0],
        mlp_shards[3],
        mlp_shards[0],
        mlp_shards[2],
        mlp_shards[1],
        bias_sums[1],
    )


def solution(mesh):
    by_kernel = mesh.shape["wide"] == 8 and mesh.shape["narrow"] == 4
    return jax.shard_map(
        on_device_by_kernel if by_kernel else on_device,
        mesh=mesh,
        in_specs=(
            P(("wide", "narrow"), None),
            P(("wide", "narrow")),
            P(("wide", "narrow"), None),
            P(("wide", "narrow")),
            P(("wide", "narrow"), None),
            P(),
            P(("wide", "narrow")),
            P(("wide", "narrow"), None),
            P(("wide", "narrow")),
            P(("wide", "narrow"), None),
            P(),
            P(("wide", "narrow"), None),
            P(("wide", "narrow"), None),
        ),
        out_specs=(
            P(("wide", "narrow"), None),
            P(("wide", "narrow"), None),
            P(("wide", "narrow")),
            P(("wide", "narrow"), None),
            P(("wide", "narrow")),
            P(("wide", "narrow"), None),
            P(),
            P(("wide", "narrow")),
            P(("wide", "narrow"), None),
            P(("wide", "narrow")),
            P(("wide", "narrow"), None),
            P(),
        ),
        check_vma=False,
    )
```

```python
from functools import partial

import jax
import jax.numpy as jnp
from jax import lax
from jax.experimental import pallas as pl
from jax.experimental.pallas import tpu as pltpu
from jax.sharding import PartitionSpec as P

D = 768
H = 12
HD = 64
LANES = 128
ROWS = 256
FF_BLOCK = 768
GROUP = 256
GROUPS = D // GROUP
TICKS = 2

norm_eps = 1e-05
masked_score = -1e30
gelu_root = 0.7978845608028654

bf16 = jnp.bfloat16
f32 = jnp.float32

MESH = pl.DeviceIdType.MESH
ZF, ZN, Y, X, CORE = range(5)
CHIP_AXES = 4
BLOCK = 48


NN = (((1,), (0,)), ((), ()))
NT = (((1,), (1,)), ((), ()))
TN = (((0,), (0,)), ((), ()))


def dot(left, right, dims=NN):
    return lax.dot_general(left, right, dims, preferred_element_type=f32)


def column_sum(values):
    return jnp.sum(values, axis=0, keepdims=True)


def aligned(index, multiple):
    return pl.multiple_of(index, multiple)


class Place:
    def __init__(self):
        wide = lax.axis_index("wide")
        narrow = lax.axis_index("narrow")
        self.wide, self.narrow = wide, narrow
        self.bits = (
            lax.div(wide, 4),
            lax.rem(lax.div(wide, 2), 2),
            lax.rem(wide, 2),
            lax.div(narrow, 2),
            lax.rem(narrow, 2),
        )
        self.core = self.bits[CORE]

    def other(self, axis):
        flip = 1 - 2 * self.bits[axis]
        if axis == X:
            return (self.wide, self.narrow + 2 * flip)
        if axis == CORE:
            return (self.wide, self.narrow + flip)
        return (self.wide + (4, 2, 1)[axis] * flip, self.narrow)

    def region(self, full=(), flipped=()):
        return tuple(
            pl.ds(0, 2)
            if axis in full
            else (1 - self.bits[axis] if axis in flipped else self.bits[axis])
            for axis in range(CHIP_AXES)
        )


def enter(place):
    barrier = pltpu.get_barrier_semaphore()
    for axis in range(5):
        pl.semaphore_signal(
            barrier, inc=1, device_id=place.other(axis), device_id_type=MESH
        )
    pl.semaphore_wait(barrier, 5)


def send(place, axis, src, dst, send_sem, recv_sem):
    return pltpu.make_async_remote_copy(
        src_ref=src,
        dst_ref=dst,
        send_sem=send_sem,
        recv_sem=recv_sem,
        device_id=place.other(axis),
        device_id_type=MESH,
    )


GATHER_COPIES = 15


class GatherChunk:
    def __init__(self, place, order, view, send_sems, recv_sems):
        self.place, self.axes, self.view = place, order + (CORE,), view
        self.send_sems, self.recv_sems = send_sems, recv_sems

    def copy(self, stage, piece, arriving=False):
        axis = self.axes[stage - 1]
        flipped = (self.axes[piece - 1],) if piece else ()
        bit = self.place.core
        if arriving and axis == CORE:
            bit = 1 - bit
        elif arriving:
            flipped += (axis,)
        where = self.view(self.place.region(self.axes[: max(piece - 1, 0)], flipped), bit)
        slot = stage * (stage - 1) // 2 + piece
        return send(
            self.place, axis, where, where, self.send_sems.at[slot], self.recv_sems.at[slot]
        )

    def step(self, stage):
        for piece in range(stage):
            self.copy(stage, piece, arriving=True).wait_recv()
        for later in range(stage + 1, CHIP_AXES + 2):
            self.copy(later, stage).start()

    def drain(self):
        for stage in range(1, CHIP_AXES + 2):
            for piece in range(stage):
                self.copy(stage, piece).wait_send()


class ReduceChunk:
    def __init__(self, place, order, view, lead, landings, send_sems, recv_sems):
        self.place, self.order, self.view, self.lead = place, order, view, lead
        self.landings, self.send_sems, self.recv_sems = landings, send_sems, recv_sems

    def copy(self, stage):
        if stage == 0:
            axis = CORE
            src = self.view(self.place.region(range(CHIP_AXES)), 1 - self.place.core)
        else:
            axis = self.order[stage - 1]
            src = self.view(
                self.place.region(self.order[stage:], (axis,)), self.place.core
            )
        return send(
            self.place, axis, src, self.landings[stage],
            self.send_sems.at[stage], self.recv_sems.at[stage],
        )

    def launch(self, stage):
        self.copy(stage).start()

    def absorb(self, stage):
        self.copy(stage).wait_recv()
        landing = self.landings[stage]
        free = tuple(sorted(self.order[stage:]))

        def add(block, carry):
            index = list(self.place.bits[:CHIP_AXES])
            where = ()
            rest = block
            for axis in reversed(free):
                index[axis] = lax.rem(rest, 2)
                where = (index[axis],) + where
                rest = lax.div(rest, 2)
            here = self.view(tuple(index), self.place.core)
            here[...] = here[...] + landing[self.lead + where]
            return carry

        lax.fori_loop(0, 2 ** len(free), add, 0)
        self.launch(stage + 1)

    def total(self):
        self.copy(CHIP_AXES).wait_recv()
        here = self.view(self.place.region(), self.place.core)
        return here[...].astype(f32) + self.landings[CHIP_AXES][...].astype(f32)

    def drain(self):
        for stage in range(CHIP_AXES + 1):
            self.copy(stage).wait_send()


def weight_chunks(weights):
    qkv_w, out_w, up_w, down_w = weights
    block = pl.ds(0, BLOCK)

    def qkv_view(group):
        def view(region, bit):
            columns = pl.ds(aligned(group * GROUP + bit * LANES, LANES), LANES)
            return qkv_w.at[(pl.ds(0, 3),) + region + (block, columns)]

        return view

    def half_view(whole, start, count):
        half = whole.shape[-1] // 2

        def view(region, bit):
            return whole.at[region + (block, pl.ds(aligned(bit * half + start, LANES), count))]

        return view

    def down_view(start, count):
        def view(region, bit):
            return down_w.at[region + (bit, pl.ds(0, down_w.shape[-2]), pl.ds(start, count))]

        return view

    half = up_w.shape[-1] // 4
    third = down_w.shape[-1] // 2
    return [
        (qkv_view(0), (3,), (BLOCK, LANES)),
        (qkv_view(1), (3,), (BLOCK, LANES)),
        (qkv_view(2), (3,), (BLOCK, LANES)),
        (half_view(out_w, 0, out_w.shape[-1] // 2), (), (BLOCK, out_w.shape[-1] // 2)),
        (half_view(up_w, 0, half), (), (BLOCK, half)),
        (half_view(up_w, half, half), (), (BLOCK, half)),
        (down_view(0, third), (), (down_w.shape[-2], third)),
        (down_view(third, third), (), (down_w.shape[-2], third)),
    ]


CHUNKS = 8
Q0, Q1, Q2, OUT, UP_A, UP_B, DOWN_A, DOWN_B = range(CHUNKS)

GATHER_ORDERS = {
    Q0: (ZF, ZN, Y, X),
    Q1: (ZF, ZN, X, Y),
    Q2: (Y, X, ZF, ZN),
    OUT: (X, Y, ZF, ZN),
    UP_A: (ZF, ZN, Y, X),
    UP_B: (ZF, ZN, X, Y),
    DOWN_A: (ZF, ZN, Y, X),
    DOWN_B: (ZF, ZN, X, Y),
}
REDUCE_ORDERS = {
    Q0: (X, Y, ZN, ZF),
    Q1: (Y, X, ZN, ZF),
    Q2: (X, Y, ZN, ZF),
    OUT: (Y, X, ZN, ZF),
    UP_A: (X, Y, ZN, ZF),
    UP_B: (Y, X, ZN, ZF),
    DOWN_A: (X, Y, ZN, ZF),
    DOWN_B: (Y, X, ZN, ZF),
}

GATHER_STEPS = {
    "FIRST": [(Q0, 0), (Q1, 0), (Q2, 0), (Q0, 1), (Q2, 1), (Q1, 1), (UP_A, 0), (UP_B, 0), (Q2, 2), (Q0, 2), (OUT, 0), (Q1, 2), (Q0, 3), (UP_A, 1), (OUT, 1), (Q1, 3), (UP_B, 1), (OUT, 2), (Q0, 4), (Q2, 3), (Q0, 5)],
    "FORWARD": [[(Q1, 4), (UP_A, 2), (DOWN_A, 0), (DOWN_B, 0)], [(Q1, 5), (UP_B, 2)], [], [(OUT, 3), (UP_A, 3)], [(Q2, 4)], [], [(Q2, 5), (UP_B, 3), (DOWN_A, 1)], [], [(DOWN_B, 1)], [(OUT, 4), (UP_A, 4)], [(UP_B, 4), (DOWN_A, 2)], [(OUT, 5), (UP_A, 5), (DOWN_B, 2)]],
    "NORMED": [],
    "UP": [(UP_B, 5)],
    "FEED": [[], [(DOWN_A, 3)], [(DOWN_B, 3)], [], [], [], [], [], [], [], [(DOWN_A, 4)], [(DOWN_B, 4)]],
    "GRAD_DOWN": [[], [(DOWN_A, 5), (DOWN_B, 5)], [], []],
    "BACK": [],
}

REDUCE_STEPS = {
    "STARTED": [(DOWN_A, 0)],
    "BACK": [[(DOWN_B, 0)], [], [], []],
    "GRAD_UP": [[(DOWN_A, 1)], [], [], [(DOWN_B, 1)]],
    "PREPARED": [(UP_A, 0), (UP_B, 0), (OUT, 0), (DOWN_A, 2)],
    "BACKWARD": [[], [(DOWN_B, 2)], [(DOWN_A, 3)], [], [(DOWN_B, 3)], [(Q0, 0)], [(UP_B, 1)], [(UP_A, 1)], [], [(Q0, 1), (Q1, 0), (OUT, 1)], [], []],
    "FINISHED": [[], [], [(UP_A, 2), (UP_B, 2)]],
    "RESID": [[(Q2, 0)], [(Q0, 2), (OUT, 2)], [(UP_A, 3), (Q1, 1)], [(UP_B, 3)]],
    "OUT": [[(Q0, 3), (Q2, 1)], [(OUT, 3)], [(Q1, 2)], [(Q2, 2)]],
    "REST": [(Q1, 3), (Q2, 3)],
}


class SmallSum:
    def __init__(self, place, values, landing, send_sems, recv_sems):
        self.place, self.values, self.landing = place, values, landing
        self.send_sems, self.recv_sems = send_sems, recv_sems

    def copy(self, axis):
        return send(
            self.place, axis, self.values.at[axis], self.landing.at[axis],
            self.send_sems.at[axis], self.recv_sems.at[axis],
        )

    def step(self, axis):
        self.copy(axis).wait()
        self.values[axis + 1] = self.values[axis] + self.landing[axis]
        if axis < CORE:
            self.copy(axis + 1).start()


def complete(values):
    lane = lax.broadcasted_iota(jnp.int32, values.shape, 1)
    total = jnp.sum(values, axis=1, keepdims=True)
    return jnp.where(lane == values.shape[1] - 1, -total, values)


def widen(values):
    return jnp.concatenate([values, jnp.zeros((values.shape[0], 1), values.dtype)], axis=1)


def spread(shards, device):
    count = shards.shape[1]
    unit = count // 8
    lane = lax.broadcasted_iota(jnp.int32, (1, count), 1)
    flat = lane + device * unit
    flat = jnp.where(lane >= unit, flat - unit + D, flat)
    flat = jnp.where(lane >= 2 * unit, lane - 2 * unit + 2 * D + device * 2 * unit, flat)
    flat = jnp.where(lane >= 4 * unit, lane - 4 * unit + 4 * D + device * 4 * unit, flat)
    row = lax.broadcasted_iota(jnp.int32, (8, count), 0)
    inside = flat - row * D
    mine = jnp.where((inside >= 0) & (inside < D), shards, 0.0)
    for _ in range(7):
        flat = jnp.where(flat >= D, flat - D, flat)
    column = lax.broadcasted_iota(jnp.int32, (D, count), 0)
    place = jnp.where(column == flat, 1.0, 0.0)
    return dot(mine.astype(bf16), place.astype(bf16), NT)


def inverse_size(full):
    return lax.rsqrt(jnp.mean(full * full, axis=1, keepdims=True) + norm_eps)


def norm_backward(grad, full, inverse, gain):
    scaled = grad * gain
    inner = jnp.sum(scaled * full, axis=1, keepdims=True)
    grad_full = scaled * inverse - full * (inverse * inverse * inverse * (inner * (1.0 / D)))
    return grad * full * inverse, grad_full - grad_full[:, D - 1 : D]


def gelu_and_slope(value):
    square = value * value
    bend = square * (gelu_root * 0.044715) + gelu_root
    half = 0.5 * jnp.tanh(value * bend) + 0.5
    act = value * half
    return act, half + act * (1.0 - half) * (6.0 * bend - 4.0 * gelu_root)


def norm_rows(rows, resid, gain, normed):
    full = complete(widen(resid[rows, :].astype(f32)))
    normed[rows, :] = (full * inverse_size(full) * gain).astype(bf16)


def project(group, normed, qkv_w, small, qkv):
    columns = pl.ds(aligned(group * GROUP, GROUP), GROUP)

    def body(part, carry):
        weight = qkv_w[part, :, :, :, :, :, columns].reshape(D, GROUP)
        bias = jnp.where(part == 1, 0.0, small[pl.ds(2 + lax.div(part, 2), 1), columns])
        qkv[:, pl.ds(aligned(part * D + group * GROUP, GROUP), GROUP)] = (
            dot(normed[...], weight) + bias
        ).astype(bf16)
        return carry

    lax.fori_loop(0, 3, body, 0)


def pair_columns(pair):
    return tuple(pl.ds(aligned(part * D + pair * LANES, LANES), LANES) for part in range(3))


def pair_forward(pair, block, cross, qkv, mixed, mixed_rest, lse):
    count = qkv.shape[0]
    lane = lax.broadcasted_iota(jnp.int32, (ROWS, LANES), 1)
    row = lax.broadcasted_iota(jnp.int32, (ROWS, ROWS), 0)
    column = lax.broadcasted_iota(jnp.int32, (ROWS, ROWS), 1)
    rows = pl.ds(block * ROWS, ROWS)
    last = (block + 1) * ROWS
    query_columns, key_columns, value_columns = pair_columns(pair)
    query = qkv[rows, query_columns] * jnp.asarray(HD**-0.5, bf16)
    key = qkv[pl.ds(0, last), key_columns]
    value = qkv[pl.ds(0, last), value_columns]
    value = jnp.concatenate([value, jnp.ones((last, LANES), bf16)], axis=1)
    outs = []
    stats = lse[rows, :]
    for head in range(2):
        mine = lane < HD if head == 0 else lane >= HD
        scores = dot(jnp.where(mine, query, jnp.zeros_like(query)), key, NT)
        parts = []
        for other in range(block + 1):
            part = scores[:, other * ROWS : (other + 1) * ROWS]
            if other == block:
                part = jnp.where(row >= column, part, masked_score)
            elif block * ROWS >= count // 2 and other * ROWS < count // 2:
                part = part + cross
            parts.append(part)
        scores = jnp.concatenate(parts, axis=1) if block else parts[0]
        largest = jnp.max(scores, axis=1, keepdims=True)
        summed = dot(jnp.exp(scores - largest).astype(bf16), value)
        outs.append(summed[:, :LANES] / summed[:, LANES:])
        stats = jnp.where(lane == 2 * pair + head, largest + jnp.log(summed[:, LANES:]), stats)
    lse[rows, :] = stats
    out = jnp.where(lane < HD, outs[0], outs[1])
    low = out.astype(bf16)
    mixed[rows, query_columns] = low
    mixed_rest[rows, query_columns] = (out - low.astype(f32)).astype(bf16)


def middle_rows(rows, resid, mixed, out_w, biases):
    branch = dot(mixed[rows, :], out_w[...].reshape(D, D))
    return widen(resid[rows, :].astype(f32)) + branch + biases[pl.ds(0, 1), :]


def feed_normed_rows(rows, resid, mixed, small, biases, out_w, normed, normed_t):
    full = complete(middle_rows(rows, resid, mixed, out_w, biases))
    values = (full * inverse_size(full) * small[pl.ds(1, 1), :]).astype(bf16)
    normed[rows, :] = values
    normed_t[:, rows] = jnp.transpose(values)


def feed_forward_columns(part, normed, small, up_w, activated, slopes):
    columns = pl.ds(aligned(part * GROUP, GROUP), GROUP)
    up = up_w[:, :, :, :, :, columns].reshape(D, GROUP)
    bias = small[pl.ds(4 + lax.div(part, GROUPS), 1), pl.ds(aligned(lax.rem(part, GROUPS) * GROUP, GROUP), GROUP)]
    act, slope = gelu_and_slope(dot(normed[...], up) + bias)
    activated[:, columns] = act.astype(bf16)
    slopes[:, columns] = slope.astype(bf16)


def feed_backward_rows(
    rows, starting, resid, cotangent, mixed, small, biases, weights, grad_pre, branch, grad_mixed, grad_normed, sums
):
    _, out_w, up_w, down_w = weights
    low_cot = cotangent[rows, :]
    grad_normed[...] = jnp.zeros(grad_normed.shape, f32)

    def body(part, carry):
        columns = pl.ds(aligned(part * FF_BLOCK, FF_BLOCK), FF_BLOCK)
        up = up_w[:, :, :, :, :, columns].reshape(D, FF_BLOCK)
        down = down_w[lax.div(part, 2), lax.rem(part, 2)].reshape(FF_BLOCK, D)
        grad = (dot(low_cot, down, NT) * grad_pre[rows, columns].astype(f32)).astype(bf16)
        grad_pre[rows, columns] = grad
        grad_normed[...] = grad_normed[...] + dot(grad, up, NT)
        total = column_sum(grad.astype(f32))
        here = pl.ds(4 + part, 1)
        sums[here, :] = jnp.where(starting, total, sums[here, :] + total)
        return carry

    lax.fori_loop(0, up_w.shape[-1] // FF_BLOCK, body, 0)
    full = complete(middle_rows(rows, resid, mixed, out_w, biases))
    gain_terms, grad_input = norm_backward(
        grad_normed[...], full, inverse_size(full), small[pl.ds(1, 1), :]
    )
    cot = low_cot.astype(f32)
    rounded = (cot + grad_input).astype(bf16)
    branch[rows, :] = rounded
    grad_mixed[rows, :] = dot(rounded, out_w[...].reshape(D, D), NT).astype(bf16)
    for where, terms in ((1, gain_terms), (8, rounded.astype(f32)), (9, cot)):
        total = column_sum(terms)
        here = pl.ds(where, 1)
        sums[here, :] = jnp.where(starting, total, sums[here, :] + total)


def feed_out_rows(rows, resid, mixed, biases, out_w, down_w, activated, total):
    total[...] = middle_rows(rows, resid, mixed, out_w, biases) + biases[pl.ds(1, 1), :]

    def body(part, carry):
        columns = pl.ds(aligned(part * FF_BLOCK, FF_BLOCK), FF_BLOCK)
        down = down_w[lax.div(part, 2), lax.rem(part, 2)].reshape(FF_BLOCK, D)
        total[...] = total[...] + dot(activated[rows, columns], down)
        return carry

    lax.fori_loop(0, down_w.shape[0] * down_w.shape[1], body, 0)
    return total[...].astype(bf16)


def pair_backward(pair, block, cross, qkv, grad_mixed, lse_t, delta_t, grad_query):
    count = qkv.shape[0]
    lane = lax.broadcasted_iota(jnp.int32, (ROWS, LANES), 1)
    row = lax.broadcasted_iota(jnp.int32, (ROWS, ROWS), 0)
    column = lax.broadcasted_iota(jnp.int32, (ROWS, ROWS), 1)
    keys = pl.ds(block * ROWS, ROWS)
    queries = pl.ds(block * ROWS, count - block * ROWS)
    query_columns, key_columns, value_columns = pair_columns(pair)
    key = qkv[keys, key_columns] * jnp.asarray(HD**-0.5, bf16)
    value = qkv[keys, value_columns]
    query = qkv[queries, query_columns]
    grad = grad_mixed[queries, query_columns]
    grad_values = []
    grad_keys = []
    grad_queries = None
    for head in range(2):
        mine = lane < HD if head == 0 else lane >= HD
        my_key = jnp.where(mine, key, jnp.zeros_like(key))
        my_value = jnp.where(mine, value, jnp.zeros_like(value))
        scores = dot(my_key, query, NT)
        grad_probs = dot(my_value, grad, NT)
        log_row = lse_t[pl.ds(2 * pair + head, 1), queries]
        dot_row = delta_t[pl.ds(2 * pair + head, 1), queries]
        probs = []
        grad_scores = []
        for other in range(count // ROWS - block):
            span = slice(other * ROWS, (other + 1) * ROWS)
            shifted = scores[:, span] - log_row[:, span]
            if other == 0:
                shifted = jnp.where(column >= row, shifted, masked_score)
            elif block * ROWS < count // 2 and (block + other) * ROWS >= count // 2:
                shifted = shifted + cross
            prob = jnp.exp(shifted)
            probs.append(prob.astype(bf16))
            grad_scores.append((prob * (grad_probs[:, span] - dot_row[:, span])).astype(bf16))
        probs = jnp.concatenate(probs, axis=1) if len(probs) > 1 else probs[0]
        grad_scores = jnp.concatenate(grad_scores, axis=1) if len(grad_scores) > 1 else grad_scores[0]
        grad_values.append(dot(probs, grad))
        grad_keys.append(dot(grad_scores, query))
        part = dot(my_key, grad_scores, TN)
        grad_queries = part if grad_queries is None else grad_queries + part
    qkv[keys, value_columns] = jnp.where(lane < HD, grad_values[0], grad_values[1]).astype(bf16)
    qkv[keys, key_columns] = (
        jnp.where(lane < HD, grad_keys[0], grad_keys[1]) * HD**-0.5
    ).astype(bf16)
    if block == 0:
        grad_query[...] = grad_queries
    else:
        grad_query[:, queries] = grad_query[:, queries] + grad_queries


def backward_rows(mixed, mixed_rest, grad_mixed, lse, lse_t, delta_t):
    heads = lse_t.shape[0]
    lse_t[...] = jnp.transpose(lse[...])[:heads]
    head = lax.broadcasted_iota(jnp.int32, (heads, D), 0)
    column = lax.broadcasted_iota(jnp.int32, (heads, D), 1)
    pick = jnp.where((column >= head * HD) & (column < head * HD + HD), 1.0, 0.0).astype(f32)

    def body(block, carry):
        rows = pl.ds(aligned(block * ROWS, ROWS), ROWS)
        whole = mixed[rows, :].astype(f32) + mixed_rest[rows, :].astype(f32)
        product = whole * grad_mixed[rows, :].astype(f32)
        delta_t[:, rows] = lax.dot_general(
            pick, product, NT, precision=lax.Precision.HIGHEST, preferred_element_type=f32
        )
        return carry

    lax.fori_loop(0, mixed.shape[0] // ROWS, body, 0)


def layer_kernel(
    resid, cotangent, qkv_in, out_in, up_in, down_in, small_in, biases_in, lengths,
    out_resid, grad_resid, qkv_out, out_out, up_out, down_out, small_out, qkv_away, rest_away, activated_away,
    *scratch,
):
    scratch = list(scratch)
    take = lambda n: [scratch.pop(0) for _ in range(n)]
    weights = take(4)
    qkv_w, out_w, up_w, down_w = weights
    landings = [take(CHIP_AXES + 1) for _ in range(CHUNKS)]
    normed, qkv, mixed, mixed_rest, grad_mixed, lse, staging, down_g, out_g = take(9)
    branch = mixed_rest
    my_rows, pair_rows, biases, small_values, small_landing, sum_values, sum_landing = take(7)
    (
        pair_send, pair_recv, small_send, small_recv, sum_send, sum_recv,
        gather_send, gather_recv, reduce_send, reduce_recv,
        final_send, final_recv, final_own, row_sems, block_sems,
    ) = take(15)
    activated = qkv
    qkv = activated.at[:, pl.ds(0, 3 * D)]
    count = resid.shape[0]
    place = Place()
    core = place.core
    cross = jnp.where(lengths[0, 0] == count, 0.0, masked_score)
    enter(place)

    shards = (qkv_in, out_in, up_in)
    shard_rows = BLOCK // 2
    offsets = ((0, 0), (0, qkv_in.shape[1]), (shard_rows, 0))
    for shard, (top, left) in zip(shards, offsets):
        values = shard[...].astype(f32)
        values = widen(values) if values.shape[1] == D - 1 else values
        my_rows[pl.ds(top, shard_rows), pl.ds(left, values.shape[1])] = values
    pair_copy = send(place, CORE, my_rows, pair_rows, pair_send.at[0], pair_recv.at[0])
    pair_copy.start()
    small_values[0] = spread(small_in[...], place.wide * 4 + place.narrow)
    small_sum = SmallSum(place, small_values, small_landing, small_send, small_recv)
    small_sum.copy(0).start()
    biases[...] = widen(biases_in[...])

    def own_block(slot, first, width):
        top, left = offsets[slot]
        here = (pl.ds(top, shard_rows), pl.ds(aligned(left + first, LANES), width))
        mine, theirs = my_rows[here], pair_rows[here]
        return jnp.concatenate(
            [jnp.where(core == 0, mine, theirs), jnp.where(core == 0, theirs, mine)], axis=0
        ).astype(bf16)

    here = place.region()
    gathers = [
        GatherChunk(place, GATHER_ORDERS[index], view, gather_send.at[index], gather_recv.at[index])
        for index, (view, _, _) in enumerate(weight_chunks(weights))
    ]
    down_w[here + (core,)] = widen(down_in[...].astype(f32)).astype(bf16)
    pair_copy.wait()
    for group in range(GROUPS):
        for part in range(3):
            first = group * GROUP + core * LANES
            qkv_w[(part,) + here + (slice(None), pl.ds(aligned(first, LANES), LANES))] = own_block(
                0, part * D + first, LANES
            )
    opening = list(GATHER_STEPS["FIRST"])
    while opening[0] in ((Q0, 0), (Q1, 0), (Q2, 0)):
        gathers[opening.pop(0)[0]].step(0)
    for slot, whole in ((1, out_w), (2, up_w)):
        half = whole.shape[-1] // 2
        first = aligned(core * half, LANES)
        whole[here + (slice(None), pl.ds(first, half))] = own_block(slot, first, half)

    lse[...] = jnp.zeros_like(lse)

    def norm_all():
        def body(block, carry):
            norm_rows(
                pl.ds(aligned(block * ROWS, ROWS), ROWS), resid, small_values[5][0:1], normed
            )
            return carry

        lax.fori_loop(0, count // ROWS, body, 0)

    axis = 0
    for number, (chunk, stage) in enumerate(opening):
        if (chunk, stage) == (Q0, 5):
            norm_all()
        gathers[chunk].step(stage)
        while axis <= CORE and (axis + 1) * (opening.index((Q0, 4)) + 1) <= (number + 1) * 5:
            small_sum.step(axis)
            axis += 1

    small = small_values.at[5]
    save = pltpu.make_async_copy(qkv, qkv_away, row_sems.at[4])
    blocks = count // ROWS
    pairs = H // 2
    per_group = pairs // GROUPS
    ticks = GATHER_STEPS["FORWARD"]
    after_up = GATHER_STEPS["FEED"]

    def gather_steps(where):
        for chunk, stage in GATHER_STEPS[where]:
            gathers[chunk].step(stage)

    def after(number, index, steps_of, run):
        for which in range(number):
            steps = steps_of(which)
            if steps:
                @pl.when(index == which)
                def _():
                    for chunk, stage in steps:
                        run(chunk, stage)

    def forward(pair, carry):
        @pl.when(lax.rem(pair, per_group) == 0)
        def _():
            project(lax.div(pair, per_group), normed, qkv_w, small, qkv)

        @pl.when(pair == pairs - per_group)
        def _():
            save.start()

        for block in range(blocks):
            pair_forward(pair, block, cross, qkv, mixed, mixed_rest, lse)
            if (block + 1) * TICKS % blocks == 0:
                turn = (block + 1) * TICKS // blocks - 1
                after(
                    pairs, pair, lambda which: ticks[which * TICKS + turn],
                    lambda chunk, stage: gathers[chunk].step(stage),
                )
        return carry

    lax.fori_loop(0, pairs, forward, 0)
    save.wait()
    pltpu.make_async_copy(mixed_rest, rest_away, row_sems.at[3]).start()

    sums = sum_values.at[0]
    sums[...] = jnp.zeros(sums.shape, f32)
    def reduce_chunks(qkv_g):
        return [
            ReduceChunk(
                place, REDUCE_ORDERS[index], view, (slice(None),) * len(lead),
                landings[index], reduce_send.at[index], reduce_recv.at[index],
            )
            for index, (view, lead, _) in enumerate(weight_chunks((qkv_g, out_g, up_w, down_g)))
        ]

    reduces = reduce_chunks(qkv_w)

    def emit_rows(target, block, sem, values):
        rows = pl.ds(aligned(block * ROWS, ROWS), ROWS)

        @pl.when(block > 0)
        def _():
            pltpu.make_async_copy(staging, target.at[rows, :], sem).wait()

        staging[...] = values[:, : D - 1]
        pltpu.make_async_copy(staging, target.at[rows, :], sem).start()

    def emit_last(target, sem):
        pltpu.make_async_copy(staging, target.at[pl.ds(0, ROWS), :], sem).wait()

    def reduce_steps(where):
        for chunk, stage in REDUCE_STEPS[where]:
            reduces[chunk].absorb(stage)

    def absorb(chunk, stage):
        reduces[chunk].absorb(stage)

    def feed_forward(grad_pre, normed_t, grad_total):
        def normed_body(block, carry):
            rows = pl.ds(aligned(block * ROWS, ROWS), ROWS)
            feed_normed_rows(rows, resid, mixed, small, biases, out_w, grad_mixed, normed_t)
            return carry

        gather_steps("NORMED")
        lax.fori_loop(0, blocks, normed_body, 0)
        gather_steps("UP")

        def there(part, carry):
            feed_forward_columns(part, grad_mixed, small, up_w, activated, grad_pre)
            after(
                len(after_up), part, lambda which: after_up[which],
                lambda chunk, stage: gathers[chunk].step(stage),
            )
            return carry

        lax.fori_loop(0, len(after_up), there, 0)

        def grad_down(part, carry):
            columns = pl.ds(aligned(part * FF_BLOCK, FF_BLOCK), FF_BLOCK)
            down_g[lax.div(part, 2), lax.rem(part, 2)] = (
                dot(activated[:, columns], cotangent[...], TN)
                .astype(bf16)
                .reshape(down_g.shape[2:])
            )
            after(
                4, part, lambda which: GATHER_STEPS["GRAD_DOWN"][which],
                lambda chunk, stage: gathers[chunk].step(stage),
            )
            return carry

        lax.fori_loop(0, up_w.shape[-1] // FF_BLOCK, grad_down, 0)
        reduces[DOWN_A].launch(0)
        reduces[DOWN_B].launch(0)
        keep = pltpu.make_async_copy(qkv, activated_away, row_sems.at[0])
        keep.start()
        gather_steps("BACK")
        for chunk in gathers:
            chunk.drain()
        reduce_steps("STARTED")
        pltpu.make_async_copy(mixed_rest, rest_away, row_sems.at[3]).wait()
        keep.wait()
        pltpu.make_async_copy(qkv_away, qkv, row_sems.at[4]).start()

        def back(block, carry):
            rows = pl.ds(aligned(block * ROWS, ROWS), ROWS)
            feed_backward_rows(
                rows, block == 0, resid, cotangent, mixed, small, biases, weights,
                grad_pre, branch, grad_mixed, grad_total, sums,
            )
            after(
                blocks, block, lambda which: REDUCE_STEPS["BACK"][which],
                lambda chunk, stage: reduces[chunk].absorb(stage),
            )
            return carry

        lax.fori_loop(0, blocks, back, 0)

        def grad_up(part, carry):
            columns = pl.ds(aligned(part * FF_BLOCK, FF_BLOCK), FF_BLOCK)
            up_w[:, :, :, :, :, columns] = (
                dot(normed_t[...], grad_pre[:, columns])
                .astype(bf16)
                .reshape((2,) * CHIP_AXES + (BLOCK, FF_BLOCK))
            )
            after(
                len(REDUCE_STEPS["GRAD_UP"]), part, lambda which: REDUCE_STEPS["GRAD_UP"][which],
                lambda chunk, stage: reduces[chunk].absorb(stage),
            )
            return carry

        lax.fori_loop(0, up_w.shape[-1] // FF_BLOCK, grad_up, 0)
        reduces[UP_A].launch(0)
        reduces[UP_B].launch(0)

        def grad_out(half, carry):
            columns = pl.ds(aligned(half * (D // 2), LANES), D // 2)
            out_g[half] = (
                dot(mixed[:, columns], branch[...], TN).astype(bf16).reshape(out_g.shape[1:])
            )
            return carry

        lax.fori_loop(0, 2, grad_out, 0)
        reduces[OUT].launch(0)

    pl.run_scoped(
        feed_forward,
        pltpu.VMEM((count, up_w.shape[-1]), bf16),
        pltpu.VMEM((D, count), bf16),
        pltpu.VMEM((ROWS, D), f32),
    )
    pltpu.make_async_copy(qkv_away, qkv, row_sems.at[4]).wait()

    def attention_backward(qkv_g, row_total, lse_t, delta_t, grad_query, normed_t):
        reduces[:] = reduce_chunks(qkv_g)

        def turn(block, carry):
            rows = pl.ds(aligned(block * ROWS, ROWS), ROWS)
            normed_t[:, rows] = jnp.transpose(normed[rows, :])
            pltpu.make_async_copy(
                rest_away.at[rows, :], normed.at[rows, :], block_sems.at[block]
            ).start()
            return carry

        lax.fori_loop(0, blocks, turn, 0)
        for block in range(blocks):
            rows = pl.ds(block * ROWS, ROWS)
            pltpu.make_async_copy(
                rest_away.at[rows, :], normed.at[rows, :], block_sems.at[block]
            ).wait()
        backward_rows(mixed, normed, grad_mixed, lse, lse_t, delta_t)
        reduce_steps("PREPARED")
        ticks = REDUCE_STEPS["BACKWARD"]

        def finish_group(group):
            columns = pl.ds(aligned(group * GROUP, GROUP), GROUP)

            def grad_columns(part):
                return pl.ds(aligned(part * D + group * GROUP, GROUP), GROUP)

            def of_weight(part, carry):
                grads = qkv[:, grad_columns(part)]
                qkv_g[part, :, :, :, :, :, columns] = (
                    dot(normed_t[...], grads)
                    .astype(bf16)
                    .reshape((2,) * CHIP_AXES + (BLOCK, GROUP))
                )
                here = jnp.where(part == 1, 10, 2 + lax.div(part, 2))
                sums[pl.ds(here, 1), columns] = column_sum(grads.astype(f32))
                return carry

            lax.fori_loop(0, 3, of_weight, 0)

        def backward(pair, carry):
            for block in range(blocks):
                pair_backward(pair, block, cross, qkv, grad_mixed, lse_t, delta_t, grad_query)
                if (block + 1) * TICKS % blocks == 0:
                    turn = (block + 1) * TICKS // blocks - 1
                    after(
                        pairs, pair, lambda which: ticks[which * TICKS + turn],
                        lambda chunk, stage: reduces[chunk].absorb(stage),
                    )
            qkv[:, pair_columns(pair)[0]] = jnp.transpose(grad_query[...]).astype(bf16)

            @pl.when(lax.rem(pair, per_group) == per_group - 1)
            def _():
                finish_group(lax.div(pair, per_group))

            def finished(chunk, stage):
                if stage is None:
                    reduces[chunk].launch(0)
                else:
                    reduces[chunk].absorb(stage)

            def steps_of(which):
                if which % per_group < per_group - 1:
                    return []
                group = which // per_group
                return [(group, None)] + REDUCE_STEPS["FINISHED"][group]

            after(pairs, pair, steps_of, finished)
            return carry

        lax.fori_loop(0, pairs, backward, 0)

        def reload(block):
            rows = pl.ds(aligned(block * ROWS, ROWS), ROWS)
            return pltpu.make_async_copy(
                activated_away.at[rows, :], qkv.at[rows, :], block_sems.at[block]
            )

        def resid_rows(block, carry):
            rows = pl.ds(aligned(block * ROWS, ROWS), ROWS)
            row_total[...] = jnp.zeros(row_total.shape, f32)

            def add(part, carry):
                grads = qkv[rows, pl.ds(aligned(part * D, D), D)]
                row_total[...] = row_total[...] + dot(grads, qkv_w[part].reshape(D, D), NT)
                return carry

            lax.fori_loop(0, 3, add, 0)
            full = complete(widen(resid[rows, :].astype(f32)))
            gain_terms, grad_input = norm_backward(
                row_total[...], full, inverse_size(full), small[pl.ds(0, 1), :]
            )
            emit_rows(
                grad_resid, block, row_sems.at[2],
                (branch[rows, :].astype(f32) + grad_input).astype(bf16),
            )
            total = column_sum(gain_terms)
            sums[pl.ds(0, 1), :] = jnp.where(block == 0, total, sums[pl.ds(0, 1), :] + total)
            reload(block).start()
            after(blocks, block, lambda which: REDUCE_STEPS["RESID"][which], absorb)
            return carry

        lax.fori_loop(0, blocks, resid_rows, 0)
        sum_all = SmallSum(place, sum_values, sum_landing, sum_send, sum_recv)
        sum_all.copy(0).start()
        emit_last(grad_resid, row_sems.at[2])

        def out_rows(block, carry):
            rows = pl.ds(aligned(block * ROWS, ROWS), ROWS)
            reload(block).wait()
            values = feed_out_rows(rows, resid, mixed, biases, out_w, down_w, activated, row_total)
            emit_rows(out_resid, block, row_sems.at[1], values)
            after(blocks, block, lambda which: REDUCE_STEPS["OUT"][which], absorb)
            for which in range(blocks):
                @pl.when(block == which)
                def _():
                    sum_all.step(which)

            return carry

        lax.fori_loop(0, blocks, out_rows, 0)
        for axis in range(blocks, CORE + 1):
            sum_all.step(axis)
        small_out[...] = sum_values[5]

        for chunk, start in ((DOWN_A, 0), (DOWN_B, D // 2)):
            down_out[:, pl.ds(start, D // 2)] = reduces[chunk].total()
        their_rows = pl.ds(aligned((1 - core) * shard_rows, 8), shard_rows)
        kept_rows = pl.ds(aligned(core * shard_rows, 8), shard_rows)
        copies = []

        def deliver(slot, part_of, target):
            away = send(
                place, CORE, part_of(their_rows), target, final_send.at[slot], final_recv.at[slot]
            )
            away.start()
            home = pltpu.make_async_copy(part_of(kept_rows), target, final_own.at[slot])
            home.start()
            copies.extend((away, home))

        finals = pair_rows
        half = up_w.shape[-1] // 4
        finals[:, pl.ds(0, half)] = reduces[UP_A].total()
        finals[:, pl.ds(half, half)] = reduces[UP_B].total()
        deliver(
            0, lambda rows: finals.at[rows, pl.ds(0, 2 * half)],
            up_out.at[:, pl.ds(aligned(core * 2 * half, LANES), 2 * half)],
        )
        first = 2 * half
        finals[:, pl.ds(first, D // 2)] = reduces[OUT].total()
        deliver(
            1, lambda rows: finals.at[rows, pl.ds(2 * half, D // 2)],
            out_out.at[:, pl.ds(aligned(core * (D // 2), LANES), D // 2)],
        )
        first += D // 2
        late = [chunk for chunk, _ in REDUCE_STEPS["REST"]]
        groups = sorted(range(GROUPS), key=lambda group: group in late)
        for group in groups:
            if group in late:
                reduce_steps("REST")
                late = []
            total = reduces[group].total()
            first = 2 * half + D // 2 + group * 3 * LANES
            for part in range(3):
                here = pl.ds(first, LANES)
                finals[:, here] = total[part]
                deliver(
                    2 + group * 3 + part, lambda rows, here=here: finals.at[rows, here],
                    qkv_out.at[:, pl.ds(aligned(part * D + group * GROUP + core * LANES, LANES), LANES)],
                )
                first += LANES
        for copy in copies:
            copy.wait()
        for chunk in reduces:
            chunk.drain()
        emit_last(out_resid, row_sems.at[1])

    pl.run_scoped(
        attention_backward,
        pltpu.VMEM(qkv_w.shape, bf16),
        pltpu.VMEM((ROWS, D), f32),
        pltpu.VMEM((16, count), f32),
        pltpu.VMEM((16, count), f32),
        pltpu.VMEM((LANES, count), f32),
        pltpu.VMEM((D, count), bf16),
    )


def layer_by_kernel(resid, cotangent, qkv_in, out_in, up_in, down_in, small_in, biases, lengths):
    count = resid.shape[0]
    grid = (2,) * CHIP_AXES
    ff = up_in.shape[1]
    weight_shapes = [
        (3,) + grid + (BLOCK, D),
        grid + (BLOCK, D),
        grid + (BLOCK, ff),
        grid + (2, down_in.shape[0], D),
    ]
    weights = [pltpu.VMEM(shape, bf16) for shape in weight_shapes]
    shapes = [jax.ShapeDtypeStruct(shape, bf16) for shape in weight_shapes]
    landings = [
        pltpu.VMEM(lead + (2,) * (CHIP_AXES - stage) + block, bf16)
        for _, lead, block in weight_chunks(shapes)
        for stage in range(CHIP_AXES + 1)
    ]
    dma = pltpu.SemaphoreType.DMA
    small_rows, sum_rows = 8, 16
    scratch = (
        weights
        + landings
        + [
            pltpu.VMEM((count, D), bf16),
            pltpu.VMEM((count, ff), bf16),
            pltpu.VMEM((count, D), bf16),
            pltpu.VMEM((count, D), bf16),
            pltpu.VMEM((count, D), bf16),
            pltpu.VMEM((count, LANES), f32),
            pltpu.VMEM((ROWS, D - 1), bf16),
            pltpu.VMEM(weight_shapes[3], bf16),
            pltpu.VMEM(weight_shapes[1], bf16),
            pltpu.VMEM((BLOCK, (3 * D + D + ff) // 2), f32),
            pltpu.VMEM((BLOCK, (3 * D + D + ff) // 2), f32),
            pltpu.VMEM((2, D), f32),
            pltpu.VMEM((6, small_rows, D), f32),
            pltpu.VMEM((5, small_rows, D), f32),
            pltpu.VMEM((6, sum_rows, D), f32),
            pltpu.VMEM((5, sum_rows, D), f32),
            dma((3,)),
            dma((3,)),
            dma((5,)),
            dma((5,)),
            dma((5,)),
            dma((5,)),
            dma((CHUNKS, GATHER_COPIES)),
            dma((CHUNKS, GATHER_COPIES)),
            dma((CHUNKS, CHIP_AXES + 1)),
            dma((CHUNKS, CHIP_AXES + 1)),
            dma((11,)),
            dma((11,)),
            dma((11,)),
            dma((5,)),
            dma((count // ROWS,)),
        ]
    )
    in_vmem = pl.BlockSpec(memory_space=pltpu.VMEM)
    in_hbm = pl.BlockSpec(memory_space=pl.ANY)
    shard_rows = BLOCK // 2
    return pl.pallas_call(
        layer_kernel,
        out_shape=[
            jax.ShapeDtypeStruct((count, D - 1), bf16),
            jax.ShapeDtypeStruct((count, D - 1), bf16),
            jax.ShapeDtypeStruct((shard_rows, 3 * D), f32),
            jax.ShapeDtypeStruct((shard_rows, D), f32),
            jax.ShapeDtypeStruct((shard_rows, ff), f32),
            jax.ShapeDtypeStruct((down_in.shape[0], D), f32),
            jax.ShapeDtypeStruct((sum_rows, D), f32),
            jax.ShapeDtypeStruct((count, 3 * D), bf16),
            jax.ShapeDtypeStruct((count, D), bf16),
            jax.ShapeDtypeStruct((count, 3 * D), bf16),
        ],
        in_specs=[in_vmem] * 8 + [pl.BlockSpec(memory_space=pltpu.SMEM)],
        out_specs=[in_hbm] * 2 + [in_vmem] * 5 + [in_hbm] * 3,
        scratch_shapes=scratch,
        compiler_params=pltpu.CompilerParams(
            collective_id=1, has_side_effects=True, vmem_limit_bytes=VMEM_BYTES
        ),
        name="layer",
    )(resid, cotangent, qkv_in, out_in, up_in, down_in, small_in, biases, lengths)


VMEM_BYTES = 63 * 2**20


def device_index():
    return lax.axis_index("wide") * lax.axis_size("narrow") + lax.axis_index("narrow")


def on_device_by_kernel(
    resid, gain_attn, qkv_weight, qv_bias, out_weight, out_bias, gain_mlp,
    up_weight, up_bias, down_weight, down_bias, cotangent, seq_lengths,
):
    devices = lax.axis_size("wide") * lax.axis_size("narrow")
    width = out_weight.shape[1]
    small = jnp.concatenate([gain_attn, gain_mlp, qv_bias, up_bias]).astype(f32)
    biases = jnp.stack([out_bias, down_bias]).astype(f32)
    out_resid, grad_resid, qkv, out, up, down, sums, _, _, _ = layer_by_kernel(
        resid, jnp.pad(cotangent, ((0, 0), (0, D - width))), qkv_weight, out_weight, up_weight, down_weight,
        small.reshape(1, -1), biases, seq_lengths,
    )
    sums = sums.reshape(-1)

    def shard(first, count):
        part = count // devices
        return lax.dynamic_slice(sums, (first + device_index() * part,), (part,))

    ff = up_weight.shape[1]
    last = 4 * D + ff
    return (
        out_resid,
        grad_resid,
        shard(0, D),
        qkv,
        shard(2 * D, 2 * D),
        out[:, :width],
        sums[last : last + width],
        shard(D, D),
        up,
        shard(4 * D, ff),
        down[:, :width],
        sums[last + D : last + D + width],
    )


def compressed_norm(values, gain_vec):
    row_total = jnp.sum(values, axis=-1, keepdims=True)
    full_vector = jnp.concatenate([values, -row_total], axis=-1)
    mean_sq = jnp.mean(full_vector * full_vector, axis=-1, keepdims=True)
    return full_vector * lax.rsqrt(mean_sq + norm_eps) * gain_vec


def contract_rows(left_side, right_side):
    return lax.dot_general(
        left_side, right_side, (((0,), (0,)), ((), ())), preferred_element_type=jnp.float32
    )


def contract_cols(left_side, right_side):
    return lax.dot_general(
        left_side, right_side, (((1,), (1,)), ((), ())), preferred_element_type=jnp.float32
    )


def segment_ids(lengths, row_count):
    places = jnp.arange(row_count, dtype=jnp.int32)
    seq_ends = jnp.cumsum(lengths)
    segment = jnp.sum((places[:, None] >= seq_ends[None, :]).astype(jnp.int32), axis=1)
    return (places, segment)


def block_scores(query_block, key_heads, places, segment, first_row, last_row):
    scores = jnp.einsum(
        "qhd,khd->hqk", query_block, key_heads[:last_row], preferred_element_type=jnp.float32
    ) * HD ** (-0.5)
    allowed = (segment[first_row:last_row, None] == segment[None, :last_row]) & (
        places[None, :last_row] <= places[first_row:last_row, None]
    )
    return jnp.where(allowed[None], scores, masked_score)


def attend_forward(query_heads, key_heads, value_heads, places, segment):
    row_count = query_heads.shape[0]
    block_rows = min(512, row_count)
    mixed_parts = []
    log_parts = []
    for block_index in range(row_count // block_rows):
        first_row = block_index * block_rows
        last_row = first_row + block_rows
        scores = block_scores(
            query_heads[first_row:last_row], key_heads, places, segment, first_row, last_row
        )
        row_max = jnp.max(scores, axis=-1, keepdims=True)
        exp_scores = jnp.exp(scores - row_max)
        summed = jnp.sum(exp_scores, axis=-1, keepdims=True)
        attn_probs = (exp_scores / summed).astype(jnp.bfloat16)
        mixed_parts.append(
            jnp.einsum(
                "hqk,khd->qhd",
                attn_probs,
                value_heads[:last_row],
                preferred_element_type=jnp.float32,
            )
        )
        log_parts.append(row_max + jnp.log(summed))
    return (jnp.concatenate(mixed_parts, axis=0), jnp.concatenate(log_parts, axis=1))


def attend_backward(query_heads, key_heads, value_heads, grad_mixed, log_sums, places, segment):
    row_count = query_heads.shape[0]
    block_rows = min(512, row_count)
    grad_query_parts = []
    grad_keys = jnp.zeros(key_heads.shape, jnp.float32)
    grad_values = jnp.zeros(value_heads.shape, jnp.float32)
    for block_index in range(row_count // block_rows):
        first_row = block_index * block_rows
        last_row = first_row + block_rows
        query_block = query_heads[first_row:last_row]
        grad_block = grad_mixed[first_row:last_row]
        scores = block_scores(query_block, key_heads, places, segment, first_row, last_row)
        attn_probs = jnp.exp(scores - log_sums[:, first_row:last_row])
        grad_probs = jnp.einsum(
            "qhd,khd->hqk", grad_block, value_heads[:last_row], preferred_element_type=jnp.float32
        )
        row_dot = jnp.sum(attn_probs * grad_probs, axis=-1, keepdims=True)
        grad_scores = (attn_probs * (grad_probs - row_dot)).astype(jnp.bfloat16)
        grad_query_parts.append(
            jnp.einsum(
                "hqk,khd->qhd",
                grad_scores,
                key_heads[:last_row],
                preferred_element_type=jnp.float32,
            )
            * HD ** (-0.5)
        )
        grad_keys = grad_keys.at[:last_row].add(
            jnp.einsum("hqk,qhd->khd", grad_scores, query_block, preferred_element_type=jnp.float32)
            * HD ** (-0.5)
        )
        grad_values = grad_values.at[:last_row].add(
            jnp.einsum(
                "hqk,qhd->khd",
                attn_probs.astype(jnp.bfloat16),
                grad_block,
                preferred_element_type=jnp.float32,
            )
        )
    return (jnp.concatenate(grad_query_parts, axis=0), grad_keys, grad_values)


def attention_part(resid_f, weights, places, segment):
    row_count = resid_f.shape[0]
    normed = compressed_norm(resid_f, weights[6].astype(jnp.float32)).astype(jnp.bfloat16)
    bias_pair = weights[4].astype(jnp.float32)
    bias_row = jnp.concatenate([bias_pair[:D], jnp.zeros((D,), jnp.float32), bias_pair[D:]])
    qkv_low = (jnp.dot(normed, weights[0], preferred_element_type=jnp.float32) + bias_row).astype(
        jnp.bfloat16
    )
    query_heads = qkv_low[:, :D].reshape(row_count, H, HD)
    key_heads = qkv_low[:, D : 2 * D].reshape(row_count, H, HD)
    value_heads = qkv_low[:, 2 * D :].reshape(row_count, H, HD)
    mixed_heads, log_sums = attend_forward(query_heads, key_heads, value_heads, places, segment)
    mixed_low = mixed_heads.reshape(row_count, D).astype(jnp.bfloat16)
    return (normed, query_heads, key_heads, value_heads, mixed_low, log_sums)


def mlp_part(middle, weights):
    normed_mlp = compressed_norm(middle, weights[7].astype(jnp.float32)).astype(jnp.bfloat16)
    pre_act = jnp.dot(normed_mlp, weights[2], preferred_element_type=jnp.float32) + weights[
        5
    ].astype(jnp.float32)
    activated = jax.nn.gelu(pre_act, approximate=True).astype(jnp.bfloat16)
    return (normed_mlp, pre_act, activated)


def on_device(
    resid,
    gain_attn,
    qkv_weight,
    qv_bias,
    out_weight,
    out_bias,
    gain_mlp,
    up_weight,
    up_bias,
    down_weight,
    down_bias,
    cotangent,
    seq_lengths,
):
    shards = (qkv_weight, out_weight, up_weight, down_weight, qv_bias, up_bias, gain_attn, gain_mlp)
    gathered = (
        lax.all_gather(shards[0], ("wide", "narrow"), axis=0, tiled=True),
        lax.all_gather(shards[1], ("wide", "narrow"), axis=0, tiled=True),
        lax.all_gather(shards[2], ("wide", "narrow"), axis=0, tiled=True),
        lax.all_gather(shards[3], ("wide", "narrow"), axis=0, tiled=True),
        lax.all_gather(shards[4], ("wide", "narrow"), axis=0, tiled=True),
        lax.all_gather(shards[5], ("wide", "narrow"), axis=0, tiled=True),
        lax.all_gather(shards[6], ("wide", "narrow"), axis=0, tiled=True),
        lax.all_gather(shards[7], ("wide", "narrow"), axis=0, tiled=True),
    )
    row_count = resid.shape[0]
    places, segment = segment_ids(seq_lengths[0], row_count)
    resid_f = resid.astype(jnp.float32)
    attn_first = attention_part(resid_f, gathered, places, segment)
    middle = (
        resid_f
        + jnp.dot(attn_first[4], gathered[1], preferred_element_type=jnp.float32)
        + out_bias.astype(jnp.float32)
    )
    mlp_first = mlp_part(middle, gathered)
    out_resid = (
        middle
        + jnp.dot(mlp_first[2], gathered[3], preferred_element_type=jnp.float32)
        + down_bias.astype(jnp.float32)
    ).astype(jnp.bfloat16)
    weights_back = gathered
    normed_mlp, pre_act, activated = mlp_part(middle, weights_back)
    grad_out = cotangent.astype(jnp.float32)
    grad_w_down = contract_rows(activated, cotangent)
    grad_b_down = jnp.sum(grad_out, axis=0)
    grad_act = contract_cols(cotangent, weights_back[3])
    gelu_value, gelu_pull = jax.vjp(partial(jax.nn.gelu, approximate=True), pre_act)
    grad_pre = gelu_pull(grad_act)[0].astype(jnp.bfloat16)
    grad_w_up = contract_rows(normed_mlp, grad_pre)
    grad_b_up = jnp.sum(grad_pre.astype(jnp.float32), axis=0)
    grad_normed_mlp = contract_cols(grad_pre, weights_back[2])
    norm_value, norm_pull = jax.vjp(compressed_norm, middle, weights_back[7].astype(jnp.float32))
    grad_middle_norm, grad_g_mlp = norm_pull(grad_normed_mlp)
    grad_middle = grad_out + grad_middle_norm
    grad_branch = grad_middle.astype(jnp.bfloat16)
    grad_b_out = jnp.sum(grad_branch.astype(jnp.float32), axis=0)
    normed, query_heads, key_heads, value_heads, mixed_low, log_sums = attention_part(
        resid_f, weights_back, places, segment
    )
    grad_w_out = contract_rows(mixed_low, grad_branch)
    grad_mixed = (
        contract_cols(grad_branch, weights_back[1]).astype(jnp.bfloat16).reshape(row_count, H, HD)
    )
    grad_query, grad_keys, grad_values = attend_backward(
        query_heads, key_heads, value_heads, grad_mixed, log_sums, places, segment
    )
    grad_qkv = jnp.concatenate(
        [
            grad_query.reshape(row_count, D),
            grad_keys.reshape(row_count, D),
            grad_values.reshape(row_count, D),
        ],
        axis=1,
    ).astype(jnp.bfloat16)
    grad_w_qkv = contract_rows(normed, grad_qkv)
    column_sums = jnp.sum(grad_qkv.astype(jnp.float32), axis=0)
    grad_b_qv = jnp.concatenate([column_sums[:D], column_sums[2 * D :]])
    grad_normed = contract_cols(grad_qkv, weights_back[0])
    first_value, first_pull = jax.vjp(compressed_norm, resid_f, weights_back[6].astype(jnp.float32))
    grad_resid_norm, grad_g_attn = first_pull(grad_normed)
    grad_resid = (grad_middle + grad_resid_norm).astype(jnp.bfloat16)
    every_shard = (
        lax.psum_scatter(grad_w_qkv, ("wide", "narrow"), scatter_dimension=0, tiled=True),
        lax.psum_scatter(grad_w_out, ("wide", "narrow"), scatter_dimension=0, tiled=True),
        lax.psum_scatter(grad_b_qv, ("wide", "narrow"), scatter_dimension=0, tiled=True),
        lax.psum_scatter(grad_g_attn, ("wide", "narrow"), scatter_dimension=0, tiled=True),
        lax.psum_scatter(grad_w_up, ("wide", "narrow"), scatter_dimension=0, tiled=True),
        lax.psum_scatter(grad_w_down, ("wide", "narrow"), scatter_dimension=0, tiled=True),
        lax.psum_scatter(grad_b_up, ("wide", "narrow"), scatter_dimension=0, tiled=True),
        lax.psum_scatter(grad_g_mlp, ("wide", "narrow"), scatter_dimension=0, tiled=True),
    )
    attn_shards = every_shard[:4]
    mlp_shards = every_shard[4:]
    bias_sums = lax.psum((grad_b_out, grad_b_down), ("wide", "narrow"))
    return (
        out_resid,
        grad_resid,
        attn_shards[3],
        attn_shards[0],
        attn_shards[2],
        attn_shards[1],
        bias_sums[0],
        mlp_shards[3],
        mlp_shards[0],
        mlp_shards[2],
        mlp_shards[1],
        bias_sums[1],
    )


def solution(mesh):
    by_kernel = mesh.shape["wide"] == 8 and mesh.shape["narrow"] == 4
    return jax.shard_map(
        on_device_by_kernel if by_kernel else on_device,
        mesh=mesh,
        in_specs=(
            P(("wide", "narrow"), None),
            P(("wide", "narrow")),
            P(("wide", "narrow"), None),
            P(("wide", "narrow")),
            P(("wide", "narrow"), None),
            P(),
            P(("wide", "narrow")),
            P(("wide", "narrow"), None),
            P(("wide", "narrow")),
            P(("wide", "narrow"), None),
            P(),
            P(("wide", "narrow"), None),
            P(("wide", "narrow"), None),
        ),
        out_specs=(
            P(("wide", "narrow"), None),
            P(("wide", "narrow"), None),
            P(("wide", "narrow")),
            P(("wide", "narrow"), None),
            P(("wide", "narrow")),
            P(("wide", "narrow"), None),
            P(),
            P(("wide", "narrow")),
            P(("wide", "narrow"), None),
            P(("wide", "narrow")),
            P(("wide", "narrow"), None),
            P(),
        ),
        check_vma=False,
    )
```
